128 devices in a mesh: grp: 8 (over x, core), sub: 16 (over y, z).
Axes of the slice: x: 4, y: 4, z: 4, core: 2. Of those that a mesh axis runs over, the one named last changes fastest.
Arguments:
- points: bfloat16 [393216, 768], P(('grp', 'sub')), may hold values from -36 to 36
- charges: bfloat16 [64, 393216], P(None, ('grp', 'sub')), may hold values from -6 to 6
- near_list: int32 [768, 2], P(('grp', 'sub')), may hold values from -1 to 95, as said below
- leaf_basis: bfloat16 [768, 512, 256], P(('grp', 'sub')), may hold values from -0.25 to 0.25
- transfer: bfloat16 [768, 256, 256], P(('grp', 'sub')), may hold values from -0.375 to 0.375
- parent: int32 [768], P(('grp', 'sub')), may hold values from 0 to 15, as said below
- coarse_far: int32 [128, 8], P(('grp', 'sub')), may hold values from -1 to 127, as said below
- coarse_coupling: bfloat16 [128, 8, 256, 256], P(('grp', 'sub')), may hold values from -0.125 to 0.125
Outputs:
- potential: float32 [64, 393216], P(None, ('grp', 'sub'))
The draws below stay inside these ranges and needn't reach their ends.
Inputs may be any that keep to these rules, and one draw needn't show every extreme that they name: `near_list`: A live entry is a leaf number within the subgroup (device index within the subgroup times 6 plus leaf index) of a leaf on another device of the same subgroup; the live entries of one device's 6 lists name leaves of any one other device at most 1 times, and in every draw some device names one device 1 times. `parent`: every coarse node of a subgroup has exactly 6 leaves of that subgroup. `coarse_far`: live entries are coarse node numbers over the whole machine; every list has at least one live entry.
All inputs are finite; a program needn't handle non-finite values.
Results may differ from the reference program's by a relative error of at most 0.003.
Values may be sent and summed in bfloat16 or wider, within the bound.
No kernel may reach another device: no remote copies, remote signals or barrier semaphores. Data moves between devices by JAX's collectives and lax.ppermute only.
A program may use at most 128 MiB of HBM per device.

```python
import jax
import jax.numpy as jnp
from jax import lax

D = 768
RHS = 64
LEAF = 512
RANK = 256
LEAF_DEV = 6
NEAR = 2
FARC = 8
LEAVES_GRP = 96
NODES_GRP = 16
NLEAF = 768
NPTS = 393216
NCOARSE = 128


latent_dims = 12


def draw_points(key, part):
    key = jax.random.fold_in(key, 13)
    keys = jax.random.split(key, 4)
    groups = NLEAF // LEAVES_GRP
    stride = max(D // latent_dims, 1)
    spread = (D / (2.0 * latent_dims)) ** 0.5
    shifts = jax.random.randint(keys[0], (groups, 1), 0, stride)
    coord = jnp.arange(D)[None, :]
    active = (coord + shifts) % stride == 0
    centre = jax.random.truncated_normal(keys[1], -3.0, 3.0, (groups, D))
    leaf_offset = jax.random.truncated_normal(keys[2], -3.0, 3.0, (NLEAF, D)) * (0.8 * spread)
    group_of_leaf = jnp.arange(NLEAF) // LEAVES_GRP
    leaf_active = active[group_of_leaf]
    leaf_centre = centre[group_of_leaf] + jnp.where(leaf_active, leaf_offset, 0.0)
    scale = jnp.where(leaf_active, spread, 0.3)
    offsets = jax.random.truncated_normal(keys[3], -3.0, 3.0, (NLEAF, LEAF, D))
    values = leaf_centre[:, None, :] + scale[:, None, :] * offsets
    return values.reshape(NPTS, D).astype(jnp.bfloat16)


def draw_near_list(key, part):
    key = jax.random.fold_in(key, 11)
    subgroup = LEAVES_GRP // LEAF_DEV
    devices_all = NLEAF // LEAF_DEV
    entries_dev = LEAF_DEV * NEAR
    first_key, second_key, third_key = jax.random.split(key, 3)

    def shuffle(subkey):
        return jax.random.permutation(subkey, subgroup - 1)
    orders = jax.vmap(shuffle)(jax.random.split(first_key, devices_all))
    position = jnp.arange(entries_dev)
    offsets = 1 + orders[:, position % (subgroup - 1)]
    member = jnp.arange(devices_all) % subgroup
    owners = (member[:, None] + offsets) % subgroup
    inside = jax.random.randint(second_key, (devices_all, entries_dev), 0, LEAF_DEV)
    counts = jax.random.randint(third_key, (devices_all,), 1, entries_dev + 1)
    counts = jnp.where(member == 0, entries_dev, counts)
    listed = jnp.where(position[None, :] < counts[:, None], owners * LEAF_DEV + inside, -1)
    return listed.reshape(NLEAF, NEAR).astype(jnp.int32)


def draw_parent(key, part):
    key = jax.random.fold_in(key, 5)
    group_total = NLEAF // LEAVES_GRP

    def shuffle(subkey):
        return jax.random.permutation(subkey, LEAVES_GRP)
    orders = jax.vmap(shuffle)(jax.random.split(key, group_total))
    return (orders // LEAF_DEV).reshape(NLEAF).astype(jnp.int32)


def draw_coarse_far(key, part):
    key = jax.random.fold_in(key, 7)
    first_key, second_key = jax.random.split(key)
    listed = jax.random.randint(first_key, (NCOARSE, FARC), 0, NCOARSE)
    counts = jax.random.randint(second_key, (NCOARSE,), 1, FARC + 1)
    counts = counts.at[0].set(FARC)
    return jnp.where(jnp.arange(FARC)[None, :] < counts[:, None], listed, -1).astype(jnp.int32)


def shard_levels(rng, dims, cuts, least, largest):
    gain, own = 1.0, jax.random.fold_in(rng, 6)
    for axis_at, blocks in cuts:
        draws = jnp.exp(jax.random.uniform(jax.random.fold_in(own, axis_at), (blocks,), jnp.float32, least / len(cuts), largest / len(cuts)))
        gain = gain * jnp.repeat(draws, dims[axis_at] // blocks).reshape([-1 if axis == axis_at else 1 for axis in range(len(dims))])
    return gain


def normal_values(own_key, dims, scale, bound, cuts=(), held_as=jnp.bfloat16):
    level = shard_levels(own_key, dims, cuts, -0.22, 0.18) if cuts else 1.0
    values = jax.random.normal(own_key, dims, jnp.float32) * scale * level
    return jnp.minimum(jnp.maximum(values, -bound), bound).astype(held_as)


def setup_inputs(seed: int = 0) -> dict:
    key_list = jax.random.split(jax.random.key(seed), 9)
    return {
        "points": draw_points(jax.random.fold_in(key_list[8], 71), 0),
        "charges": normal_values(key_list[1], (RHS, NPTS), 1.0, 6.0, ((1, 128),)),
        "near_list": draw_near_list(jax.random.fold_in(key_list[8], 71), 0),
        "leaf_basis": normal_values(key_list[3], (NLEAF, LEAF, RANK), LEAF ** -0.5, 0.25, ((0, 128),)),
        "transfer": normal_values(key_list[4], (NLEAF, RANK, RANK), RANK ** -0.5, 0.375, ((0, 128),)),
        "parent": draw_parent(jax.random.fold_in(key_list[8], 71), 0),
        "coarse_far": draw_coarse_far(jax.random.fold_in(key_list[8], 71), 0),
        "coarse_coupling": normal_values(key_list[7], (NCOARSE, FARC, RANK, RANK), (RANK * FARC) ** -0.5, 0.125, ((0, 128),)),
    }


def squares(block):
    return jnp.sum(jnp.square(block.astype(jnp.float32)), axis=-1)


def tile_apply(target_points, target_norms, source_points, source_norms, source_charges, gamma):
    gram = lax.dot_general(target_points, source_points, (((1,), (1,)), ((), ())), preferred_element_type=jnp.float32)
    kernel = jnp.exp(-gamma * (target_norms[:, None] + source_norms[None, :] - 2.0 * gram)).astype(jnp.bfloat16)
    return lax.dot_general(source_charges, kernel, (((1,), (1,)), ((), ())), preferred_element_type=jnp.float32)


def reference(points, charges, near_list, leaf_basis, transfer, parent, coarse_far, coarse_coupling):
    gamma = 2.0 / D
    norms = squares(points)
    leaf_points = points.reshape(NLEAF, LEAF, D)
    leaf_norms = norms.reshape(NLEAF, LEAF)
    leaf_charges = charges.reshape(RHS, NLEAF, LEAF).transpose(1, 0, 2)
    block_size = LEAF_DEV * LEAF

    def near_one(target):
        start = ((target // LEAF_DEV) * block_size).astype(jnp.int32)
        own_points = lax.dynamic_slice_in_dim(points, start, block_size, 0)
        own_norms = lax.dynamic_slice_in_dim(norms, start, block_size, 0)
        own_charges = lax.dynamic_slice_in_dim(charges, start, block_size, 1)
        total = tile_apply(leaf_points[target], leaf_norms[target], own_points, own_norms, own_charges, gamma)
        base = (target // LEAVES_GRP) * LEAVES_GRP
        for column in range(NEAR):
            entry = near_list[target, column]
            source = (base + jnp.maximum(entry, 0)).astype(jnp.int32)
            term = tile_apply(leaf_points[target], leaf_norms[target], leaf_points[source], leaf_norms[source], leaf_charges[source], gamma)
            total = total + jnp.where(entry >= 0, term, jnp.zeros_like(term))
        return total

    near_field = lax.map(near_one, jnp.arange(NLEAF, dtype=jnp.int32))
    skeleton = lax.dot_general(leaf_charges, leaf_basis, (((2,), (1,)), ((0,), (0,))), preferred_element_type=jnp.float32).astype(jnp.bfloat16)
    lifted = lax.dot_general(skeleton, transfer, (((2,), (1,)), ((0,), (0,))), preferred_element_type=jnp.float32)
    coarse_id = ((jnp.arange(NLEAF, dtype=jnp.int32) // LEAVES_GRP) * NODES_GRP + parent).astype(jnp.int32)
    weights = jax.ops.segment_sum(lifted, coarse_id, num_segments=NCOARSE).astype(jnp.bfloat16)

    def far_one(node):
        far_ids = coarse_far[node]
        sources = weights[jnp.maximum(far_ids, 0)]
        terms = lax.dot_general(sources, coarse_coupling[node], (((2,), (1,)), ((0,), (0,))), preferred_element_type=jnp.float32)
        alive = (far_ids >= 0).astype(jnp.float32)
        return jnp.sum(terms * alive[:, None, None], axis=0).astype(jnp.bfloat16)

    fields = lax.map(far_one, jnp.arange(NCOARSE, dtype=jnp.int32))
    parent_fields = fields[coarse_id]
    descended = lax.dot_general(parent_fields, transfer, (((2,), (2,)), ((0,), (0,))), preferred_element_type=jnp.float32).astype(jnp.bfloat16)
    far_field = lax.dot_general(descended, leaf_basis, (((2,), (2,)), ((0,), (0,))), preferred_element_type=jnp.float32)
    total_field = near_field + far_field
    return total_field.transpose(1, 0, 2).reshape(RHS, NPTS)
```

```python
import functools

import jax
import jax.numpy as jnp
from jax import lax
from jax.experimental import pallas as pl
from jax.experimental.pallas import tpu as pltpu
from jax.sharding import PartitionSpec as P

BF = jnp.bfloat16
F32 = jnp.float32
LOG2E = 1.4426950408889634
TILE_ROWS = 16
TILE_LANES = 128
VMEM = 48 * 1024 * 1024


def params(n=1):
    return pltpu.CompilerParams(dimension_semantics=("arbitrary",) * n, vmem_limit_bytes=VMEM)


def tiles_of(rows, lanes):
    return [(r, l) for r in range(0, rows, TILE_ROWS) for l in range(0, lanes, TILE_LANES)]


def spot(index, base, width):
    per_row = width // TILE_LANES
    return base + TILE_ROWS * (index // per_row), TILE_LANES * (index % per_row)


def pack_body(chosen, points, charges, extra, out):
    count, width = points.shape
    out[0, 0:count, :] = points[...]
    place = 0
    for source in (charges, extra):
        if source is None:
            continue
        for r, l in tiles_of(*source.shape):
            row, lane = spot(place, count, width)
            out[0, row : row + TILE_ROWS, lane : lane + TILE_LANES] = source[
                r : r + TILE_ROWS, l : l + TILE_LANES
            ]
            place += 1


def pack(points, charges, chosen, extra, count, first, leaf_size):
    width = points.shape[1]
    columns = charges.shape[0]
    members = chosen.shape[0]
    per_leaf = leaf_size // count
    rows = count + 2 * TILE_ROWS
    specs = [
        pl.BlockSpec((count, width), lambda d, c: (c[d] * per_leaf + first // count, 0)),
        pl.BlockSpec((columns, count), lambda d, c: (0, c[d] * per_leaf + first // count)),
    ]
    args = [points, charges]
    if extra is not None:
        specs.append(pl.BlockSpec(extra.shape, lambda d, c: (0, 0)))
        args.append(extra)
        body = pack_body
    else:

        def body(chosen, points, charges, out):
            pack_body(chosen, points, charges, None, out)

    return pl.pallas_call(
        body,
        grid_spec=pltpu.PrefetchScalarGridSpec(
            num_scalar_prefetch=1,
            grid=(members,),
            in_specs=specs,
            out_specs=pl.BlockSpec((1, rows, width), lambda d, c: (d, 0, 0)),
        ),
        out_shape=jax.ShapeDtypeStruct((members, rows, width), BF),
        compiler_params=params(),
        name="pack",
    )(chosen, *args)


def gauss(source, source_norms, target, target_norms, gamma):
    gram = lax.dot_general(
        source, target, (((1,), (1,)), ((), ())), preferred_element_type=F32
    )
    scale = gamma * LOG2E
    shift = -scale * source_norms
    return jnp.exp2((shift + (-scale) * target_norms) + (2.0 * scale) * gram).astype(BF)


def own_body(gamma, targets, sources, source_norms, target_norms, charges, out):
    j = pl.program_id(1)
    kernel = gauss(sources[...], source_norms[...], targets[...], target_norms[...], gamma)
    term = jnp.dot(charges[...], kernel, preferred_element_type=F32)

    @pl.when(j == 0)
    def _():
        out[...] = term

    @pl.when(j > 0)
    def _():
        out[...] += term


def own(points, charges, norms, leaf_count, leaf_size, gamma):
    width = points.shape[1]
    columns = charges.shape[0]
    total = points.shape[0]
    return pl.pallas_call(
        functools.partial(own_body, gamma),
        grid=(leaf_count, leaf_count),
        in_specs=[
            pl.BlockSpec((leaf_size, width), lambda i, j: (i, 0)),
            pl.BlockSpec((leaf_size, width), lambda i, j: (j, 0)),
            pl.BlockSpec((leaf_size, 1), lambda i, j: (j, 0)),
            pl.BlockSpec((1, leaf_size), lambda i, j: (0, i)),
            pl.BlockSpec((columns, leaf_size), lambda i, j: (0, j)),
        ],
        out_specs=pl.BlockSpec((columns, leaf_size), lambda i, j: (0, i)),
        out_shape=jax.ShapeDtypeStruct((columns, total), F32),
        compiler_params=params(2),
        cost_estimate=pl.CostEstimate(
            flops=2 * total * total * (width + columns),
            bytes_accessed=total * width * 4,
            transcendentals=total * total,
        ),
        name="own",
    )(points, points, norms[:, None], norms[None, :], charges)


def near_body(gamma, count, near_count, owner, live, fetched, targets, target_norms, before, out):
    e = pl.program_id(0)
    width = fetched.shape[2]
    columns = before.shape[0]

    @pl.when(e % near_count == 0)
    def _():
        out[...] = before[...]

    @pl.when(live[e] > 0)
    def _():
        source = fetched[0, 0:count, :]
        wide = source.astype(F32)
        norms = jnp.sum(wide * wide, axis=1, keepdims=True)
        pieces = []
        place = 0
        for r in range(0, columns, TILE_ROWS):
            line = []
            for _l in range(0, count, TILE_LANES):
                row, lane = spot(place, count, width)
                line.append(fetched[0, row : row + TILE_ROWS, lane : lane + TILE_LANES])
                place += 1
            pieces.append(jnp.concatenate(line, axis=1) if len(line) > 1 else line[0])
        charges = jnp.concatenate(pieces, axis=0)
        kernel = gauss(source, norms, targets[...], target_norms[...], gamma)
        out[...] += jnp.dot(charges, kernel, preferred_element_type=F32)


def near(fetched, owner, live, points, norms, before, count, leaf_size, near_count, gamma):
    width = points.shape[1]
    columns = before.shape[0]
    entries = owner.shape[0]
    rows = fetched.shape[1]
    return pl.pallas_call(
        functools.partial(near_body, gamma, count, near_count),
        grid_spec=pltpu.PrefetchScalarGridSpec(
            num_scalar_prefetch=2,
            grid=(entries,),
            in_specs=[
                pl.BlockSpec((1, rows, width), lambda e, o, v: (o[e], 0, 0)),
                pl.BlockSpec((leaf_size, width), lambda e, o, v: (e // near_count, 0)),
                pl.BlockSpec((1, leaf_size), lambda e, o, v: (0, e // near_count)),
                pl.BlockSpec((columns, leaf_size), lambda e, o, v: (0, e // near_count)),
            ],
            out_specs=pl.BlockSpec((columns, leaf_size), lambda e, o, v: (0, e // near_count)),
        ),
        out_shape=jax.ShapeDtypeStruct(before.shape, F32),
        compiler_params=params(),
        cost_estimate=pl.CostEstimate(
            flops=2 * entries * count * leaf_size * (width + columns),
            bytes_accessed=entries * rows * width * 2 + points.size * 2,
            transcendentals=entries * count * leaf_size,
        ),
        name="near",
    )(owner, live, fetched, points, norms[None, :], before)


def unpack(fetched, count, skip, rows, lanes):
    width = fetched.shape[2]
    lines = []
    place = skip
    for _ in range(0, rows, TILE_ROWS):
        line = []
        for _l in range(0, lanes, TILE_LANES):
            row, lane = spot(place, count, width)
            line.append(fetched[:, row : row + TILE_ROWS, lane : lane + TILE_LANES])
            place += 1
        lines.append(jnp.concatenate(line, axis=2))
    return jnp.concatenate(lines, axis=1)


def after(value, *others):
    return lax.optimization_barrier((value, *others))[0]


def exchange(block):
    return lax.all_to_all(block, "sub", split_axis=0, concat_axis=0, tiled=True)


def local(points, charges, near_list, leaf_basis, transfer, parent, coarse_far, coarse_coupling):
    leaf_count, leaf_size, rank = leaf_basis.shape
    width = points.shape[1]
    columns = charges.shape[0]
    near_count = near_list.shape[1]
    members = lax.axis_size("sub")
    groups = lax.axis_size("grp")
    gamma = 2.0 / width
    leaf_charges = charges.reshape(columns, leaf_count, leaf_size).transpose(1, 0, 2)

    entries = near_list.reshape(-1)
    alive = entries >= 0
    owner = jnp.where(alive, entries // leaf_count, 0)
    inner = jnp.where(alive, entries % leaf_count, 0)
    matches = (owner[None, :] == jnp.arange(members)[:, None]) & alive[None, :]
    requests = jnp.sum(jnp.where(matches, inner[None, :] + 1, 0), axis=1)

    skeleton = lax.dot_general(
        leaf_charges, leaf_basis, (((2,), (1,)), ((0,), (0,))), preferred_element_type=F32
    ).astype(BF)
    lifted = lax.dot_general(
        skeleton, transfer, (((2,), (1,)), ((0,), (0,))), preferred_element_type=F32
    )
    membership = parent[None, :] == jnp.arange(members)[:, None]
    partial_sums = sum(
        jnp.where(membership[:, k, None, None], lifted[k][None], 0.0) for k in range(leaf_count)
    ).astype(BF)
    asking = jnp.broadcast_to(
        requests.astype(F32).astype(BF)[:, None, None], (members, TILE_ROWS, rank)
    )
    got = exchange(jnp.concatenate([partial_sums, asking], axis=1))
    chosen = jnp.maximum(got[:, columns, 0].astype(F32).astype(jnp.int32) - 1, 0)
    own_weight = jnp.sum(got[:, :columns].astype(F32), axis=0).astype(BF)

    quarter = leaf_size // 4
    send_a = pack(points, charges, chosen, own_weight, quarter, 0, leaf_size)
    got_a = exchange(send_a)
    send_b = pack(points, charges, chosen, None, 2 * quarter, 2 * quarter, leaf_size)
    got_b = exchange(after(send_b, got_a))
    norms = jnp.sum(jnp.square(points.astype(F32)), axis=-1)
    total = own(points, charges, norms, leaf_count, leaf_size, gamma)

    weights = unpack(got_a, quarter, columns // TILE_ROWS, columns, rank)
    half = groups // 2
    turned = [weights] + [
        lax.ppermute(weights, "grp", [(i, (i + 2 * k) % groups) for i in range(groups)])
        for k in range(1, half)
    ]
    mine = jnp.stack(turned)
    other = lax.ppermute(mine, "grp", [(i, i ^ 1) for i in range(groups)])
    both = jnp.stack([mine, other])
    far_ids = coarse_far[0]
    far_alive = (far_ids >= 0).astype(F32)
    ids = jnp.maximum(far_ids, 0)
    here = lax.axis_index("grp")
    from_group = ids // members
    side = (from_group % 2) ^ (here % 2)
    turn = (here // 2 - from_group // 2) % half
    sources = both.reshape(2 * half * members, columns, rank)[
        (side * half + turn) * members + ids % members
    ]
    far_terms = lax.dot_general(
        sources, coarse_coupling[0], (((2,), (1,)), ((0,), (0,))), preferred_element_type=F32
    )
    field = jnp.sum(far_terms * far_alive[:, None, None], axis=0).astype(BF)

    live = alive.astype(jnp.int32)
    add = functools.partial(
        near, leaf_size=leaf_size, near_count=near_count, gamma=gamma
    )
    total = add(got_a, owner, live, points, norms, total, quarter)
    send_c = pack(points, charges, chosen, field, quarter, quarter, leaf_size)
    got_c = exchange(after(send_c, got_b))
    total = add(got_b, owner, live, points, norms, total, 2 * quarter)
    total = add(got_c, owner, live, points, norms, total, quarter)

    fields = unpack(got_c, quarter, columns // TILE_ROWS, columns, rank)
    parent_fields = fields[parent]
    descended = lax.dot_general(
        parent_fields, transfer, (((2,), (2,)), ((0,), (0,))), preferred_element_type=F32
    ).astype(BF)
    far_field = lax.dot_general(
        descended, leaf_basis, (((2,), (2,)), ((0,), (0,))), preferred_element_type=F32
    )
    return total + far_field.transpose(1, 0, 2).reshape(columns, leaf_count * leaf_size)


def solution(mesh):
    placed = (
        P(("grp", "sub"), None),
        P(None, ("grp", "sub")),
        P(("grp", "sub"), None),
        P(("grp", "sub"), None, None),
        P(("grp", "sub"), None, None),
        P(("grp", "sub")),
        P(("grp", "sub"), None),
        P(("grp", "sub"), None, None, None),
    )
    return jax.shard_map(
        local, mesh=mesh, in_specs=placed, out_specs=P(None, ("grp", "sub")), check_vma=False
    )
```

```python
import functools

import jax
import jax.numpy as jnp
from jax import lax
from jax.experimental import pallas as pl
from jax.experimental.pallas import tpu as pltpu
from jax.sharding import PartitionSpec as P

BF = jnp.bfloat16
F32 = jnp.float32
LOG2E = 1.4426950408889634
TILE_ROWS = 16
TILE_LANES = 128
NT = (((1,), (1,)), ((), ()))
VMEM = 48 * 1024 * 1024


def params(n=1):
    return pltpu.CompilerParams(dimension_semantics=("arbitrary",) * n, vmem_limit_bytes=VMEM)


def tiles_of(rows, lanes):
    return [(r, l) for r in range(0, rows, TILE_ROWS) for l in range(0, lanes, TILE_LANES)]


def spot(index, base, width):
    per_row = width // TILE_LANES
    return base + TILE_ROWS * (index // per_row), TILE_LANES * (index % per_row)


def pack_body(chosen, points, charges, extra, out):
    count, width = points.shape
    out[0, 0:count, :] = points[...]
    place = 0
    for source in (charges, extra):
        if source is None:
            continue
        for r, l in tiles_of(*source.shape):
            row, lane = spot(place, count, width)
            out[0, row : row + TILE_ROWS, lane : lane + TILE_LANES] = source[
                r : r + TILE_ROWS, l : l + TILE_LANES
            ]
            place += 1


def pack(points, charges, chosen, extra, count, first, leaf_size):
    width = points.shape[1]
    columns = charges.shape[0]
    members = chosen.shape[0]
    per_leaf = leaf_size // count
    rows = count + 2 * TILE_ROWS
    specs = [
        pl.BlockSpec((count, width), lambda d, c: (c[d] * per_leaf + first // count, 0)),
        pl.BlockSpec((columns, count), lambda d, c: (0, c[d] * per_leaf + first // count)),
    ]
    args = [points, charges]
    if extra is not None:
        specs.append(pl.BlockSpec(extra.shape, lambda d, c: (0, 0)))
        args.append(extra)
        body = pack_body
    else:

        def body(chosen, points, charges, out):
            pack_body(chosen, points, charges, None, out)

    return pl.pallas_call(
        body,
        grid_spec=pltpu.PrefetchScalarGridSpec(
            num_scalar_prefetch=1,
            grid=(members,),
            in_specs=specs,
            out_specs=pl.BlockSpec((1, rows, width), lambda d, c: (d, 0, 0)),
        ),
        out_shape=jax.ShapeDtypeStruct((members, rows, width), BF),
        compiler_params=params(),
        name="pack",
    )(chosen, *args)


def gauss(source, source_norms, target, target_norms, scale):
    gram = lax.dot_general(source, target, NT, preferred_element_type=F32)
    return jnp.exp2((2.0 * scale) * gram - (source_norms + target_norms)).astype(BF)


def own_body(scale, leaf_size, first, second, ti, sj, ci, cj, out, rows, col):
    step = pl.program_id(0)
    width = ti.shape[1]
    i0 = pl.multiple_of(first[step] * leaf_size, leaf_size)
    j0 = pl.multiple_of(second[step] * leaf_size, leaf_size)
    ones = jnp.ones((8, width), BF)
    lanes = jnp.ones((width, TILE_LANES), BF)

    @pl.when(step == 0)
    def _():
        out[...] = jnp.zeros_like(out)

    @pl.when(i0 == j0)
    def _():
        wide = sj[...].astype(F32)
        square = wide * wide
        high = square.astype(BF)
        low = (square - high.astype(F32)).astype(BF)
        row = lax.dot_general(ones, high, NT, preferred_element_type=F32) + lax.dot_general(
            ones, low, NT, preferred_element_type=F32
        )
        rows[:, pl.ds(i0, leaf_size)] = scale * row
        column = jnp.dot(high, lanes, preferred_element_type=F32) + jnp.dot(
            low, lanes, preferred_element_type=F32
        )
        col[pl.ds(i0, leaf_size), :] = scale * column

    gram = lax.dot_general(sj[...], ti[...], NT, preferred_element_type=F32)
    norms = col[pl.ds(j0, leaf_size), :][:, :1] + rows[0:1, pl.ds(i0, leaf_size)]
    kernel = jnp.exp2((2.0 * scale) * gram - norms).astype(BF)
    out[:, pl.ds(i0, leaf_size)] += jnp.dot(cj[...], kernel, preferred_element_type=F32)

    @pl.when(i0 != j0)
    def _():
        out[:, pl.ds(j0, leaf_size)] += lax.dot_general(
            ci[...], kernel, NT, preferred_element_type=F32
        )


def own(points, charges, leaf_count, leaf_size, gamma):
    width = points.shape[1]
    columns = charges.shape[0]
    total = points.shape[0]
    pairs = [(i, j) for j in range(leaf_count) for i in range(j, -1, -1)]
    first = jnp.array([p[0] for p in pairs], jnp.int32)
    second = jnp.array([p[1] for p in pairs], jnp.int32)
    return pl.pallas_call(
        functools.partial(own_body, gamma * LOG2E, leaf_size),
        grid_spec=pltpu.PrefetchScalarGridSpec(
            num_scalar_prefetch=2,
            grid=(len(pairs),),
            in_specs=[
                pl.BlockSpec((leaf_size, width), lambda s, a, b: (a[s], 0)),
                pl.BlockSpec((leaf_size, width), lambda s, a, b: (b[s], 0)),
                pl.BlockSpec((columns, leaf_size), lambda s, a, b: (0, a[s])),
                pl.BlockSpec((columns, leaf_size), lambda s, a, b: (0, b[s])),
            ],
            out_specs=[
                pl.BlockSpec((columns, total), lambda s, a, b: (0, 0)),
                pl.BlockSpec((8, total), lambda s, a, b: (0, 0)),
            ],
            scratch_shapes=[pltpu.VMEM((total, TILE_LANES), F32)],
        ),
        out_shape=[
            jax.ShapeDtypeStruct((columns, total), F32),
            jax.ShapeDtypeStruct((8, total), F32),
        ],
        compiler_params=params(),
        cost_estimate=pl.CostEstimate(
            flops=2 * len(pairs) * leaf_size * leaf_size * (width + 2 * columns),
            bytes_accessed=total * width * 8,
            transcendentals=len(pairs) * leaf_size * leaf_size,
        ),
        name="own",
    )(first, second, points, points, charges, charges)


def near_body(scale, count, near_count, owner, live, fetched, targets, target_norms, before, out):
    e = pl.program_id(0)
    width = fetched.shape[2]
    columns = before.shape[0]

    @pl.when(e % near_count == 0)
    def _():
        out[...] = before[...]

    @pl.when(live[e] > 0)
    def _():
        source = fetched[0, 0:count, :]
        wide = source.astype(F32)
        norms = scale * jnp.sum(wide * wide, axis=1, keepdims=True)
        pieces = []
        place = 0
        for r in range(0, columns, TILE_ROWS):
            line = []
            for _l in range(0, count, TILE_LANES):
                row, lane = spot(place, count, width)
                line.append(fetched[0, row : row + TILE_ROWS, lane : lane + TILE_LANES])
                place += 1
            pieces.append(jnp.concatenate(line, axis=1) if len(line) > 1 else line[0])
        charges = jnp.concatenate(pieces, axis=0)
        kernel = gauss(source, norms, targets[...], target_norms[0:1, :], scale)
        out[...] += jnp.dot(charges, kernel, preferred_element_type=F32)


def near(fetched, owner, live, points, norms, before, count, leaf_size, near_count, gamma):
    width = points.shape[1]
    columns = before.shape[0]
    entries = owner.shape[0]
    rows = fetched.shape[1]
    return pl.pallas_call(
        functools.partial(near_body, gamma * LOG2E, count, near_count),
        grid_spec=pltpu.PrefetchScalarGridSpec(
            num_scalar_prefetch=2,
            grid=(entries,),
            in_specs=[
                pl.BlockSpec((1, rows, width), lambda e, o, v: (o[e], 0, 0)),
                pl.BlockSpec((leaf_size, width), lambda e, o, v: (e // near_count, 0)),
                pl.BlockSpec((8, leaf_size), lambda e, o, v: (0, e // near_count)),
                pl.BlockSpec((columns, leaf_size), lambda e, o, v: (0, e // near_count)),
            ],
            out_specs=pl.BlockSpec((columns, leaf_size), lambda e, o, v: (0, e // near_count)),
        ),
        out_shape=jax.ShapeDtypeStruct(before.shape, F32),
        compiler_params=params(),
        cost_estimate=pl.CostEstimate(
            flops=2 * entries * count * leaf_size * (width + columns),
            bytes_accessed=entries * rows * width * 2 + points.size * 2,
            transcendentals=entries * count * leaf_size,
        ),
        name="near",
    )(owner, live, fetched, points, norms, before)


def unpack(fetched, count, skip, rows, lanes):
    width = fetched.shape[2]
    lines = []
    place = skip
    for _ in range(0, rows, TILE_ROWS):
        line = []
        for _l in range(0, lanes, TILE_LANES):
            row, lane = spot(place, count, width)
            line.append(fetched[:, row : row + TILE_ROWS, lane : lane + TILE_LANES])
            place += 1
        lines.append(jnp.concatenate(line, axis=2))
    return jnp.concatenate(lines, axis=1)


def after(value, *others):
    return lax.optimization_barrier((value, *others))[0]


def exchange(block):
    return lax.all_to_all(block, "sub", split_axis=0, concat_axis=0, tiled=True)


def local(points, charges, near_list, leaf_basis, transfer, parent, coarse_far, coarse_coupling):
    leaf_count, leaf_size, rank = leaf_basis.shape
    width = points.shape[1]
    columns = charges.shape[0]
    near_count = near_list.shape[1]
    members = lax.axis_size("sub")
    groups = lax.axis_size("grp")
    gamma = 2.0 / width
    leaf_charges = charges.reshape(columns, leaf_count, leaf_size).transpose(1, 0, 2)

    entries = near_list.reshape(-1)
    alive = entries >= 0
    owner = jnp.where(alive, entries // leaf_count, 0)
    inner = jnp.where(alive, entries % leaf_count, 0)
    matches = (owner[None, :] == jnp.arange(members)[:, None]) & alive[None, :]
    requests = jnp.sum(jnp.where(matches, inner[None, :] + 1, 0), axis=1)

    skeleton = lax.dot_general(
        leaf_charges, leaf_basis, (((2,), (1,)), ((0,), (0,))), preferred_element_type=F32
    ).astype(BF)
    lifted = lax.dot_general(
        skeleton, transfer, (((2,), (1,)), ((0,), (0,))), preferred_element_type=F32
    )
    membership = parent[None, :] == jnp.arange(members)[:, None]
    partial_sums = sum(
        jnp.where(membership[:, k, None, None], lifted[k][None], 0.0) for k in range(leaf_count)
    ).astype(BF)
    asking = jnp.broadcast_to(
        requests.astype(F32).astype(BF)[:, None, None], (members, TILE_ROWS, rank)
    )
    got = exchange(jnp.concatenate([partial_sums, asking], axis=1))
    chosen = jnp.maximum(got[:, columns, 0].astype(F32).astype(jnp.int32) - 1, 0)
    own_weight = jnp.sum(got[:, :columns].astype(F32), axis=0).astype(BF)

    quarter = leaf_size // 4
    send_a = pack(points, charges, chosen, own_weight, quarter, 0, leaf_size)
    got_a = exchange(send_a)
    send_b = pack(points, charges, chosen, None, 2 * quarter, 2 * quarter, leaf_size)
    got_b = exchange(after(send_b, got_a))
    total, norms = own(points, charges, leaf_count, leaf_size, gamma)

    weights = unpack(got_a, quarter, columns // TILE_ROWS, columns, rank)
    half = groups // 2
    turned = [weights] + [
        lax.ppermute(weights, "grp", [(i, (i + 2 * k) % groups) for i in range(groups)])
        for k in range(1, half)
    ]
    mine = jnp.stack(turned)
    other = lax.ppermute(mine, "grp", [(i, i ^ 1) for i in range(groups)])
    both = jnp.stack([mine, other])
    far_ids = coarse_far[0]
    far_alive = (far_ids >= 0).astype(F32)
    ids = jnp.maximum(far_ids, 0)
    here = lax.axis_index("grp")
    from_group = ids // members
    side = (from_group % 2) ^ (here % 2)
    turn = (here // 2 - from_group // 2) % half
    sources = both.reshape(2 * half * members, columns, rank)[
        (side * half + turn) * members + ids % members
    ]
    far_terms = lax.dot_general(
        sources, coarse_coupling[0], (((2,), (1,)), ((0,), (0,))), preferred_element_type=F32
    )
    field = jnp.sum(far_terms * far_alive[:, None, None], axis=0).astype(BF)

    live = alive.astype(jnp.int32)
    add = functools.partial(
        near, leaf_size=leaf_size, near_count=near_count, gamma=gamma
    )
    total = add(got_a, owner, live, points, norms, total, quarter)
    send_c = pack(points, charges, chosen, field, quarter, quarter, leaf_size)
    got_c = exchange(after(send_c, got_b, total))
    total = add(got_b, owner, live, points, norms, total, 2 * quarter)
    total = add(got_c, owner, live, points, norms, total, quarter)

    fields = unpack(got_c, quarter, columns // TILE_ROWS, columns, rank)
    parent_fields = fields[parent]
    descended = lax.dot_general(
        parent_fields, transfer, (((2,), (2,)), ((0,), (0,))), preferred_element_type=F32
    ).astype(BF)
    far_field = lax.dot_general(
        descended, leaf_basis, (((2,), (2,)), ((0,), (0,))), preferred_element_type=F32
    )
    return total + far_field.transpose(1, 0, 2).reshape(columns, leaf_count * leaf_size)


def solution(mesh):
    placed = (
        P(("grp", "sub"), None),
        P(None, ("grp", "sub")),
        P(("grp", "sub"), None),
        P(("grp", "sub"), None, None),
        P(("grp", "sub"), None, None),
        P(("grp", "sub")),
        P(("grp", "sub"), None),
        P(("grp", "sub"), None, None, None),
    )
    return jax.shard_map(
        local, mesh=mesh, in_specs=placed, out_specs=P(None, ("grp", "sub")), check_vma=False
    )
```

```python
import functools

import jax
import jax.numpy as jnp
from jax import lax
from jax.experimental import pallas as pl
from jax.experimental.pallas import tpu as pltpu
from jax.sharding import PartitionSpec as P

BF = jnp.bfloat16
F32 = jnp.float32
LOG2E = 1.4426950408889634
TILE_ROWS = 16
TILE_LANES = 128
RING = 4
QUARTERS = 4
NT = (((1,), (1,)), ((), ()))
VMEM = 40 * 1024 * 1024
DIRECTIONS = [(axis, way) for axis in range(2) for way in range(2)]


def params(n=1):
    return pltpu.CompilerParams(dimension_semantics=("arbitrary",) * n, vmem_limit_bytes=VMEM)


def offset(axis, along, across):
    return (along, across) if axis == 0 else (across, along)


def number(steps):
    return steps[0] * RING + steps[1]


def one(way):
    return 1 if way == 0 else RING - 1


def travel(axis, way):
    y, z = offset(axis, one(way), 0)
    return [
        (d, (d // RING + y) % RING * RING + (d % RING + z) % RING) for d in range(RING * RING)
    ]


def step(block, axis, way):
    return lax.ppermute(block, "sub", travel(axis, way))


def start_all(copies):
    for copy in copies:
        copy.start()
    for copy in copies:
        copy.wait()


def collect(units, asked, place, plans):
    count = sum(len(plan) for plan in plans)
    shape = units.shape[1:]
    sizes = [sum(run[2] for run in plan) for plan in plans]

    def body(asked, place, units, *rest):
        outs, sems = rest[:-1], rest[-1]
        copies = []
        for plan, out in zip(plans, outs):
            at = 0
            for steps, quarter, length in plan:
                device = (place[0] + steps[0]) % RING * RING + (place[1] + steps[1]) % RING
                leaf = jnp.maximum(asked[device] - 1, 0)
                copies.append(
                    pltpu.make_async_copy(
                        units.at[pl.ds(leaf * QUARTERS + quarter, length)],
                        out.at[pl.ds(at, length)],
                        sems.at[len(copies)],
                    )
                )
                at += length
        start_all(copies)

    return pl.pallas_call(
        body,
        in_specs=[
            pl.BlockSpec(memory_space=pltpu.SMEM),
            pl.BlockSpec(memory_space=pltpu.SMEM),
            pl.BlockSpec(memory_space=pl.ANY),
        ],
        out_specs=[pl.BlockSpec(memory_space=pl.ANY)] * len(plans),
        out_shape=[jax.ShapeDtypeStruct((size, *shape), BF) for size in sizes],
        scratch_shapes=[pltpu.SemaphoreType.DMA((count,))],
        compiler_params=pltpu.CompilerParams(vmem_limit_bytes=1024 * 1024),
        name="collect",
    )(asked, place, units)


def weave(sources, plans):
    count = sum(len(plan) for plan in plans)
    shape = sources[0].shape[1:]
    sizes = [sum(run[2] for run in plan) for plan in plans]

    def body(*refs):
        ins, outs, sems = refs[: len(sources)], refs[len(sources) : -1], refs[-1]
        copies = []
        for plan, out in zip(plans, outs):
            at = 0
            for source, first, length in plan:
                copies.append(
                    pltpu.make_async_copy(
                        ins[source].at[pl.ds(first, length)],
                        out.at[pl.ds(at, length)],
                        sems.at[len(copies)],
                    )
                )
                at += length
        start_all(copies)

    return pl.pallas_call(
        body,
        in_specs=[pl.BlockSpec(memory_space=pl.ANY)] * len(sources),
        out_specs=[pl.BlockSpec(memory_space=pl.ANY)] * len(plans),
        out_shape=[jax.ShapeDtypeStruct((size, *shape), BF) for size in sizes],
        scratch_shapes=[pltpu.SemaphoreType.DMA((count,))],
        compiler_params=pltpu.CompilerParams(vmem_limit_bytes=1024 * 1024),
        name="weave",
    )(*sources)


def gauss(source, source_norms, target, target_norms, scale):
    gram = lax.dot_general(source, target, NT, preferred_element_type=F32)
    return jnp.exp2((2.0 * scale) * gram - (source_norms + target_norms)).astype(BF)


def own_body(scale, leaf_size, first, second, ti, sj, ci, cj, out, rows, col):
    step = pl.program_id(0)
    width = ti.shape[1]
    i0 = pl.multiple_of(first[step] * leaf_size, leaf_size)
    j0 = pl.multiple_of(second[step] * leaf_size, leaf_size)
    ones = jnp.ones((8, width), BF)
    lanes = jnp.ones((width, TILE_LANES), BF)

    @pl.when(step == 0)
    def _():
        out[...] = jnp.zeros_like(out)

    @pl.when(i0 == j0)
    def _():
        wide = sj[...].astype(F32)
        square = wide * wide
        high = square.astype(BF)
        low = (square - high.astype(F32)).astype(BF)
        row = lax.dot_general(ones, high, NT, preferred_element_type=F32) + lax.dot_general(
            ones, low, NT, preferred_element_type=F32
        )
        rows[:, pl.ds(i0, leaf_size)] = scale * row
        column = jnp.dot(high, lanes, preferred_element_type=F32) + jnp.dot(
            low, lanes, preferred_element_type=F32
        )
        col[pl.ds(i0, leaf_size), :] = scale * column

    gram = lax.dot_general(sj[...], ti[...], NT, preferred_element_type=F32)
    norms = col[pl.ds(j0, leaf_size), :][:, :1] + rows[0:1, pl.ds(i0, leaf_size)]
    kernel = jnp.exp2((2.0 * scale) * gram - norms).astype(BF)
    out[:, pl.ds(i0, leaf_size)] += jnp.dot(cj[...], kernel, preferred_element_type=F32)

    @pl.when(i0 != j0)
    def _():
        out[:, pl.ds(j0, leaf_size)] += lax.dot_general(
            ci[...], kernel, NT, preferred_element_type=F32
        )


def own(points, charges, leaf_count, leaf_size, gamma):
    width = points.shape[1]
    columns = charges.shape[0]
    total = points.shape[0]
    pairs = [(i, j) for j in range(leaf_count) for i in range(j, -1, -1)]
    first = jnp.array([p[0] for p in pairs], jnp.int32)
    second = jnp.array([p[1] for p in pairs], jnp.int32)
    return pl.pallas_call(
        functools.partial(own_body, gamma * LOG2E, leaf_size),
        grid_spec=pltpu.PrefetchScalarGridSpec(
            num_scalar_prefetch=2,
            grid=(len(pairs),),
            in_specs=[
                pl.BlockSpec((leaf_size, width), lambda s, a, b: (a[s], 0)),
                pl.BlockSpec((leaf_size, width), lambda s, a, b: (b[s], 0)),
                pl.BlockSpec((columns, leaf_size), lambda s, a, b: (0, a[s])),
                pl.BlockSpec((columns, leaf_size), lambda s, a, b: (0, b[s])),
            ],
            out_specs=[
                pl.BlockSpec((columns, total), lambda s, a, b: (0, 0)),
                pl.BlockSpec((8, total), lambda s, a, b: (0, 0)),
            ],
            scratch_shapes=[pltpu.VMEM((total, TILE_LANES), F32)],
        ),
        out_shape=[
            jax.ShapeDtypeStruct((columns, total), F32),
            jax.ShapeDtypeStruct((8, total), F32),
        ],
        compiler_params=params(),
        cost_estimate=pl.CostEstimate(
            flops=2 * len(pairs) * leaf_size * leaf_size * (width + 2 * columns),
            bytes_accessed=total * width * 8,
            transcendentals=len(pairs) * leaf_size * leaf_size,
        ),
        name="own",
    )(first, second, points, points, charges, charges)


def near_body(scale, groups, leaf_size, target, points, norms, before, *refs):
    buffers, out = refs[:-1], refs[-1]
    columns = before.shape[0]
    rows = buffers[0].shape[1] - TILE_ROWS
    out[...] = before[...]
    for units, source_steps in groups:
        leaf = target[source_steps]

        @pl.when(leaf >= 0)
        def _(units=units, leaf=leaf):
            source = jnp.concatenate([buffers[b][u, 0:rows, :] for b, u in units], axis=0)
            charges = jnp.concatenate(
                [
                    jnp.concatenate(
                        [
                            buffers[b][u, rows:, g * TILE_LANES : (g + 1) * TILE_LANES]
                            for g in range(columns // TILE_ROWS)
                        ],
                        axis=0,
                    )
                    for b, u in units
                ],
                axis=1,
            )
            wide = source.astype(F32)
            source_norms = scale * jnp.sum(wide * wide, axis=1, keepdims=True)
            start = pl.multiple_of(leaf * leaf_size, leaf_size)
            kernel = gauss(
                source,
                source_norms,
                points[pl.ds(start, leaf_size), :],
                norms[0:1, pl.ds(start, leaf_size)],
                scale,
            )
            out[:, pl.ds(start, leaf_size)] += jnp.dot(
                charges, kernel, preferred_element_type=F32
            )


def near(buffers, groups, target, points, norms, before, leaf_size, gamma):
    width = points.shape[1]
    columns = before.shape[0]
    rows = sum(len(units) for units, _ in groups) * TILE_LANES
    whole = pl.BlockSpec(memory_space=pltpu.VMEM)
    return pl.pallas_call(
        functools.partial(near_body, gamma * LOG2E, groups, leaf_size),
        in_specs=[pl.BlockSpec(memory_space=pltpu.SMEM)] + [whole] * (3 + len(buffers)),
        out_specs=whole,
        out_shape=jax.ShapeDtypeStruct(before.shape, F32),
        compiler_params=pltpu.CompilerParams(vmem_limit_bytes=VMEM),
        cost_estimate=pl.CostEstimate(
            flops=2 * rows * leaf_size * (width + columns),
            bytes_accessed=rows * width * 2 + points.size * 2,
            transcendentals=rows * leaf_size,
        ),
        name="near",
    )(target, points, norms, before, *buffers)


def after(value, *others):
    return lax.optimization_barrier((value, *others))[0]


def exchange(block):
    return lax.all_to_all(block, "sub", split_axis=0, concat_axis=0, tiled=True)


def local(points, charges, near_list, leaf_basis, transfer, parent, coarse_far, coarse_coupling):
    leaf_count, leaf_size, rank = leaf_basis.shape
    width = points.shape[1]
    columns = charges.shape[0]
    near_count = near_list.shape[1]
    members = lax.axis_size("sub")
    groups = lax.axis_size("grp")
    gamma = 2.0 / width
    here = lax.axis_index("sub")
    place = jnp.stack([here // RING, here % RING]).astype(jnp.int32)

    entries = near_list.reshape(-1)
    alive = entries >= 0
    owner = jnp.where(alive, entries // leaf_count, 0)
    inner = jnp.where(alive, entries % leaf_count, 0)
    devices = jnp.arange(members)
    matches = (owner[None, :] == devices[:, None]) & alive[None, :]
    requests = jnp.sum(jnp.where(matches, inner[None, :] + 1, 0), axis=1)
    asked = exchange(requests[:, None])[:, 0]
    steps = (place[0] - owner // RING) % RING * RING + (place[1] - owner % RING) % RING
    leaves = jnp.arange(entries.shape[0]) // near_count
    hits = (steps[None, :] == devices[:, None]) & alive[None, :]
    target = jnp.sum(jnp.where(hits, leaves[None, :] + 1, 0), axis=1) - 1

    pieces = leaf_count * QUARTERS
    rows = leaf_size // QUARTERS
    lines = columns // TILE_ROWS
    unit_charges = (
        charges.reshape(lines, TILE_ROWS, pieces, rows)
        .transpose(2, 1, 0, 3)
        .reshape(pieces, TILE_ROWS, lines * rows)
    )
    units = jnp.concatenate(
        [
            points.reshape(pieces, rows, width),
            jnp.pad(unit_charges, ((0, 0), (0, 0), (0, width - lines * rows))),
        ],
        axis=1,
    )

    leaf_charges = charges.reshape(columns, leaf_count, leaf_size).transpose(1, 0, 2)
    skeleton = lax.dot_general(
        leaf_charges, leaf_basis, (((2,), (1,)), ((0,), (0,))), preferred_element_type=F32
    ).astype(BF)
    lifted = lax.dot_general(
        skeleton, transfer, (((2,), (1,)), ((0,), (0,))), preferred_element_type=F32
    )
    membership = parent[None, :] == devices[:, None]
    partial_sums = sum(
        jnp.where(membership[:, k, None, None], lifted[k][None], 0.0) for k in range(leaf_count)
    ).astype(BF)
    summed = exchange(after(partial_sums, asked))
    own_weight = jnp.sum(summed.astype(F32), axis=0).astype(BF)

    half = {0: 0, 1: QUARTERS // 2}
    plan_1, plan_2, plan_5 = [], [], []
    for axis, way in DIRECTIONS:
        h = half[axis]
        near_side = one(way)
        plan_1.append(
            [(offset(axis, 2, 0), 2 * way, 2)]
            + [(offset(axis, 2, across), h + way, 1) for across in (1, 3, 2)]
        )
        plan_2.append([(offset(axis, near_side, across), h, 2) for across in (1, 3, 2)])
        plan_5.append([(offset(axis, near_side, 0), 0, QUARTERS)])

    def send(blocks):
        return [step(b, *d) for b, d in zip(blocks, DIRECTIONS)]

    sent_1 = collect(units, asked, place, plan_1)
    got_1 = send(sent_1)
    sent_2 = collect(after(units, *sent_1), asked, place, plan_2)
    got_2 = send(sent_2)
    total, norms = own(after(points, *sent_2), charges, leaf_count, leaf_size, gamma)
    got_3 = send(got_1)
    sent_5 = collect(after(units, *got_2), asked, place, plan_5)
    got_5 = send(sent_5)
    plan_x, plan_y = [], []
    for axis, way in DIRECTIONS:
        first = 2 * (1 - axis)
        plan_x.append(
            [(first, 4 + way, 1), (first + 1, 4 + way, 1), (4 + first + way, 4, 1)]
        )
        plan_y.append(
            [(first, 2 * way, 2), (first + 1, 2 * way, 2)]
            + [(4 + first, 2 + way, 1), (4 + first + 1, 2 + way, 1)]
        )
    woven = weave([*got_2, *got_3], plan_x + plan_y)
    got_x = send(woven[: len(plan_x)])
    got_y = send(woven[len(plan_x) :])
    got_6 = send(got_x)

    groups_a, groups_b, groups_c = [], [], []
    for d, (axis, way) in enumerate(DIRECTIONS):
        groups_a.append(([(d, 0), (d, 1)], number(offset(axis, 2, 0))))
        for k in range(0, QUARTERS, 2):
            groups_a.append(([(4 + d, k), (4 + d, k + 1)], number(offset(axis, one(way), 0))))
        for k, along in enumerate((1, 3, 2)):
            pair = [(d, 2 * k), (d, 2 * k + 1)]
            groups_b.append((pair, number(offset(1 - axis, along, one(way)))))
            if way == 0:
                groups_c.append(([(d, k), (d + 1, k)], number(offset(1 - axis, along, 2))))

    weights = exchange(jnp.broadcast_to(own_weight[None], (members, columns, rank)))
    chips = groups // 2
    turned = [weights] + [
        lax.ppermute(weights, "grp", [(i, (i + 2 * k) % groups) for i in range(groups)])
        for k in range(1, chips)
    ]
    mine = jnp.stack(turned)
    other = lax.ppermute(mine, "grp", [(i, i ^ 1) for i in range(groups)])
    far_ids = coarse_far[0]
    far_alive = (far_ids >= 0).astype(F32)
    ids = jnp.maximum(far_ids, 0)
    group = lax.axis_index("grp")
    from_group = ids // members
    side = (from_group % 2) != (group % 2)
    at = (group // 2 - from_group // 2) % chips * members + ids % members
    flat = (chips * members, columns, rank)
    sources = jnp.where(
        side[:, None, None], other.reshape(flat)[at], mine.reshape(flat)[at]
    )
    far_terms = lax.dot_general(
        sources, coarse_coupling[0], (((2,), (1,)), ((0,), (0,))), preferred_element_type=F32
    )
    field = jnp.sum(far_terms * far_alive[:, None, None], axis=0).astype(BF)
    fields = exchange(jnp.broadcast_to(field[None], (members, columns, rank)))
    parent_fields = fields[parent]
    descended = lax.dot_general(
        parent_fields, transfer, (((2,), (2,)), ((0,), (0,))), preferred_element_type=F32
    ).astype(BF)
    far_field = lax.dot_general(
        descended, leaf_basis, (((2,), (2,)), ((0,), (0,))), preferred_element_type=F32
    )
    far_field = far_field.transpose(1, 0, 2).reshape(columns, leaf_count * leaf_size)

    add = functools.partial(near, leaf_size=leaf_size, gamma=gamma)
    total = add([*got_3, *got_5], groups_a, target, points, norms, total)
    total = add(got_y, groups_b, target, points, norms, total)
    total = total + far_field
    return add(got_6, groups_c, target, points, norms, total)


def solution(mesh):
    placed = (
        P(("grp", "sub"), None),
        P(None, ("grp", "sub")),
        P(("grp", "sub"), None),
        P(("grp", "sub"), None, None),
        P(("grp", "sub"), None, None),
        P(("grp", "sub")),
        P(("grp", "sub"), None),
        P(("grp", "sub"), None, None, None),
    )
    return jax.shard_map(
        local, mesh=mesh, in_specs=placed, out_specs=P(None, ("grp", "sub")), check_vma=False
    )
```

```python
import functools

import jax
import jax.numpy as jnp
from jax import lax
from jax.experimental import pallas as pl
from jax.experimental.pallas import tpu as pltpu
from jax.sharding import PartitionSpec as P

BF = jnp.bfloat16
F32 = jnp.float32
LOG2E = 1.4426950408889634
TILE_ROWS = 16
TILE_LANES = 128
RING = 4
NT = (((1,), (1,)), ((), ()))
VMEM = 40 * 1024 * 1024


def params(n=1):
    return pltpu.CompilerParams(dimension_semantics=("arbitrary",) * n, vmem_limit_bytes=VMEM)


def turn(block, y, z):
    pairs = [
        (d, (d // RING + y) % RING * RING + (d % RING + z) % RING) for d in range(RING * RING)
    ]
    return lax.ppermute(block, "sub", pairs)


def around_y(block):
    return [block] + [turn(block, y, 0) for y in range(1, RING)]


def around_z(block):
    return [block] + [turn(block, 0, z) for z in range(1, RING)]


def collect(points, tails, asked, place):
    leaves, rows, width = points.shape
    members = asked.shape[0]
    extra = tails.shape[1]

    def body(asked, place, points, tails, out, sems):
        def copies(p):
            device = (place[0] - p // RING) % RING * RING + (place[1] - p % RING) % RING
            leaf = jnp.maximum(asked[p] - 1, 0)
            return (
                pltpu.make_async_copy(
                    points.at[leaf], out.at[device, pl.ds(0, rows)], sems.at[p, 0]
                ),
                pltpu.make_async_copy(
                    tails.at[leaf], out.at[device, pl.ds(rows, extra)], sems.at[p, 1]
                ),
            )

        for p in range(1, members):

            @pl.when(asked[p] > 0)
            def _(p=p):
                for copy in copies(p):
                    copy.start()

        for p in range(1, members):

            @pl.when(asked[p] > 0)
            def _(p=p):
                for copy in copies(p):
                    copy.wait()

    scalar = pl.BlockSpec(memory_space=pltpu.SMEM)
    return pl.pallas_call(
        body,
        in_specs=[scalar, scalar] + [pl.BlockSpec(memory_space=pl.ANY)] * 2,
        out_specs=pl.BlockSpec(memory_space=pl.ANY),
        out_shape=jax.ShapeDtypeStruct((members, rows + extra, width), BF),
        scratch_shapes=[pltpu.SemaphoreType.DMA((members, 2))],
        compiler_params=pltpu.CompilerParams(vmem_limit_bytes=VMEM),
        cost_estimate=pl.CostEstimate(
            flops=0, bytes_accessed=members * rows * width * 4, transcendentals=0
        ),
        name="collect",
    )(asked, place, points, tails)


def lift(charges, leaf_basis, transfer, slots, members):
    leaf_count, leaf_size, rank = leaf_basis.shape
    columns = charges.shape[0]

    def body(slots, charges, basis, transfer, out, sums):
        t = pl.program_id(0)

        @pl.when(t == 0)
        def _():
            sums[...] = jnp.zeros_like(sums)

        skeleton = jnp.dot(charges[...], basis[0], preferred_element_type=F32).astype(BF)
        sums[slots[t]] += jnp.dot(skeleton, transfer[0], preferred_element_type=F32)

        @pl.when(t == leaf_count - 1)
        def _():
            out[...] = sums[...].astype(BF)

    return pl.pallas_call(
        body,
        grid_spec=pltpu.PrefetchScalarGridSpec(
            num_scalar_prefetch=1,
            grid=(leaf_count,),
            in_specs=[
                pl.BlockSpec((columns, leaf_size), lambda t, s: (0, t)),
                pl.BlockSpec((1, leaf_size, rank), lambda t, s: (t, 0, 0)),
                pl.BlockSpec((1, rank, rank), lambda t, s: (t, 0, 0)),
            ],
            out_specs=pl.BlockSpec((members, columns, rank), lambda t, s: (0, 0, 0)),
            scratch_shapes=[pltpu.VMEM((members, columns, rank), F32)],
        ),
        out_shape=jax.ShapeDtypeStruct((members, columns, rank), BF),
        compiler_params=params(),
        name="lift",
    )(slots, charges, leaf_basis, transfer)


def finish(fields, slots, transfer, leaf_basis, total):
    leaf_count, leaf_size, rank = leaf_basis.shape
    columns = total.shape[0]

    def body(slots, field, transfer, basis, total, out):
        descended = lax.dot_general(
            field[0], transfer[0], NT, preferred_element_type=F32
        ).astype(BF)
        out[...] = total[...] + lax.dot_general(
            descended, basis[0], NT, preferred_element_type=F32
        )

    return pl.pallas_call(
        body,
        grid_spec=pltpu.PrefetchScalarGridSpec(
            num_scalar_prefetch=1,
            grid=(leaf_count,),
            in_specs=[
                pl.BlockSpec((1, columns, rank), lambda t, s: (s[t], 0, 0)),
                pl.BlockSpec((1, rank, rank), lambda t, s: (t, 0, 0)),
                pl.BlockSpec((1, leaf_size, rank), lambda t, s: (t, 0, 0)),
                pl.BlockSpec((columns, leaf_size), lambda t, s: (0, t)),
            ],
            out_specs=pl.BlockSpec((columns, leaf_size), lambda t, s: (0, t)),
        ),
        out_shape=jax.ShapeDtypeStruct(total.shape, F32),
        compiler_params=params(),
        name="finish",
    )(slots, fields, transfer, leaf_basis, total)


def gauss(source, source_norms, target, target_norms, scale):
    gram = lax.dot_general(source, target, NT, preferred_element_type=F32)
    return jnp.exp2((2.0 * scale) * gram - (source_norms + target_norms)).astype(BF)


def own_body(scale, leaf_size, first, second, ti, sj, ci, cj, out, rows, col):
    step = pl.program_id(0)
    width = ti.shape[1]
    i0 = pl.multiple_of(first[step] * leaf_size, leaf_size)
    j0 = pl.multiple_of(second[step] * leaf_size, leaf_size)
    ones = jnp.ones((8, width), BF)
    lanes = jnp.ones((width, TILE_LANES), BF)

    @pl.when(step == 0)
    def _():
        out[...] = jnp.zeros_like(out)

    @pl.when(i0 == j0)
    def _():
        wide = sj[...].astype(F32)
        square = wide * wide
        high = square.astype(BF)
        low = (square - high.astype(F32)).astype(BF)
        row = lax.dot_general(ones, high, NT, preferred_element_type=F32) + lax.dot_general(
            ones, low, NT, preferred_element_type=F32
        )
        rows[:, pl.ds(i0, leaf_size)] = scale * row
        column = jnp.dot(high, lanes, preferred_element_type=F32) + jnp.dot(
            low, lanes, preferred_element_type=F32
        )
        col[pl.ds(i0, leaf_size), :] = scale * column

    gram = lax.dot_general(sj[...], ti[...], NT, preferred_element_type=F32)
    norms = col[pl.ds(j0, leaf_size), :][:, :1] + rows[0:1, pl.ds(i0, leaf_size)]
    kernel = jnp.exp2((2.0 * scale) * gram - norms).astype(BF)
    out[:, pl.ds(i0, leaf_size)] += jnp.dot(cj[...], kernel, preferred_element_type=F32)

    @pl.when(i0 != j0)
    def _():
        out[:, pl.ds(j0, leaf_size)] += lax.dot_general(
            ci[...], kernel, NT, preferred_element_type=F32
        )


def own(points, charges, leaf_count, leaf_size, gamma):
    width = points.shape[1]
    columns = charges.shape[0]
    total = points.shape[0]
    pairs = [(i, j) for j in range(leaf_count) for i in range(j, -1, -1)]
    first = jnp.array([p[0] for p in pairs], jnp.int32)
    second = jnp.array([p[1] for p in pairs], jnp.int32)
    return pl.pallas_call(
        functools.partial(own_body, gamma * LOG2E, leaf_size),
        grid_spec=pltpu.PrefetchScalarGridSpec(
            num_scalar_prefetch=2,
            grid=(len(pairs),),
            in_specs=[
                pl.BlockSpec((leaf_size, width), lambda s, a, b: (a[s], 0)),
                pl.BlockSpec((leaf_size, width), lambda s, a, b: (b[s], 0)),
                pl.BlockSpec((columns, leaf_size), lambda s, a, b: (0, a[s])),
                pl.BlockSpec((columns, leaf_size), lambda s, a, b: (0, b[s])),
            ],
            out_specs=[
                pl.BlockSpec((columns, total), lambda s, a, b: (0, 0)),
                pl.BlockSpec((8, total), lambda s, a, b: (0, 0)),
            ],
            scratch_shapes=[pltpu.VMEM((total, TILE_LANES), F32)],
        ),
        out_shape=[
            jax.ShapeDtypeStruct((columns, total), F32),
            jax.ShapeDtypeStruct((8, total), F32),
        ],
        compiler_params=params(),
        cost_estimate=pl.CostEstimate(
            flops=2 * len(pairs) * leaf_size * leaf_size * (width + 2 * columns),
            bytes_accessed=total * width * 8,
            transcendentals=len(pairs) * leaf_size * leaf_size,
        ),
        name="own",
    )(first, second, points, points, charges, charges)


def near_body(scale, near_count, owner, live, fetched, targets, target_norms, before, out):
    e = pl.program_id(0)
    columns, leaf_size = before.shape
    width = fetched.shape[2]

    @pl.when(e % near_count == 0)
    def _():
        out[...] = before[...]

    @pl.when(live[e] > 0)
    def _():
        source = fetched[0, 0:leaf_size, :]
        wide = source.astype(F32)
        norms = scale * jnp.sum(wide * wide, axis=1, keepdims=True)
        across = leaf_size // TILE_LANES
        per_row = width // TILE_LANES
        lines = []
        for g in range(columns // TILE_ROWS):
            line = []
            for q in range(across):
                k = g * across + q
                row = leaf_size + TILE_ROWS * (k // per_row)
                lane = TILE_LANES * (k % per_row)
                line.append(fetched[0, row : row + TILE_ROWS, lane : lane + TILE_LANES])
            lines.append(jnp.concatenate(line, axis=1))
        charges = jnp.concatenate(lines, axis=0)
        kernel = gauss(source, norms, targets[...], target_norms[0:1, :], scale)
        out[...] += jnp.dot(charges, kernel, preferred_element_type=F32)


def near(fetched, owner, live, points, norms, before, leaf_size, near_count, gamma):
    width = points.shape[1]
    columns = before.shape[0]
    entries = owner.shape[0]
    rows = fetched.shape[1]
    return pl.pallas_call(
        functools.partial(near_body, gamma * LOG2E, near_count),
        grid_spec=pltpu.PrefetchScalarGridSpec(
            num_scalar_prefetch=2,
            grid=(entries,),
            in_specs=[
                pl.BlockSpec((1, rows, width), lambda e, o, v: (o[e], 0, 0)),
                pl.BlockSpec((leaf_size, width), lambda e, o, v: (e // near_count, 0)),
                pl.BlockSpec((8, leaf_size), lambda e, o, v: (0, e // near_count)),
                pl.BlockSpec((columns, leaf_size), lambda e, o, v: (0, e // near_count)),
            ],
            out_specs=pl.BlockSpec((columns, leaf_size), lambda e, o, v: (0, e // near_count)),
        ),
        out_shape=jax.ShapeDtypeStruct(before.shape, F32),
        compiler_params=params(),
        cost_estimate=pl.CostEstimate(
            flops=2 * entries * leaf_size * leaf_size * (width + columns),
            bytes_accessed=entries * rows * width * 2 + points.size * 2,
            transcendentals=entries * leaf_size * leaf_size,
        ),
        name="near",
    )(owner, live, fetched, points, norms, before)


def after(value, *others):
    return lax.optimization_barrier((value, *others))[0]


def local(points, charges, near_list, leaf_basis, transfer, parent, coarse_far, coarse_coupling):
    leaf_count, leaf_size, rank = leaf_basis.shape
    width = points.shape[1]
    columns = charges.shape[0]
    near_count = near_list.shape[1]
    members = lax.axis_size("sub")
    groups = lax.axis_size("grp")
    gamma = 2.0 / width
    here = lax.axis_index("sub")
    y, z = here // RING, here % RING

    entries = near_list.reshape(1, -1)
    lists = jnp.concatenate(around_z(entries), axis=0)
    lists = jnp.concatenate(around_y(lists), axis=0)
    hit = lists // leaf_count == here
    asked = jnp.sum(jnp.where(hit & (lists >= 0), lists % leaf_count + 1, 0), axis=1)

    slots = (parent % RING - z) % RING * RING + parent // RING
    partial_sums = lift(charges, leaf_basis, transfer, slots, members)
    parts = partial_sums.reshape(RING, RING, columns, rank)
    column = parts[0].astype(F32)
    for k in range(1, RING):
        column = column + turn(parts[k], 0, k).astype(F32)
    summed = around_y(column.astype(BF))
    row_weights = sum(part.astype(F32) for part in summed).astype(BF)
    weights = jnp.concatenate(around_z(row_weights), axis=0)

    lines, across, per_row = columns // TILE_ROWS, leaf_size // TILE_LANES, width // TILE_LANES
    pieces = lines * across
    deep = -(-pieces // per_row)
    tails = charges.reshape(lines, TILE_ROWS, leaf_count, across, TILE_LANES)
    tails = tails.transpose(2, 0, 3, 1, 4).reshape(leaf_count, pieces, TILE_ROWS, TILE_LANES)
    tails = jnp.pad(tails, ((0, 0), (0, deep * per_row - pieces), (0, 0), (0, 0)))
    tails = tails.reshape(leaf_count, deep, per_row, TILE_ROWS, TILE_LANES)
    tails = tails.transpose(0, 1, 3, 2, 4).reshape(leaf_count, deep * TILE_ROWS, width)

    sent = collect(
        points.reshape(leaf_count, leaf_size, width),
        tails,
        asked,
        jnp.stack([y, z]).astype(jnp.int32),
    )
    fetched = lax.all_to_all(
        after(sent, weights), "sub", split_axis=0, concat_axis=0, tiled=True
    )
    total, norms = own(after(points, sent), charges, leaf_count, leaf_size, gamma)

    chips = groups // 2
    mine = jnp.concatenate(
        [weights]
        + [
            lax.ppermute(weights, "grp", [(i, (i + 2 * k) % groups) for i in range(groups)])
            for k in range(1, chips)
        ],
        axis=0,
    )
    other = lax.ppermute(mine, "grp", [(i, i ^ 1) for i in range(groups)])
    far_ids = coarse_far[0]
    far_alive = (far_ids >= 0).astype(F32)
    ids = jnp.maximum(far_ids, 0)
    group = lax.axis_index("grp")
    from_group, node = ids // members, ids % members
    side = (from_group % 2) != (group % 2)
    at = (group // 2 - from_group // 2) % chips * members
    at = at + (z - node % RING) % RING * RING + node // RING
    sources = jnp.where(side[:, None, None], other[at], mine[at])
    far_terms = lax.dot_general(
        sources, coarse_coupling[0], (((2,), (1,)), ((0,), (0,))), preferred_element_type=F32
    )
    field = jnp.sum(far_terms * far_alive[:, None, None], axis=0).astype(BF)
    fields = jnp.concatenate(around_y(after(field, total)[None]), axis=0)
    fields = jnp.concatenate(around_z(fields), axis=0)
    places = (z - parent % RING) % RING * RING + (y - parent // RING) % RING

    flat = near_list.reshape(-1)
    live = (flat >= 0).astype(jnp.int32)
    owner = jnp.where(flat >= 0, flat // leaf_count, 0)
    total = near(fetched, owner, live, points, norms, total, leaf_size, near_count, gamma)
    return finish(fields, places, transfer, leaf_basis, total)


def solution(mesh):
    placed = (
        P(("grp", "sub"), None),
        P(None, ("grp", "sub")),
        P(("grp", "sub"), None),
        P(("grp", "sub"), None, None),
        P(("grp", "sub"), None, None),
        P(("grp", "sub")),
        P(("grp", "sub"), None),
        P(("grp", "sub"), None, None, None),
    )
    return jax.shard_map(
        local, mesh=mesh, in_specs=placed, out_specs=P(None, ("grp", "sub")), check_vma=False
    )
```

```python
import functools

import jax
import jax.numpy as jnp
from jax import lax
from jax.experimental import pallas as pl
from jax.experimental.pallas import tpu as pltpu
from jax.sharding import PartitionSpec as P

BF = jnp.bfloat16
F32 = jnp.float32
LOG2E = 1.4426950408889634
TILE_ROWS = 16
TILE_LANES = 128
RING = 4
QUARTERS = 4
DIRECTIONS = [(axis, way) for axis in range(2) for way in range(2)]
NT = (((1,), (1,)), ((), ()))
VMEM = 40 * 1024 * 1024


def params(n=1):
    return pltpu.CompilerParams(dimension_semantics=("arbitrary",) * n, vmem_limit_bytes=VMEM)


def offset(axis, along, across):
    return (along, across) if axis == 0 else (across, along)


def number(steps):
    return steps[0] * RING + steps[1]


def one(way):
    return 1 if way == 0 else RING - 1


def step(block, direction):
    return turn(block, *offset(direction[0], one(direction[1]), 0))


def turn(block, y, z):
    pairs = [
        (d, (d // RING + y) % RING * RING + (d % RING + z) % RING) for d in range(RING * RING)
    ]
    return lax.ppermute(block, "sub", pairs)


def around_y(block):
    return [block] + [turn(block, y, 0) for y in range(1, RING)]


def around_z(block):
    return [block] + [turn(block, 0, z) for z in range(1, RING)]


def collect(points, tails, asked, place, plans):
    pieces, rows, width = points.shape
    extra = tails.shape[1]
    sizes = [sum(run[2] for run in plan) for plan in plans]
    runs = []
    for number, plan in enumerate(plans):
        at = 0
        for steps, quarter, length in plan:
            runs.append((number, at, steps, quarter, length))
            at += length

    def body(asked, place, points, tails, *rest):
        outs, sems = rest[:-1], rest[-1]

        def wanted(steps):
            y = (place[0] + steps[0]) % RING
            z = (place[1] + steps[1]) % RING
            return asked[y * RING + z]

        def copies(k):
            number, at, steps, quarter, length = runs[k]
            first = jnp.maximum(wanted(steps) - 1, 0) * QUARTERS + quarter
            return (
                pltpu.make_async_copy(
                    points.at[pl.ds(first, length)],
                    outs[number].at[pl.ds(at, length), pl.ds(0, rows)],
                    sems.at[k, 0],
                ),
                pltpu.make_async_copy(
                    tails.at[pl.ds(first, length)],
                    outs[number].at[pl.ds(at, length), pl.ds(rows, extra)],
                    sems.at[k, 1],
                ),
            )

        for k in range(len(runs)):

            @pl.when(wanted(runs[k][2]) > 0)
            def _(k=k):
                for copy in copies(k):
                    copy.start()

        for k in range(len(runs)):

            @pl.when(wanted(runs[k][2]) > 0)
            def _(k=k):
                for copy in copies(k):
                    copy.wait()

    scalar = pl.BlockSpec(memory_space=pltpu.SMEM)
    return pl.pallas_call(
        body,
        in_specs=[scalar, scalar] + [pl.BlockSpec(memory_space=pl.ANY)] * 2,
        out_specs=[pl.BlockSpec(memory_space=pltpu.HBM)] * len(plans),
        out_shape=[jax.ShapeDtypeStruct((n, rows + extra, width), BF) for n in sizes],
        scratch_shapes=[pltpu.SemaphoreType.DMA((len(runs), 2))],
        compiler_params=pltpu.CompilerParams(vmem_limit_bytes=VMEM),
        cost_estimate=pl.CostEstimate(
            flops=0, bytes_accessed=sum(sizes) * rows * width * 4, transcendentals=0
        ),
        name="collect",
    )(asked, place, points, tails)


def lift(charges, leaf_basis, transfer, slots, members):
    leaf_count, leaf_size, rank = leaf_basis.shape
    columns = charges.shape[0]

    def body(slots, charges, basis, transfer, out, sums):
        t = pl.program_id(0)

        @pl.when(t == 0)
        def _():
            sums[...] = jnp.zeros_like(sums)

        skeleton = jnp.dot(charges[...], basis[0], preferred_element_type=F32).astype(BF)
        sums[slots[t]] += jnp.dot(skeleton, transfer[0], preferred_element_type=F32)

        @pl.when(t == leaf_count - 1)
        def _():
            out[...] = sums[...].astype(BF)

    return pl.pallas_call(
        body,
        grid_spec=pltpu.PrefetchScalarGridSpec(
            num_scalar_prefetch=1,
            grid=(leaf_count,),
            in_specs=[
                pl.BlockSpec((columns, leaf_size), lambda t, s: (0, t)),
                pl.BlockSpec((1, leaf_size, rank), lambda t, s: (t, 0, 0)),
                pl.BlockSpec((1, rank, rank), lambda t, s: (t, 0, 0)),
            ],
            out_specs=pl.BlockSpec((members, columns, rank), lambda t, s: (0, 0, 0)),
            scratch_shapes=[pltpu.VMEM((members, columns, rank), F32)],
        ),
        out_shape=jax.ShapeDtypeStruct((members, columns, rank), BF),
        compiler_params=params(),
        name="lift",
    )(slots, charges, leaf_basis, transfer)


def finish(fields, slots, transfer, leaf_basis, total):
    leaf_count, leaf_size, rank = leaf_basis.shape
    columns = total.shape[0]

    def body(slots, field, transfer, basis, total, out):
        descended = lax.dot_general(
            field[0], transfer[0], NT, preferred_element_type=F32
        ).astype(BF)
        out[...] = total[...] + lax.dot_general(
            descended, basis[0], NT, preferred_element_type=F32
        )

    return pl.pallas_call(
        body,
        grid_spec=pltpu.PrefetchScalarGridSpec(
            num_scalar_prefetch=1,
            grid=(leaf_count,),
            in_specs=[
                pl.BlockSpec((1, columns, rank), lambda t, s: (s[t], 0, 0)),
                pl.BlockSpec((1, rank, rank), lambda t, s: (t, 0, 0)),
                pl.BlockSpec((1, leaf_size, rank), lambda t, s: (t, 0, 0)),
                pl.BlockSpec((columns, leaf_size), lambda t, s: (0, t)),
            ],
            out_specs=pl.BlockSpec((columns, leaf_size), lambda t, s: (0, t)),
        ),
        out_shape=jax.ShapeDtypeStruct(total.shape, F32),
        compiler_params=params(),
        name="finish",
    )(slots, fields, transfer, leaf_basis, total)


def gauss(source, source_norms, target, target_norms, scale):
    gram = lax.dot_general(source, target, NT, preferred_element_type=F32)
    return jnp.exp2((2.0 * scale) * gram - (source_norms + target_norms)).astype(BF)


def own_body(scale, leaf_size, first, second, ti, sj, ci, cj, *rest):
    before, (out, rows, col) = rest[:-3], rest[-3:]
    step = pl.program_id(0)
    width = ti.shape[1]
    i0 = pl.multiple_of(first[step] * leaf_size, leaf_size)
    j0 = pl.multiple_of(second[step] * leaf_size, leaf_size)
    ones = jnp.ones((8, width), BF)
    lanes = jnp.ones((width, TILE_LANES), BF)

    @pl.when(step == 0)
    def _():
        if before:
            out[...] = before[0][...]
            rows[...] = before[1][...]
        else:
            out[...] = jnp.zeros_like(out)
            rows[...] = jnp.zeros_like(rows)

    @pl.when(i0 == j0)
    def _():
        wide = sj[...].astype(F32)
        square = wide * wide
        high = square.astype(BF)
        low = (square - high.astype(F32)).astype(BF)
        row = lax.dot_general(ones, high, NT, preferred_element_type=F32) + lax.dot_general(
            ones, low, NT, preferred_element_type=F32
        )
        rows[:, pl.ds(i0, leaf_size)] = scale * row
        column = jnp.dot(high, lanes, preferred_element_type=F32) + jnp.dot(
            low, lanes, preferred_element_type=F32
        )
        col[pl.ds(i0, leaf_size), :] = scale * column

    gram = lax.dot_general(sj[...], ti[...], NT, preferred_element_type=F32)
    norms = col[pl.ds(j0, leaf_size), :][:, :1] + rows[0:1, pl.ds(i0, leaf_size)]
    kernel = jnp.exp2((2.0 * scale) * gram - norms).astype(BF)
    out[:, pl.ds(i0, leaf_size)] += jnp.dot(cj[...], kernel, preferred_element_type=F32)

    @pl.when(i0 != j0)
    def _():
        out[:, pl.ds(j0, leaf_size)] += lax.dot_general(
            ci[...], kernel, NT, preferred_element_type=F32
        )


def own(points, charges, columns_of, leaf_size, gamma, before=()):
    width = points.shape[1]
    columns = charges.shape[0]
    total = points.shape[0]
    pairs = [(i, j) for j in columns_of for i in range(j, -1, -1)]
    first = jnp.array([p[0] for p in pairs], jnp.int32)
    second = jnp.array([p[1] for p in pairs], jnp.int32)
    return pl.pallas_call(
        functools.partial(own_body, gamma * LOG2E, leaf_size),
        grid_spec=pltpu.PrefetchScalarGridSpec(
            num_scalar_prefetch=2,
            grid=(len(pairs),),
            in_specs=[
                pl.BlockSpec((leaf_size, width), lambda s, a, b: (a[s], 0)),
                pl.BlockSpec((leaf_size, width), lambda s, a, b: (b[s], 0)),
                pl.BlockSpec((columns, leaf_size), lambda s, a, b: (0, a[s])),
                pl.BlockSpec((columns, leaf_size), lambda s, a, b: (0, b[s])),
            ]
            + [pl.BlockSpec(b.shape, lambda s, a, b: (0, 0)) for b in before],
            out_specs=[
                pl.BlockSpec((columns, total), lambda s, a, b: (0, 0)),
                pl.BlockSpec((8, total), lambda s, a, b: (0, 0)),
            ],
            scratch_shapes=[pltpu.VMEM((total, TILE_LANES), F32)],
        ),
        out_shape=[
            jax.ShapeDtypeStruct((columns, total), F32),
            jax.ShapeDtypeStruct((8, total), F32),
        ],
        compiler_params=params(),
        cost_estimate=pl.CostEstimate(
            flops=2 * len(pairs) * leaf_size * leaf_size * (width + 2 * columns),
            bytes_accessed=total * width * 8,
            transcendentals=len(pairs) * leaf_size * leaf_size,
        ),
        name="own",
    )(first, second, points, points, charges, charges, *before)


def near_body(scale, groups, leaf_size, target, points, norms, before, *refs):
    buffers, out = refs[:-1], refs[-1]
    columns = before.shape[0]
    rows = buffers[0].shape[1] - TILE_ROWS
    out[...] = before[...]
    for units, source_steps in groups:
        leaf = target[source_steps]

        @pl.when(leaf >= 0)
        def _(units=units, leaf=leaf):
            source = jnp.concatenate([buffers[b][u, 0:rows, :] for b, u in units], axis=0)
            charges = jnp.concatenate(
                [
                    jnp.concatenate(
                        [
                            buffers[b][u, rows:, g * TILE_LANES : (g + 1) * TILE_LANES]
                            for g in range(columns // TILE_ROWS)
                        ],
                        axis=0,
                    )
                    for b, u in units
                ],
                axis=1,
            )
            wide = source.astype(F32)
            source_norms = scale * jnp.sum(wide * wide, axis=1, keepdims=True)
            start = pl.multiple_of(leaf * leaf_size, leaf_size)
            kernel = gauss(
                source,
                source_norms,
                points[pl.ds(start, leaf_size), :],
                norms[0:1, pl.ds(start, leaf_size)],
                scale,
            )
            out[:, pl.ds(start, leaf_size)] += jnp.dot(
                charges, kernel, preferred_element_type=F32
            )


def near(buffers, groups, target, points, norms, before, leaf_size, gamma):
    width = points.shape[1]
    columns = before.shape[0]
    rows = sum(len(units) for units, _ in groups) * TILE_LANES
    whole = pl.BlockSpec(memory_space=pltpu.VMEM)
    return pl.pallas_call(
        functools.partial(near_body, gamma * LOG2E, groups, leaf_size),
        in_specs=[pl.BlockSpec(memory_space=pltpu.SMEM)] + [whole] * (3 + len(buffers)),
        out_specs=whole,
        out_shape=jax.ShapeDtypeStruct(before.shape, F32),
        compiler_params=pltpu.CompilerParams(vmem_limit_bytes=VMEM),
        cost_estimate=pl.CostEstimate(
            flops=2 * rows * leaf_size * (width + columns),
            bytes_accessed=rows * width * 2 + points.size * 2,
            transcendentals=rows * leaf_size,
        ),
        name="near",
    )(target, points, norms, before, *buffers)


def after(value, *others):
    return lax.optimization_barrier((value, *others))[0]


def local(points, charges, near_list, leaf_basis, transfer, parent, coarse_far, coarse_coupling):
    leaf_count, leaf_size, rank = leaf_basis.shape
    width = points.shape[1]
    columns = charges.shape[0]
    near_count = near_list.shape[1]
    members = lax.axis_size("sub")
    groups = lax.axis_size("grp")
    gamma = 2.0 / width
    here = lax.axis_index("sub")
    y, z = here // RING, here % RING

    entries = near_list.reshape(-1)
    wanted = (entries // leaf_count)[None, :] == jnp.arange(members)[:, None]
    wanted = wanted & (entries >= 0)[None, :]
    requests = jnp.sum(jnp.where(wanted, entries[None, :] % leaf_count + 1, 0), axis=1)
    asked = lax.all_to_all(requests[:, None], "sub", split_axis=0, concat_axis=0, tiled=True)
    asked = asked[:, 0]

    slots = (parent % RING - z) % RING * RING + parent // RING
    partial_sums = lift(charges, leaf_basis, transfer, slots, members)
    parts = partial_sums.reshape(RING, RING, columns, rank)
    column = parts[0].astype(F32)
    for k in range(1, RING):
        column = column + turn(parts[k], 0, k).astype(F32)
    summed = around_y(column.astype(BF))
    row_weights = sum(part.astype(F32) for part in summed).astype(BF)
    weights = jnp.concatenate(around_z(row_weights), axis=0)

    pieces, rows = leaf_count * QUARTERS, leaf_size // QUARTERS
    lines = columns // TILE_ROWS
    tails = charges.reshape(lines, TILE_ROWS, pieces, rows).transpose(2, 1, 0, 3)
    tails = tails.reshape(pieces, TILE_ROWS, lines * rows)
    tails = jnp.pad(tails, ((0, 0), (0, 0), (0, width - lines * rows)))

    plans = [[], [], []]
    for axis, way in DIRECTIONS:
        h = axis * (QUARTERS // 2)
        plans[0].append(
            [(offset(axis, 2, 0), 2 * way, 2)]
            + [(offset(axis, 2, across), h + way, 1) for across in (1, 3, 2)]
        )
        plans[1].append([(offset(axis, one(way), across), h, 2) for across in (1, 3, 2)])
        plans[2].append([(offset(axis, one(way), 0), 0, QUARTERS)])
    blocks = collect(
        points.reshape(pieces, rows, width),
        tails,
        asked,
        jnp.stack([y, z]).astype(jnp.int32),
        plans[0] + plans[1] + plans[2],
    )
    count = len(DIRECTIONS)

    def send(wait, values):
        return [step(v, d) for v, d in zip(held(wait, values), DIRECTIONS)]

    def held(wait, values):
        return [after(v, w, *wait[1:]) for v, w in zip(values, wait[0])]

    half = leaf_count * 2 // 3
    chips = groups // 2

    def along_x(k, block, *gate):
        pairs = [(i, (i + 2 * k) % groups) for i in range(groups)]
        return lax.ppermute(after(block, *gate), "grp", pairs)

    got_1 = [step(v, d) for v, d in zip(blocks[:count], DIRECTIONS)]
    x_1 = along_x(1, weights, blocks[0])
    total, norms = own(after(points, blocks[0]), charges, range(half), leaf_size, gamma)
    got_2 = send((got_1, total, x_1), blocks[count : 2 * count])
    x_2 = along_x(2, weights, got_1[0])
    total, norms = own(
        after(points, got_1[0]),
        charges,
        range(half, leaf_count),
        leaf_size,
        gamma,
        (total, norms),
    )
    got_3 = send((got_2, total, x_2), got_1)
    x_3 = along_x(3, weights, got_2[0])
    got_4 = send((got_3, x_3), blocks[2 * count :])
    mine = jnp.concatenate([weights, x_1, x_2, x_3], axis=0)
    other = lax.ppermute(mine, "grp", [(i, i ^ 1) for i in range(groups)])
    block_5, block_6 = [], []
    for axis, way in DIRECTIONS:
        first = 2 * (1 - axis)
        plus, minus = got_2[first], got_2[first + 1]
        turned = got_3[first : first + 2]
        block_5.append(
            jnp.concatenate(
                [plus[4 + way :][:1], minus[4 + way :][:1], turned[way][4:]], axis=0
            )
        )
        block_6.append(
            jnp.concatenate(
                [plus[2 * way :][:2], minus[2 * way :][:2]]
                + [block[2 + way :][:1] for block in turned],
                axis=0,
            )
        )
    add = functools.partial(near, leaf_size=leaf_size, gamma=gamma)
    groups_3, groups_4, groups_6, groups_7 = [], [], [], []
    for d, (axis, way) in enumerate(DIRECTIONS):
        groups_3.append(([(d, 0), (d, 1)], number(offset(axis, 2, 0))))
        for k in range(0, QUARTERS, 2):
            groups_4.append(([(d, k), (d, k + 1)], number(offset(axis, one(way), 0))))
        for k, along in enumerate((1, 3, 2)):
            pair = [(d, 2 * k), (d, 2 * k + 1)]
            groups_6.append((pair, number(offset(1 - axis, along, one(way)))))
            if way == 0:
                groups_7.append(([(d, k), (d + 1, k)], number(offset(1 - axis, along, 2))))
    flat = near_list.reshape(-1)
    owner = jnp.where(flat >= 0, flat // leaf_count, 0)
    back = (y - owner // RING) % RING * RING + (z - owner % RING) % RING
    leaves = jnp.arange(flat.shape[0]) // near_count + 1
    match = (back[None, :] == jnp.arange(members)[:, None]) & (flat >= 0)[None, :]
    target = jnp.sum(jnp.where(match, leaves[None, :], 0), axis=1) - 1
    total = add(got_3, groups_3, target, points, norms, after(total, *block_6))
    got_5 = send((got_4, total), block_5)
    total = add(got_4, groups_4, target, points, norms, total)
    got_6 = send((got_5, total), block_6)

    far_ids = coarse_far[0]
    far_alive = (far_ids >= 0).astype(F32)
    ids = jnp.maximum(far_ids, 0)
    group = lax.axis_index("grp")
    from_group, node = ids // members, ids % members
    side = (from_group % 2) != (group % 2)
    at = (group // 2 - from_group // 2) % chips * members
    at = at + (z - node % RING) % RING * RING + node // RING
    sources = jnp.where(side[:, None, None], other[at], mine[at])
    far_terms = lax.dot_general(
        sources, coarse_coupling[0], (((2,), (1,)), ((0,), (0,))), preferred_element_type=F32
    )
    field = jnp.sum(far_terms * far_alive[:, None, None], axis=0).astype(BF)
    fields = lax.all_to_all(
        jnp.broadcast_to(after(field, got_5[0])[None], (members, columns, rank)),
        "sub",
        split_axis=0,
        concat_axis=0,
        tiled=True,
    )
    got_7 = send((got_6,), got_5)
    total = add(got_6, groups_6, target, points, norms, total)
    total = add(got_7, groups_7, target, points, norms, total)
    return finish(fields, parent, transfer, leaf_basis, total)


def solution(mesh):
    placed = (
        P(("grp", "sub"), None),
        P(None, ("grp", "sub")),
        P(("grp", "sub"), None),
        P(("grp", "sub"), None, None),
        P(("grp", "sub"), None, None),
        P(("grp", "sub")),
        P(("grp", "sub"), None),
        P(("grp", "sub"), None, None, None),
    )
    return jax.shard_map(
        local, mesh=mesh, in_specs=placed, out_specs=P(None, ("grp", "sub")), check_vma=False
    )
```

```python
import functools

import jax
import jax.numpy as jnp
from jax import lax
from jax.experimental import pallas as pl
from jax.experimental.pallas import tpu as pltpu
from jax.sharding import PartitionSpec as P

BF = jnp.bfloat16
F32 = jnp.float32
LOG2E = 1.4426950408889634
TILE_ROWS = 16
TILE_LANES = 128
RING = 4
QUARTERS = 4
DIRECTIONS = [(axis, way) for axis in range(2) for way in range(2)]
NT = (((1,), (1,)), ((), ()))
VMEM = 40 * 1024 * 1024


def params(n=1):
    return pltpu.CompilerParams(dimension_semantics=("arbitrary",) * n, vmem_limit_bytes=VMEM)


def offset(axis, along, across):
    return (along, across) if axis == 0 else (across, along)


def number(steps):
    return steps[0] * RING + steps[1]


def one(way):
    return 1 if way == 0 else RING - 1


def step(block, direction):
    return turn(block, *offset(direction[0], one(direction[1]), 0))


def turn(block, y, z):
    pairs = [
        (d, (d // RING + y) % RING * RING + (d % RING + z) % RING) for d in range(RING * RING)
    ]
    return lax.ppermute(block, "sub", pairs)


def collect(points, tails, asked, place, plans):
    pieces, rows, width = points.shape
    extra = tails.shape[1]
    sizes = [sum(run[2] for run in plan) for plan in plans]
    runs = []
    for number, plan in enumerate(plans):
        at = 0
        for steps, quarter, length in plan:
            runs.append((number, at, steps, quarter, length))
            at += length

    def body(asked, place, points, tails, *rest):
        outs, sems = rest[:-1], rest[-1]

        def wanted(steps):
            y = (place[0] + steps[0]) % RING
            z = (place[1] + steps[1]) % RING
            return asked[y * RING + z]

        def copies(k):
            number, at, steps, quarter, length = runs[k]
            first = jnp.maximum(wanted(steps) - 1, 0) * QUARTERS + quarter
            return (
                pltpu.make_async_copy(
                    points.at[pl.ds(first, length)],
                    outs[number].at[pl.ds(at, length), pl.ds(0, rows)],
                    sems.at[k, 0],
                ),
                pltpu.make_async_copy(
                    tails.at[pl.ds(first, length)],
                    outs[number].at[pl.ds(at, length), pl.ds(rows, extra)],
                    sems.at[k, 1],
                ),
            )

        for k in range(len(runs)):

            @pl.when(wanted(runs[k][2]) > 0)
            def _(k=k):
                for copy in copies(k):
                    copy.start()

        for k in range(len(runs)):

            @pl.when(wanted(runs[k][2]) > 0)
            def _(k=k):
                for copy in copies(k):
                    copy.wait()

    scalar = pl.BlockSpec(memory_space=pltpu.SMEM)
    return pl.pallas_call(
        body,
        in_specs=[scalar, scalar] + [pl.BlockSpec(memory_space=pl.ANY)] * 2,
        out_specs=[pl.BlockSpec(memory_space=pltpu.HBM)] * len(plans),
        out_shape=[jax.ShapeDtypeStruct((n, rows + extra, width), BF) for n in sizes],
        scratch_shapes=[pltpu.SemaphoreType.DMA((len(runs), 2))],
        compiler_params=pltpu.CompilerParams(vmem_limit_bytes=VMEM),
        cost_estimate=pl.CostEstimate(
            flops=0, bytes_accessed=sum(sizes) * rows * width * 4, transcendentals=0
        ),
        name="collect",
    )(asked, place, points, tails)


def lift(charges, leaf_basis, transfer, slots, members):
    leaf_count, leaf_size, rank = leaf_basis.shape
    columns = charges.shape[0]

    def body(slots, charges, basis, transfer, out, sums):
        t = pl.program_id(0)

        @pl.when(t == 0)
        def _():
            sums[...] = jnp.zeros_like(sums)

        skeleton = jnp.dot(charges[...], basis[0], preferred_element_type=F32).astype(BF)
        sums[slots[t]] += jnp.dot(skeleton, transfer[0], preferred_element_type=F32)

        @pl.when(t == leaf_count - 1)
        def _():
            out[...] = sums[...].astype(BF)

    return pl.pallas_call(
        body,
        grid_spec=pltpu.PrefetchScalarGridSpec(
            num_scalar_prefetch=1,
            grid=(leaf_count,),
            in_specs=[
                pl.BlockSpec((columns, leaf_size), lambda t, s: (0, t)),
                pl.BlockSpec((1, leaf_size, rank), lambda t, s: (t, 0, 0)),
                pl.BlockSpec((1, rank, rank), lambda t, s: (t, 0, 0)),
            ],
            out_specs=pl.BlockSpec((members, columns, rank), lambda t, s: (0, 0, 0)),
            scratch_shapes=[pltpu.VMEM((members, columns, rank), F32)],
        ),
        out_shape=jax.ShapeDtypeStruct((members, columns, rank), BF),
        compiler_params=params(),
        name="lift",
    )(slots, charges, leaf_basis, transfer)


def finish(fields, slots, transfer, leaf_basis, total):
    leaf_count, leaf_size, rank = leaf_basis.shape
    columns = total.shape[0]

    def body(slots, field, transfer, basis, total, out):
        descended = lax.dot_general(
            field[0], transfer[0], NT, preferred_element_type=F32
        ).astype(BF)
        out[...] = total[...] + lax.dot_general(
            descended, basis[0], NT, preferred_element_type=F32
        )

    return pl.pallas_call(
        body,
        grid_spec=pltpu.PrefetchScalarGridSpec(
            num_scalar_prefetch=1,
            grid=(leaf_count,),
            in_specs=[
                pl.BlockSpec((1, columns, rank), lambda t, s: (s[t], 0, 0)),
                pl.BlockSpec((1, rank, rank), lambda t, s: (t, 0, 0)),
                pl.BlockSpec((1, leaf_size, rank), lambda t, s: (t, 0, 0)),
                pl.BlockSpec((columns, leaf_size), lambda t, s: (0, t)),
            ],
            out_specs=pl.BlockSpec((columns, leaf_size), lambda t, s: (0, t)),
        ),
        out_shape=jax.ShapeDtypeStruct(total.shape, F32),
        compiler_params=params(),
        name="finish",
    )(slots, fields, transfer, leaf_basis, total)


def gauss(source, source_norms, target, target_norms, scale):
    gram = lax.dot_general(source, target, NT, preferred_element_type=F32)
    return jnp.exp2((2.0 * scale) * gram - (source_norms + target_norms)).astype(BF)


def own_body(scale, leaf_size, first, second, ti, sj, ci, cj, *rest):
    before, (out, rows, col) = rest[:-3], rest[-3:]
    step = pl.program_id(0)
    width = ti.shape[1]
    i0 = pl.multiple_of(first[step] * leaf_size, leaf_size)
    j0 = pl.multiple_of(second[step] * leaf_size, leaf_size)
    ones = jnp.ones((8, width), BF)
    lanes = jnp.ones((width, TILE_LANES), BF)

    @pl.when(step == 0)
    def _():
        if before:
            out[...] = before[0][...]
            rows[...] = before[1][...]
        else:
            out[...] = jnp.zeros_like(out)
            rows[...] = jnp.zeros_like(rows)

    @pl.when(i0 == j0)
    def _():
        wide = sj[...].astype(F32)
        square = wide * wide
        high = square.astype(BF)
        low = (square - high.astype(F32)).astype(BF)
        row = lax.dot_general(ones, high, NT, preferred_element_type=F32) + lax.dot_general(
            ones, low, NT, preferred_element_type=F32
        )
        rows[:, pl.ds(i0, leaf_size)] = scale * row
        column = jnp.dot(high, lanes, preferred_element_type=F32) + jnp.dot(
            low, lanes, preferred_element_type=F32
        )
        col[pl.ds(i0, leaf_size), :] = scale * column

    gram = lax.dot_general(sj[...], ti[...], NT, preferred_element_type=F32)
    norms = col[pl.ds(j0, leaf_size), :][:, :1] + rows[0:1, pl.ds(i0, leaf_size)]
    kernel = jnp.exp2((2.0 * scale) * gram - norms).astype(BF)
    out[:, pl.ds(i0, leaf_size)] += jnp.dot(cj[...], kernel, preferred_element_type=F32)

    @pl.when(i0 != j0)
    def _():
        out[:, pl.ds(j0, leaf_size)] += lax.dot_general(
            ci[...], kernel, NT, preferred_element_type=F32
        )


def own(points, charges, columns_of, leaf_size, gamma, before=()):
    width = points.shape[1]
    columns = charges.shape[0]
    total = points.shape[0]
    pairs = [(i, j) for j in columns_of for i in range(j, -1, -1)]
    first = jnp.array([p[0] for p in pairs], jnp.int32)
    second = jnp.array([p[1] for p in pairs], jnp.int32)
    return pl.pallas_call(
        functools.partial(own_body, gamma * LOG2E, leaf_size),
        grid_spec=pltpu.PrefetchScalarGridSpec(
            num_scalar_prefetch=2,
            grid=(len(pairs),),
            in_specs=[
                pl.BlockSpec((leaf_size, width), lambda s, a, b: (a[s], 0)),
                pl.BlockSpec((leaf_size, width), lambda s, a, b: (b[s], 0)),
                pl.BlockSpec((columns, leaf_size), lambda s, a, b: (0, a[s])),
                pl.BlockSpec((columns, leaf_size), lambda s, a, b: (0, b[s])),
            ]
            + [pl.BlockSpec(b.shape, lambda s, a, b: (0, 0)) for b in before],
            out_specs=[
                pl.BlockSpec((columns, total), lambda s, a, b: (0, 0)),
                pl.BlockSpec((8, total), lambda s, a, b: (0, 0)),
            ],
            scratch_shapes=[pltpu.VMEM((total, TILE_LANES), F32)],
        ),
        out_shape=[
            jax.ShapeDtypeStruct((columns, total), F32),
            jax.ShapeDtypeStruct((8, total), F32),
        ],
        compiler_params=params(),
        cost_estimate=pl.CostEstimate(
            flops=2 * len(pairs) * leaf_size * leaf_size * (width + 2 * columns),
            bytes_accessed=total * width * 8,
            transcendentals=len(pairs) * leaf_size * leaf_size,
        ),
        name="own",
    )(first, second, points, points, charges, charges, *before)


def near_body(scale, groups, leaf_size, target, points, norms, before, *refs):
    buffers, out = refs[:-1], refs[-1]
    columns = before.shape[0]
    rows = buffers[0].shape[1] - TILE_ROWS
    out[...] = before[...]
    for units, source_steps in groups:
        leaf = target[source_steps]

        @pl.when(leaf >= 0)
        def _(units=units, leaf=leaf):
            source = jnp.concatenate([buffers[b][u, 0:rows, :] for b, u in units], axis=0)
            charges = jnp.concatenate(
                [
                    jnp.concatenate(
                        [
                            buffers[b][u, rows:, g * TILE_LANES : (g + 1) * TILE_LANES]
                            for g in range(columns // TILE_ROWS)
                        ],
                        axis=0,
                    )
                    for b, u in units
                ],
                axis=1,
            )
            wide = source.astype(F32)
            source_norms = scale * jnp.sum(wide * wide, axis=1, keepdims=True)
            start = pl.multiple_of(leaf * leaf_size, leaf_size)
            kernel = gauss(
                source,
                source_norms,
                points[pl.ds(start, leaf_size), :],
                norms[0:1, pl.ds(start, leaf_size)],
                scale,
            )
            out[:, pl.ds(start, leaf_size)] += jnp.dot(
                charges, kernel, preferred_element_type=F32
            )


def near(buffers, groups, target, points, norms, before, leaf_size, gamma):
    width = points.shape[1]
    columns = before.shape[0]
    rows = sum(len(units) for units, _ in groups) * TILE_LANES
    whole = pl.BlockSpec(memory_space=pltpu.VMEM)
    return pl.pallas_call(
        functools.partial(near_body, gamma * LOG2E, groups, leaf_size),
        in_specs=[pl.BlockSpec(memory_space=pltpu.SMEM)] + [whole] * (3 + len(buffers)),
        out_specs=whole,
        out_shape=jax.ShapeDtypeStruct(before.shape, F32),
        compiler_params=pltpu.CompilerParams(vmem_limit_bytes=VMEM),
        cost_estimate=pl.CostEstimate(
            flops=2 * rows * leaf_size * (width + columns),
            bytes_accessed=rows * width * 2 + points.size * 2,
            transcendentals=rows * leaf_size,
        ),
        name="near",
    )(target, points, norms, before, *buffers)


def after(value, *others):
    return lax.optimization_barrier((value, *others))[0]


def local(points, charges, near_list, leaf_basis, transfer, parent, coarse_far, coarse_coupling):
    leaf_count, leaf_size, rank = leaf_basis.shape
    width = points.shape[1]
    columns = charges.shape[0]
    near_count = near_list.shape[1]
    members = lax.axis_size("sub")
    groups = lax.axis_size("grp")
    gamma = 2.0 / width

    def exchange(block):
        return lax.all_to_all(block, "sub", split_axis=0, concat_axis=0, tiled=True)

    def spread(block):
        return jnp.broadcast_to(block[None], (members, *block.shape))

    here = lax.axis_index("sub")
    y, z = here // RING, here % RING

    entries = near_list.reshape(-1)
    wanted = (entries // leaf_count)[None, :] == jnp.arange(members)[:, None]
    wanted = wanted & (entries >= 0)[None, :]
    requests = jnp.sum(jnp.where(wanted, entries[None, :] % leaf_count + 1, 0), axis=1)
    asked = exchange(requests[:, None])[:, 0]

    partial_sums = lift(charges, leaf_basis, transfer, parent, members)

    pieces, rows = leaf_count * QUARTERS, leaf_size // QUARTERS
    lines = columns // TILE_ROWS
    tails = charges.reshape(lines, TILE_ROWS, pieces, rows).transpose(2, 1, 0, 3)
    tails = tails.reshape(pieces, TILE_ROWS, lines * rows)
    tails = jnp.pad(tails, ((0, 0), (0, 0), (0, width - lines * rows)))

    plans = [[], [], []]
    for axis, way in DIRECTIONS:
        h = axis * (QUARTERS // 2)
        plans[0].append(
            [(offset(axis, 2, 0), 2 * way, 2)]
            + [(offset(axis, 2, across), h + way, 1) for across in (1, 3, 2)]
        )
        plans[1].append([(offset(axis, one(way), across), h, 2) for across in (1, 3, 2)])
        plans[2].append([(offset(axis, one(way), 0), 0, QUARTERS)])
    blocks = collect(
        points.reshape(pieces, rows, width),
        tails,
        after(asked, partial_sums),
        jnp.stack([y, z]).astype(jnp.int32),
        plans[0] + plans[1] + plans[2],
    )
    count = len(DIRECTIONS)

    def send(wait, values):
        return [step(v, d) for v, d in zip(held(wait, values), DIRECTIONS)]

    def held(wait, values):
        return [after(v, w, *wait[1:]) for v, w in zip(values, wait[0])]

    half = leaf_count * 2 // 3
    chips = groups // 2

    def along_x(k, block, *gate):
        pairs = [(i, (i + 2 * k) % groups) for i in range(groups)]
        return lax.ppermute(after(block, *gate), "grp", pairs)

    got_1 = [step(v, d) for v, d in zip(blocks[:count], DIRECTIONS)]
    total, norms = own(after(points, blocks[0]), charges, range(half), leaf_size, gamma)
    summed = exchange(after(partial_sums, total))
    got_2 = send((got_1, total, summed), blocks[count : 2 * count])
    total, norms = own(
        after(points, got_1[0]),
        charges,
        range(half, leaf_count),
        leaf_size,
        gamma,
        (total, norms),
    )
    own_weight = jnp.sum(after(summed, total).astype(F32), axis=0).astype(BF)
    weights = exchange(spread(own_weight))
    got_3 = send((got_2, total, weights), got_1)
    x_1 = along_x(1, weights, got_2[0])
    x_2 = along_x(2, weights, got_2[0])
    got_4 = send((got_3, x_1, x_2), blocks[2 * count :])
    x_3 = along_x(3, weights, got_3[0])
    block_5, block_6 = [], []
    for axis, way in DIRECTIONS:
        first = 2 * (1 - axis)
        plus, minus = got_2[first], got_2[first + 1]
        turned = got_3[first : first + 2]
        block_5.append(
            jnp.concatenate(
                [plus[4 + way :][:1], minus[4 + way :][:1], turned[way][4:]], axis=0
            )
        )
        block_6.append(
            jnp.concatenate(
                [plus[2 * way :][:2], minus[2 * way :][:2]]
                + [block[2 + way :][:1] for block in turned],
                axis=0,
            )
        )
    add = functools.partial(near, leaf_size=leaf_size, gamma=gamma)
    groups_3, groups_4, groups_6, groups_7 = [], [], [], []
    for d, (axis, way) in enumerate(DIRECTIONS):
        groups_3.append(([(d, 0), (d, 1)], number(offset(axis, 2, 0))))
        for k in range(0, QUARTERS, 2):
            groups_4.append(([(d, k), (d, k + 1)], number(offset(axis, one(way), 0))))
        for k, along in enumerate((1, 3, 2)):
            pair = [(d, 2 * k), (d, 2 * k + 1)]
            groups_6.append((pair, number(offset(1 - axis, along, one(way)))))
            if way == 0:
                groups_7.append(([(d, k), (d + 1, k)], number(offset(1 - axis, along, 2))))
    flat = near_list.reshape(-1)
    owner = jnp.where(flat >= 0, flat // leaf_count, 0)
    back = (y - owner // RING) % RING * RING + (z - owner % RING) % RING
    leaves = jnp.arange(flat.shape[0]) // near_count + 1
    match = (back[None, :] == jnp.arange(members)[:, None]) & (flat >= 0)[None, :]
    target = jnp.sum(jnp.where(match, leaves[None, :], 0), axis=1) - 1
    total = add(got_3, groups_3, target, points, norms, after(total, *block_6))
    got_5 = send((got_4, total, x_3), block_5)
    mine = jnp.concatenate([weights, x_1, x_2, x_3], axis=0)
    other = lax.ppermute(after(mine, got_4[0]), "grp", [(i, i ^ 1) for i in range(groups)])
    total = add(got_4, groups_4, target, points, norms, total)
    got_6 = send((got_5, total, other), block_6)

    far_ids = coarse_far[0]
    far_alive = (far_ids >= 0).astype(F32)
    ids = jnp.maximum(far_ids, 0)
    group = lax.axis_index("grp")
    from_group, node = ids // members, ids % members
    side = (from_group % 2) != (group % 2)
    at = (group // 2 - from_group // 2) % chips * members
    at = at + node
    gated = after(other, got_5[0])
    sources = jnp.where(side[:, None, None], gated[at], mine[at])
    far_terms = lax.dot_general(
        sources, coarse_coupling[0], (((2,), (1,)), ((0,), (0,))), preferred_element_type=F32
    )
    field = jnp.sum(far_terms * far_alive[:, None, None], axis=0).astype(BF)
    fields = exchange(spread(field))
    got_7 = send((got_6, fields), got_5)
    total = add(got_6, groups_6, target, points, norms, total)
    total = finish(fields, parent, transfer, leaf_basis, total)
    return add(got_7, groups_7, target, points, norms, total)


def solution(mesh):
    placed = (
        P(("grp", "sub"), None),
        P(None, ("grp", "sub")),
        P(("grp", "sub"), None),
        P(("grp", "sub"), None, None),
        P(("grp", "sub"), None, None),
        P(("grp", "sub")),
        P(("grp", "sub"), None),
        P(("grp", "sub"), None, None, None),
    )
    return jax.shard_map(
        local, mesh=mesh, in_specs=placed, out_specs=P(None, ("grp", "sub")), check_vma=False
    )
```

```python
import functools

import jax
import jax.numpy as jnp
from jax import lax
from jax.experimental import pallas as pl
from jax.experimental.pallas import tpu as pltpu
from jax.sharding import PartitionSpec as P

BF = jnp.bfloat16
F32 = jnp.float32
LOG2E = 1.4426950408889634
TILE_ROWS = 16
TILE_LANES = 128
RING = 4
QUARTERS = 4
DIRECTIONS = [(axis, way) for axis in range(2) for way in range(2)]
NT = (((1,), (1,)), ((), ()))
VMEM = 24 * 1024 * 1024


def params(n=1):
    return pltpu.CompilerParams(dimension_semantics=("arbitrary",) * n, vmem_limit_bytes=VMEM)


def offset(axis, along, across):
    return (along, across) if axis == 0 else (across, along)


def number(steps):
    return steps[0] * RING + steps[1]


def one(way):
    return 1 if way == 0 else RING - 1


def step(block, direction):
    return turn(block, *offset(direction[0], one(direction[1]), 0))


def turn(block, y, z):
    pairs = [
        (d, (d // RING + y) % RING * RING + (d % RING + z) % RING) for d in range(RING * RING)
    ]
    return lax.ppermute(block, "sub", pairs)


def collect(points, tails, asked, place, plans):
    pieces, rows, width = points.shape
    extra = tails.shape[1]
    sizes = [sum(run[2] for run in plan) for plan in plans]
    runs = []
    for number, plan in enumerate(plans):
        at = 0
        for steps, quarter, length in plan:
            runs.append((number, at, steps, quarter, length))
            at += length

    def body(asked, place, points, tails, *rest):
        outs, sems = rest[:-1], rest[-1]

        def wanted(steps):
            y = (place[0] + steps[0]) % RING
            z = (place[1] + steps[1]) % RING
            return asked[y * RING + z]

        def copies(k):
            number, at, steps, quarter, length = runs[k]
            first = jnp.maximum(wanted(steps) - 1, 0) * QUARTERS + quarter
            return (
                pltpu.make_async_copy(
                    points.at[pl.ds(first, length)],
                    outs[number].at[pl.ds(at, length), pl.ds(0, rows)],
                    sems.at[k, 0],
                ),
                pltpu.make_async_copy(
                    tails.at[pl.ds(first, length)],
                    outs[number].at[pl.ds(at, length), pl.ds(rows, extra)],
                    sems.at[k, 1],
                ),
            )

        for k in range(len(runs)):

            @pl.when(wanted(runs[k][2]) > 0)
            def _(k=k):
                for copy in copies(k):
                    copy.start()

        for k in range(len(runs)):

            @pl.when(wanted(runs[k][2]) > 0)
            def _(k=k):
                for copy in copies(k):
                    copy.wait()

    scalar = pl.BlockSpec(memory_space=pltpu.SMEM)
    return pl.pallas_call(
        body,
        in_specs=[scalar, scalar] + [pl.BlockSpec(memory_space=pltpu.VMEM)] * 2,
        out_specs=[pl.BlockSpec(memory_space=pltpu.HBM)] * len(plans),
        out_shape=[jax.ShapeDtypeStruct((n, rows + extra, width), BF) for n in sizes],
        scratch_shapes=[pltpu.SemaphoreType.DMA((len(runs), 2))],
        compiler_params=pltpu.CompilerParams(vmem_limit_bytes=VMEM),
        cost_estimate=pl.CostEstimate(
            flops=0, bytes_accessed=sum(sizes) * rows * width * 4, transcendentals=0
        ),
        name="collect",
    )(asked, place, points, tails)


def weave(sources, plans):
    count = sum(len(plan) for plan in plans)
    shape = sources[0].shape[1:]
    sizes = [sum(run[2] for run in plan) for plan in plans]

    def body(*refs):
        ins, outs, sems = refs[: len(sources)], refs[len(sources) : -1], refs[-1]
        copies = []
        for plan, out in zip(plans, outs):
            at = 0
            for source, first, length in plan:
                copies.append(
                    pltpu.make_async_copy(
                        ins[source].at[pl.ds(first, length)],
                        out.at[pl.ds(at, length)],
                        sems.at[len(copies)],
                    )
                )
                at += length
        for copy in copies:
            copy.start()
        for copy in copies:
            copy.wait()

    return pl.pallas_call(
        body,
        in_specs=[pl.BlockSpec(memory_space=pltpu.VMEM)] * len(sources),
        out_specs=[pl.BlockSpec(memory_space=pltpu.HBM)] * len(plans),
        out_shape=[jax.ShapeDtypeStruct((size, *shape), BF) for size in sizes],
        scratch_shapes=[pltpu.SemaphoreType.DMA((count,))],
        compiler_params=pltpu.CompilerParams(vmem_limit_bytes=VMEM),
        cost_estimate=pl.CostEstimate(
            flops=0,
            bytes_accessed=4 * sum(sizes) * shape[0] * shape[1],
            transcendentals=0,
        ),
        name="weave",
    )(*sources)


def lift(charges, leaf_basis, transfer, slots, members, width):
    leaf_count, leaf_size, rank = leaf_basis.shape
    columns = charges.shape[0]
    lines, rows = columns // TILE_ROWS, leaf_size // QUARTERS

    def body(slots, charges, basis, transfer, out, tails, sums):
        t = pl.program_id(0)
        tails[...] = jnp.zeros_like(tails)
        for q in range(QUARTERS):
            for g in range(lines):
                tails[q, :, g * rows : (g + 1) * rows] = charges[
                    g * TILE_ROWS : (g + 1) * TILE_ROWS, q * rows : (q + 1) * rows
                ]

        @pl.when(t == 0)
        def _():
            sums[...] = jnp.zeros_like(sums)

        skeleton = jnp.dot(charges[...], basis[0], preferred_element_type=F32).astype(BF)
        sums[slots[t]] += jnp.dot(skeleton, transfer[0], preferred_element_type=F32)

        @pl.when(t == leaf_count - 1)
        def _():
            out[...] = sums[...].astype(BF)

    return pl.pallas_call(
        body,
        grid_spec=pltpu.PrefetchScalarGridSpec(
            num_scalar_prefetch=1,
            grid=(leaf_count,),
            in_specs=[
                pl.BlockSpec((columns, leaf_size), lambda t, s: (0, t)),
                pl.BlockSpec((1, leaf_size, rank), lambda t, s: (t, 0, 0)),
                pl.BlockSpec((1, rank, rank), lambda t, s: (t, 0, 0)),
            ],
            out_specs=[
                pl.BlockSpec((members, columns, rank), lambda t, s: (0, 0, 0)),
                pl.BlockSpec((QUARTERS, TILE_ROWS, width), lambda t, s: (t, 0, 0)),
            ],
            scratch_shapes=[pltpu.VMEM((members, columns, rank), F32)],
        ),
        out_shape=[
            jax.ShapeDtypeStruct((members, columns, rank), BF),
            jax.ShapeDtypeStruct((leaf_count * QUARTERS, TILE_ROWS, width), BF),
        ],
        compiler_params=params(),
        name="lift",
    )(slots, charges, leaf_basis, transfer)


def finish(fields, slots, transfer, leaf_basis, total):
    leaf_count, leaf_size, rank = leaf_basis.shape
    columns = total.shape[0]

    def body(slots, field, transfer, basis, total, out):
        descended = lax.dot_general(
            field[0], transfer[0], NT, preferred_element_type=F32
        ).astype(BF)
        out[...] = total[...] + lax.dot_general(
            descended, basis[0], NT, preferred_element_type=F32
        )

    return pl.pallas_call(
        body,
        grid_spec=pltpu.PrefetchScalarGridSpec(
            num_scalar_prefetch=1,
            grid=(leaf_count,),
            in_specs=[
                pl.BlockSpec((1, columns, rank), lambda t, s: (s[t], 0, 0)),
                pl.BlockSpec((1, rank, rank), lambda t, s: (t, 0, 0)),
                pl.BlockSpec((1, leaf_size, rank), lambda t, s: (t, 0, 0)),
                pl.BlockSpec((columns, leaf_size), lambda t, s: (0, t)),
            ],
            out_specs=pl.BlockSpec((columns, leaf_size), lambda t, s: (0, t)),
        ),
        out_shape=jax.ShapeDtypeStruct(total.shape, F32),
        compiler_params=params(),
        name="finish",
    )(slots, fields, transfer, leaf_basis, total)


def gauss(source, source_norms, target, target_norms, scale):
    gram = lax.dot_general(source, target, NT, preferred_element_type=F32)
    return jnp.exp2((2.0 * scale) * gram - (source_norms + target_norms)).astype(BF)


def own_body(scale, leaf_size, first, second, ti, sj, ci, cj, *rest):
    before, (out, rows, col) = rest[:-3], rest[-3:]
    step = pl.program_id(0)
    width = ti.shape[1]
    i0 = pl.multiple_of(first[step] * leaf_size, leaf_size)
    j0 = pl.multiple_of(second[step] * leaf_size, leaf_size)
    ones = jnp.ones((8, width), BF)
    lanes = jnp.ones((width, TILE_LANES), BF)

    @pl.when(step == 0)
    def _():
        if before:
            out[...] = before[0][...]
            rows[...] = before[1][...]
        else:
            out[...] = jnp.zeros_like(out)
            rows[...] = jnp.zeros_like(rows)

    @pl.when(i0 == j0)
    def _():
        wide = sj[...].astype(F32)
        square = wide * wide
        high = square.astype(BF)
        low = (square - high.astype(F32)).astype(BF)
        row = lax.dot_general(ones, high, NT, preferred_element_type=F32) + lax.dot_general(
            ones, low, NT, preferred_element_type=F32
        )
        rows[:, pl.ds(i0, leaf_size)] = scale * row
        column = jnp.dot(high, lanes, preferred_element_type=F32) + jnp.dot(
            low, lanes, preferred_element_type=F32
        )
        col[pl.ds(i0, leaf_size), :] = scale * column

    gram = lax.dot_general(sj[...], ti[...], NT, preferred_element_type=F32)
    norms = col[pl.ds(j0, leaf_size), :][:, :1] + rows[0:1, pl.ds(i0, leaf_size)]
    kernel = jnp.exp2((2.0 * scale) * gram - norms).astype(BF)
    out[:, pl.ds(i0, leaf_size)] += jnp.dot(cj[...], kernel, preferred_element_type=F32)

    @pl.when(i0 != j0)
    def _():
        out[:, pl.ds(j0, leaf_size)] += lax.dot_general(
            ci[...], kernel, NT, preferred_element_type=F32
        )


def own(points, charges, columns_of, leaf_size, gamma, before=()):
    width = points.shape[1]
    columns = charges.shape[0]
    total = points.shape[0]
    pairs = [(i, j) for j in columns_of for i in range(j, -1, -1)]
    first = jnp.array([p[0] for p in pairs], jnp.int32)
    second = jnp.array([p[1] for p in pairs], jnp.int32)
    return pl.pallas_call(
        functools.partial(own_body, gamma * LOG2E, leaf_size),
        grid_spec=pltpu.PrefetchScalarGridSpec(
            num_scalar_prefetch=2,
            grid=(len(pairs),),
            in_specs=[
                pl.BlockSpec((leaf_size, width), lambda s, a, b: (a[s], 0)),
                pl.BlockSpec((leaf_size, width), lambda s, a, b: (b[s], 0)),
                pl.BlockSpec((columns, leaf_size), lambda s, a, b: (0, a[s])),
                pl.BlockSpec((columns, leaf_size), lambda s, a, b: (0, b[s])),
            ]
            + [pl.BlockSpec(b.shape, lambda s, a, b: (0, 0)) for b in before],
            out_specs=[
                pl.BlockSpec((columns, total), lambda s, a, b: (0, 0)),
                pl.BlockSpec((8, total), lambda s, a, b: (0, 0)),
            ],
            scratch_shapes=[pltpu.VMEM((total, TILE_LANES), F32)],
        ),
        out_shape=[
            jax.ShapeDtypeStruct((columns, total), F32),
            jax.ShapeDtypeStruct((8, total), F32),
        ],
        compiler_params=params(),
        cost_estimate=pl.CostEstimate(
            flops=2 * len(pairs) * leaf_size * leaf_size * (width + 2 * columns),
            bytes_accessed=total * width * 8,
            transcendentals=len(pairs) * leaf_size * leaf_size,
        ),
        name="own",
    )(first, second, points, points, charges, charges, *before)


def near_body(scale, groups, leaf_size, target, points, norms, before, *refs):
    buffers, out = refs[:-1], refs[-1]
    columns = before.shape[0]
    rows = buffers[0].shape[1] - TILE_ROWS
    out[...] = before[...]
    for units, source_steps in groups:
        leaf = target[source_steps]

        @pl.when(leaf >= 0)
        def _(units=units, leaf=leaf):
            source = jnp.concatenate([buffers[b][u, 0:rows, :] for b, u in units], axis=0)
            charges = jnp.concatenate(
                [
                    jnp.concatenate(
                        [
                            buffers[b][u, rows:, g * TILE_LANES : (g + 1) * TILE_LANES]
                            for g in range(columns // TILE_ROWS)
                        ],
                        axis=0,
                    )
                    for b, u in units
                ],
                axis=1,
            )
            wide = source.astype(F32)
            source_norms = scale * jnp.sum(wide * wide, axis=1, keepdims=True)
            start = pl.multiple_of(leaf * leaf_size, leaf_size)
            kernel = gauss(
                source,
                source_norms,
                points[pl.ds(start, leaf_size), :],
                norms[0:1, pl.ds(start, leaf_size)],
                scale,
            )
            out[:, pl.ds(start, leaf_size)] += jnp.dot(
                charges, kernel, preferred_element_type=F32
            )


def near(buffers, groups, target, points, norms, before, leaf_size, gamma):
    width = points.shape[1]
    columns = before.shape[0]
    rows = sum(len(units) for units, _ in groups) * TILE_LANES
    whole = pl.BlockSpec(memory_space=pltpu.VMEM)
    return pl.pallas_call(
        functools.partial(near_body, gamma * LOG2E, groups, leaf_size),
        in_specs=[pl.BlockSpec(memory_space=pltpu.SMEM)] + [whole] * (3 + len(buffers)),
        out_specs=whole,
        out_shape=jax.ShapeDtypeStruct(before.shape, F32),
        compiler_params=pltpu.CompilerParams(vmem_limit_bytes=VMEM),
        cost_estimate=pl.CostEstimate(
            flops=2 * rows * leaf_size * (width + columns),
            bytes_accessed=rows * width * 2 + points.size * 2,
            transcendentals=rows * leaf_size,
        ),
        name="near",
    )(target, points, norms, before, *buffers)


def after(value, *others):
    return lax.optimization_barrier((value, *others))[0]


def local(points, charges, near_list, leaf_basis, transfer, parent, coarse_far, coarse_coupling):
    leaf_count, leaf_size, rank = leaf_basis.shape
    width = points.shape[1]
    columns = charges.shape[0]
    near_count = near_list.shape[1]
    members = lax.axis_size("sub")
    groups = lax.axis_size("grp")
    gamma = 2.0 / width

    def exchange(block):
        return lax.all_to_all(block, "sub", split_axis=0, concat_axis=0, tiled=True)

    def spread(block):
        return jnp.broadcast_to(block[None], (members, *block.shape))

    here = lax.axis_index("sub")
    y, z = here // RING, here % RING

    entries = near_list.reshape(-1)
    wanted = (entries // leaf_count)[None, :] == jnp.arange(members)[:, None]
    wanted = wanted & (entries >= 0)[None, :]
    requests = jnp.sum(jnp.where(wanted, entries[None, :] % leaf_count + 1, 0), axis=1)
    asked = exchange(requests[:, None])[:, 0]

    partial_sums, tails = lift(charges, leaf_basis, transfer, parent, members, width)

    pieces, rows = leaf_count * QUARTERS, leaf_size // QUARTERS
    plans = [[], [], []]
    for axis, way in DIRECTIONS:
        h = axis * (QUARTERS // 2)
        plans[0].append(
            [(offset(axis, 2, 0), 2 * way, 2)]
            + [(offset(axis, 2, across), h + way, 1) for across in (1, 3, 2)]
        )
        plans[1].append([(offset(axis, one(way), across), h, 2) for across in (1, 3, 2)])
        plans[2].append([(offset(axis, one(way), 0), 0, QUARTERS)])
    blocks = collect(
        points.reshape(pieces, rows, width),
        tails,
        after(asked, partial_sums),
        jnp.stack([y, z]).astype(jnp.int32),
        plans[0] + plans[1] + plans[2],
    )
    count = len(DIRECTIONS)

    def send(wait, values):
        return [step(v, d) for v, d in zip(held(wait, values), DIRECTIONS)]

    def held(wait, values):
        first = [after(values[0], *wait[0], *wait[1:])]
        return first + [after(v, w, *wait[1:]) for v, w in zip(values[1:], wait[0][1:])]

    chips = groups // 2

    def along_x(k, block, *gate):
        pairs = [(i, (i + 2 * k) % groups) for i in range(groups)]
        return lax.ppermute(after(block, *gate), "grp", pairs)

    def own_part(first, last, gate, *before):
        return own(after(points, *gate), charges, range(first, last), leaf_size, gamma, before)

    cut_1, cut_2 = leaf_count // 2, leaf_count * 2 // 3
    got_1 = [step(v, d) for v, d in zip(blocks[:count], DIRECTIONS)]
    total, norms = own_part(0, cut_1, blocks[:count])
    summed = exchange(after(partial_sums, total))
    got_2 = send((got_1, total, summed), blocks[count : 2 * count])
    total, norms = own_part(cut_1, cut_2, got_1, total, norms)
    own_weight = jnp.sum(after(summed, total).astype(F32), axis=0).astype(BF)
    weights = exchange(spread(own_weight))
    got_3 = send((got_2, total, weights), got_1)
    x_1 = along_x(1, weights, *got_2)
    total, norms = own_part(cut_2, leaf_count, got_2, total, norms)
    x_2 = along_x(2, weights, total)
    got_4 = send((got_3, x_1, x_2, total), blocks[2 * count :])
    plan_5, plan_6 = [], []
    for axis, way in DIRECTIONS:
        first = 2 * (1 - axis)
        plan_5.append(
            [(first, 4 + way, 1), (first + 1, 4 + way, 1), (4 + first + way, 4, 1)]
        )
        plan_6.append(
            [(first, 2 * way, 2), (first + 1, 2 * way, 2)]
            + [(4 + first, 2 + way, 1), (4 + first + 1, 2 + way, 1)]
        )
    woven = weave([*got_2, *[after(block, total) for block in got_3]], plan_5 + plan_6)
    x_3 = along_x(3, weights, *woven)
    got_5 = send((got_4, x_3), woven[:count])
    mine = jnp.concatenate([weights, x_1, x_2, x_3], axis=0)
    other = lax.ppermute(after(mine, *got_4), "grp", [(i, i ^ 1) for i in range(groups)])
    far_ids = coarse_far[0]
    far_alive = (far_ids >= 0).astype(F32)
    ids = jnp.maximum(far_ids, 0)
    group = lax.axis_index("grp")
    from_group, node = ids // members, ids % members
    side = (from_group % 2) != (group % 2)
    at = (group // 2 - from_group // 2) % chips * members
    at = at + node
    gated = after(other, *got_5)
    sources = jnp.where(side[:, None, None], gated[at], mine[at])
    far_terms = lax.dot_general(
        sources, coarse_coupling[0], (((2,), (1,)), ((0,), (0,))), preferred_element_type=F32
    )
    field = jnp.sum(far_terms * far_alive[:, None, None], axis=0).astype(BF)
    got_6 = send((got_5, other), woven[count:])
    add = functools.partial(near, leaf_size=leaf_size, gamma=gamma)
    groups_4, groups_6, groups_7 = [], [], []
    for d, (axis, way) in enumerate(DIRECTIONS):
        groups_4.append(([(count + d, 0), (count + d, 1)], number(offset(axis, 2, 0))))
        for k in range(0, QUARTERS, 2):
            groups_4.append(([(d, k), (d, k + 1)], number(offset(axis, one(way), 0))))
        for k, along in enumerate((1, 3, 2)):
            pair = [(d, 2 * k), (d, 2 * k + 1)]
            groups_6.append((pair, number(offset(1 - axis, along, one(way)))))
            if way == 0:
                groups_7.append(([(d, k), (d + 1, k)], number(offset(1 - axis, along, 2))))
    flat = near_list.reshape(-1)
    owner = jnp.where(flat >= 0, flat // leaf_count, 0)
    back = (y - owner // RING) % RING * RING + (z - owner % RING) % RING
    leaves = jnp.arange(flat.shape[0]) // near_count + 1
    match = (back[None, :] == jnp.arange(members)[:, None]) & (flat >= 0)[None, :]
    target = jnp.sum(jnp.where(match, leaves[None, :], 0), axis=1) - 1
    total = add([*got_4, *got_3], groups_4, target, points, norms, after(total, *got_5))
    fields = exchange(spread(after(field, total)))
    got_7 = send((got_6, fields), got_5)
    total = add(got_6, groups_6, target, points, norms, total)
    total = finish(fields, parent, transfer, leaf_basis, total)
    return add(got_7, groups_7, target, points, norms, total)


def solution(mesh):
    placed = (
        P(("grp", "sub"), None),
        P(None, ("grp", "sub")),
        P(("grp", "sub"), None),
        P(("grp", "sub"), None, None),
        P(("grp", "sub"), None, None),
        P(("grp", "sub")),
        P(("grp", "sub"), None),
        P(("grp", "sub"), None, None, None),
    )
    return jax.shard_map(
        local, mesh=mesh, in_specs=placed, out_specs=P(None, ("grp", "sub")), check_vma=False
    )
```

```python
import functools

import jax
import jax.numpy as jnp
from jax import lax
from jax.experimental import pallas as pl
from jax.experimental.pallas import tpu as pltpu
from jax.sharding import PartitionSpec as P

BF = jnp.bfloat16
F32 = jnp.float32
LOG2E = 1.4426950408889634
TILE_ROWS = 16
TILE_LANES = 128
RING = 4
QUARTERS = 4
DIRECTIONS = [(axis, way) for axis in range(2) for way in range(2)]
NT = (((1,), (1,)), ((), ()))
VMEM = 24 * 1024 * 1024


def params(n=1):
    return pltpu.CompilerParams(dimension_semantics=("arbitrary",) * n, vmem_limit_bytes=VMEM)


def offset(axis, along, across):
    return (along, across) if axis == 0 else (across, along)


def number(steps):
    return steps[0] * RING + steps[1]


def one(way):
    return 1 if way == 0 else RING - 1


def step(block, direction):
    return turn(block, *offset(direction[0], one(direction[1]), 0))


def turn(block, y, z):
    pairs = [
        (d, (d // RING + y) % RING * RING + (d % RING + z) % RING) for d in range(RING * RING)
    ]
    return lax.ppermute(block, "sub", pairs)


def collect(points, tails, asked, place, plans):
    pieces, rows, width = points.shape
    extra = tails.shape[1]
    sizes = [sum(run[2] for run in plan) for plan in plans]
    runs = []
    for number, plan in enumerate(plans):
        at = 0
        for steps, quarter, length in plan:
            runs.append((number, at, steps, quarter, length))
            at += length

    def body(asked, place, points, tails, *rest):
        outs, sems = rest[:-1], rest[-1]

        def wanted(steps):
            y = (place[0] + steps[0]) % RING
            z = (place[1] + steps[1]) % RING
            return asked[y * RING + z]

        def copies(k):
            number, at, steps, quarter, length = runs[k]
            first = jnp.maximum(wanted(steps) - 1, 0) * QUARTERS + quarter
            return (
                pltpu.make_async_copy(
                    points.at[pl.ds(first, length)],
                    outs[number].at[pl.ds(at, length), pl.ds(0, rows)],
                    sems.at[k, 0],
                ),
                pltpu.make_async_copy(
                    tails.at[pl.ds(first, length)],
                    outs[number].at[pl.ds(at, length), pl.ds(rows, extra)],
                    sems.at[k, 1],
                ),
            )

        for k in range(len(runs)):

            @pl.when(wanted(runs[k][2]) > 0)
            def _(k=k):
                for copy in copies(k):
                    copy.start()

        for k in range(len(runs)):

            @pl.when(wanted(runs[k][2]) > 0)
            def _(k=k):
                for copy in copies(k):
                    copy.wait()

    scalar = pl.BlockSpec(memory_space=pltpu.SMEM)
    return pl.pallas_call(
        body,
        in_specs=[scalar, scalar] + [pl.BlockSpec(memory_space=pltpu.VMEM)] * 2,
        out_specs=[pl.BlockSpec(memory_space=pltpu.HBM)] * len(plans),
        out_shape=[jax.ShapeDtypeStruct((n, rows + extra, width), BF) for n in sizes],
        scratch_shapes=[pltpu.SemaphoreType.DMA((len(runs), 2))],
        compiler_params=pltpu.CompilerParams(vmem_limit_bytes=VMEM),
        cost_estimate=pl.CostEstimate(
            flops=0, bytes_accessed=sum(sizes) * rows * width * 4, transcendentals=0
        ),
        name="collect",
    )(asked, place, points, tails)


def weave(sources, plans):
    count = sum(len(plan) for plan in plans)
    shape = sources[0].shape[1:]
    sizes = [sum(run[2] for run in plan) for plan in plans]

    def body(*refs):
        ins, outs, sems = refs[: len(sources)], refs[len(sources) : -1], refs[-1]
        copies = []
        for plan, out in zip(plans, outs):
            at = 0
            for source, first, length in plan:
                copies.append(
                    pltpu.make_async_copy(
                        ins[source].at[pl.ds(first, length)],
                        out.at[pl.ds(at, length)],
                        sems.at[len(copies)],
                    )
                )
                at += length
        for copy in copies:
            copy.start()
        for copy in copies:
            copy.wait()

    return pl.pallas_call(
        body,
        in_specs=[pl.BlockSpec(memory_space=pltpu.VMEM)] * len(sources),
        out_specs=[pl.BlockSpec(memory_space=pltpu.HBM)] * len(plans),
        out_shape=[jax.ShapeDtypeStruct((size, *shape), BF) for size in sizes],
        scratch_shapes=[pltpu.SemaphoreType.DMA((count,))],
        compiler_params=pltpu.CompilerParams(vmem_limit_bytes=VMEM),
        cost_estimate=pl.CostEstimate(
            flops=0,
            bytes_accessed=4 * sum(sizes) * shape[0] * shape[1],
            transcendentals=0,
        ),
        name="weave",
    )(*sources)


def lift(charges, leaf_basis, transfer, slots, members, width):
    leaf_count, leaf_size, rank = leaf_basis.shape
    columns = charges.shape[0]
    lines, rows = columns // TILE_ROWS, leaf_size // QUARTERS

    def body(slots, charges, basis, transfer, out, tails, sums):
        t = pl.program_id(0)
        tails[...] = jnp.zeros_like(tails)
        for q in range(QUARTERS):
            for g in range(lines):
                tails[q, :, g * rows : (g + 1) * rows] = charges[
                    g * TILE_ROWS : (g + 1) * TILE_ROWS, q * rows : (q + 1) * rows
                ]

        @pl.when(t == 0)
        def _():
            sums[...] = jnp.zeros_like(sums)

        skeleton = jnp.dot(charges[...], basis[0], preferred_element_type=F32).astype(BF)
        sums[slots[t]] += jnp.dot(skeleton, transfer[0], preferred_element_type=F32)

        @pl.when(t == leaf_count - 1)
        def _():
            out[...] = sums[...].astype(BF)

    return pl.pallas_call(
        body,
        grid_spec=pltpu.PrefetchScalarGridSpec(
            num_scalar_prefetch=1,
            grid=(leaf_count,),
            in_specs=[
                pl.BlockSpec((columns, leaf_size), lambda t, s: (0, t)),
                pl.BlockSpec((1, leaf_size, rank), lambda t, s: (t, 0, 0)),
                pl.BlockSpec((1, rank, rank), lambda t, s: (t, 0, 0)),
            ],
            out_specs=[
                pl.BlockSpec((members, columns, rank), lambda t, s: (0, 0, 0)),
                pl.BlockSpec((QUARTERS, TILE_ROWS, width), lambda t, s: (t, 0, 0)),
            ],
            scratch_shapes=[pltpu.VMEM((members, columns, rank), F32)],
        ),
        out_shape=[
            jax.ShapeDtypeStruct((members, columns, rank), BF),
            jax.ShapeDtypeStruct((leaf_count * QUARTERS, TILE_ROWS, width), BF),
        ],
        compiler_params=params(),
        name="lift",
    )(slots, charges, leaf_basis, transfer)


def finish(fields, slots, transfer, leaf_basis, total):
    leaf_count, leaf_size, rank = leaf_basis.shape
    columns = total.shape[0]

    def body(slots, field, transfer, basis, total, out):
        descended = lax.dot_general(
            field[0], transfer[0], NT, preferred_element_type=F32
        ).astype(BF)
        out[...] = total[...] + lax.dot_general(
            descended, basis[0], NT, preferred_element_type=F32
        )

    return pl.pallas_call(
        body,
        grid_spec=pltpu.PrefetchScalarGridSpec(
            num_scalar_prefetch=1,
            grid=(leaf_count,),
            in_specs=[
                pl.BlockSpec((1, columns, rank), lambda t, s: (s[t], 0, 0)),
                pl.BlockSpec((1, rank, rank), lambda t, s: (t, 0, 0)),
                pl.BlockSpec((1, leaf_size, rank), lambda t, s: (t, 0, 0)),
                pl.BlockSpec((columns, leaf_size), lambda t, s: (0, t)),
            ],
            out_specs=pl.BlockSpec((columns, leaf_size), lambda t, s: (0, t)),
        ),
        out_shape=jax.ShapeDtypeStruct(total.shape, F32),
        compiler_params=params(),
        name="finish",
    )(slots, fields, transfer, leaf_basis, total)


def gauss(source, source_norms, target, target_norms, scale):
    gram = lax.dot_general(source, target, NT, preferred_element_type=F32)
    return jnp.exp2((2.0 * scale) * gram - (source_norms + target_norms)).astype(BF)


def own_body(scale, leaf_size, first, second, ti, sj, ci, cj, *rest):
    before, (out, rows, col) = rest[:-3], rest[-3:]
    step = pl.program_id(0)
    width = ti.shape[1]
    i0 = pl.multiple_of(first[step] * leaf_size, leaf_size)
    j0 = pl.multiple_of(second[step] * leaf_size, leaf_size)
    ones = jnp.ones((8, width), BF)
    lanes = jnp.ones((width, TILE_LANES), BF)

    @pl.when(step == 0)
    def _():
        if before:
            out[...] = before[0][...]
            rows[...] = before[1][...]
        else:
            out[...] = jnp.zeros_like(out)
            rows[...] = jnp.zeros_like(rows)

    @pl.when(i0 == j0)
    def _():
        wide = sj[...].astype(F32)
        square = wide * wide
        high = square.astype(BF)
        low = (square - high.astype(F32)).astype(BF)
        row = lax.dot_general(ones, high, NT, preferred_element_type=F32) + lax.dot_general(
            ones, low, NT, preferred_element_type=F32
        )
        rows[:, pl.ds(i0, leaf_size)] = scale * row
        column = jnp.dot(high, lanes, preferred_element_type=F32) + jnp.dot(
            low, lanes, preferred_element_type=F32
        )
        col[pl.ds(i0, leaf_size), :] = scale * column

    gram = lax.dot_general(sj[...], ti[...], NT, preferred_element_type=F32)
    norms = col[pl.ds(j0, leaf_size), :][:, :1] + rows[0:1, pl.ds(i0, leaf_size)]
    kernel = jnp.exp2((2.0 * scale) * gram - norms).astype(BF)
    out[:, pl.ds(i0, leaf_size)] += jnp.dot(cj[...], kernel, preferred_element_type=F32)

    @pl.when(i0 != j0)
    def _():
        out[:, pl.ds(j0, leaf_size)] += lax.dot_general(
            ci[...], kernel, NT, preferred_element_type=F32
        )


def own(points, charges, columns_of, leaf_size, gamma, before=()):
    width = points.shape[1]
    columns = charges.shape[0]
    total = points.shape[0]
    pairs = [(i, j) for j in columns_of for i in range(j, -1, -1)]
    first = jnp.array([p[0] for p in pairs], jnp.int32)
    second = jnp.array([p[1] for p in pairs], jnp.int32)
    return pl.pallas_call(
        functools.partial(own_body, gamma * LOG2E, leaf_size),
        grid_spec=pltpu.PrefetchScalarGridSpec(
            num_scalar_prefetch=2,
            grid=(len(pairs),),
            in_specs=[
                pl.BlockSpec((leaf_size, width), lambda s, a, b: (a[s], 0)),
                pl.BlockSpec((leaf_size, width), lambda s, a, b: (b[s], 0)),
                pl.BlockSpec((columns, leaf_size), lambda s, a, b: (0, a[s])),
                pl.BlockSpec((columns, leaf_size), lambda s, a, b: (0, b[s])),
            ]
            + [pl.BlockSpec(b.shape, lambda s, a, b: (0, 0)) for b in before],
            out_specs=[
                pl.BlockSpec((columns, total), lambda s, a, b: (0, 0)),
                pl.BlockSpec((8, total), lambda s, a, b: (0, 0)),
            ],
            scratch_shapes=[pltpu.VMEM((total, TILE_LANES), F32)],
        ),
        out_shape=[
            jax.ShapeDtypeStruct((columns, total), F32),
            jax.ShapeDtypeStruct((8, total), F32),
        ],
        compiler_params=params(),
        cost_estimate=pl.CostEstimate(
            flops=2 * len(pairs) * leaf_size * leaf_size * (width + 2 * columns),
            bytes_accessed=total * width * 8,
            transcendentals=len(pairs) * leaf_size * leaf_size,
        ),
        name="own",
    )(first, second, points, points, charges, charges, *before)


def near_body(scale, groups, leaf_size, target, points, norms, before, *refs):
    buffers, out = refs[:-1], refs[-1]
    columns = before.shape[0]
    rows = buffers[0].shape[1] - TILE_ROWS
    out[...] = before[...]
    for units, source_steps in groups:
        leaf = target[source_steps]

        @pl.when(leaf >= 0)
        def _(units=units, leaf=leaf):
            source = jnp.concatenate([buffers[b][u, 0:rows, :] for b, u in units], axis=0)
            charges = jnp.concatenate(
                [
                    jnp.concatenate(
                        [
                            buffers[b][u, rows:, g * TILE_LANES : (g + 1) * TILE_LANES]
                            for g in range(columns // TILE_ROWS)
                        ],
                        axis=0,
                    )
                    for b, u in units
                ],
                axis=1,
            )
            wide = source.astype(F32)
            source_norms = scale * jnp.sum(wide * wide, axis=1, keepdims=True)
            start = pl.multiple_of(leaf * leaf_size, leaf_size)
            kernel = gauss(
                source,
                source_norms,
                points[pl.ds(start, leaf_size), :],
                norms[0:1, pl.ds(start, leaf_size)],
                scale,
            )
            out[:, pl.ds(start, leaf_size)] += jnp.dot(
                charges, kernel, preferred_element_type=F32
            )


def near(buffers, groups, target, points, norms, before, leaf_size, gamma):
    width = points.shape[1]
    columns = before.shape[0]
    rows = sum(len(units) for units, _ in groups) * TILE_LANES
    whole = pl.BlockSpec(memory_space=pltpu.VMEM)
    return pl.pallas_call(
        functools.partial(near_body, gamma * LOG2E, groups, leaf_size),
        in_specs=[pl.BlockSpec(memory_space=pltpu.SMEM)] + [whole] * (3 + len(buffers)),
        out_specs=whole,
        out_shape=jax.ShapeDtypeStruct(before.shape, F32),
        compiler_params=pltpu.CompilerParams(vmem_limit_bytes=VMEM),
        cost_estimate=pl.CostEstimate(
            flops=2 * rows * leaf_size * (width + columns),
            bytes_accessed=rows * width * 2 + points.size * 2,
            transcendentals=rows * leaf_size,
        ),
        name="near",
    )(target, points, norms, before, *buffers)


def after(value, *others):
    return lax.optimization_barrier((value, *others))[0]


def local(points, charges, near_list, leaf_basis, transfer, parent, coarse_far, coarse_coupling):
    leaf_count, leaf_size, rank = leaf_basis.shape
    width = points.shape[1]
    columns = charges.shape[0]
    near_count = near_list.shape[1]
    members = lax.axis_size("sub")
    groups = lax.axis_size("grp")
    gamma = 2.0 / width

    def exchange(block):
        return lax.all_to_all(block, "sub", split_axis=0, concat_axis=0, tiled=True)

    def spread(block):
        return jnp.broadcast_to(block[None], (members, *block.shape))

    here = lax.axis_index("sub")
    y, z = here // RING, here % RING

    entries = near_list.reshape(-1)
    wanted = (entries // leaf_count)[None, :] == jnp.arange(members)[:, None]
    wanted = wanted & (entries >= 0)[None, :]
    requests = jnp.sum(jnp.where(wanted, entries[None, :] % leaf_count + 1, 0), axis=1)
    asked = exchange(requests[:, None])[:, 0]

    partial_sums, tails = lift(charges, leaf_basis, transfer, parent, members, width)

    pieces, rows = leaf_count * QUARTERS, leaf_size // QUARTERS
    plans = [[], [], []]
    for axis, way in DIRECTIONS:
        h = axis * (QUARTERS // 2)
        plans[0].append(
            [(offset(axis, 2, 0), 2 * way, 2)]
            + [(offset(axis, 2, across), h + way, 1) for across in (1, 3, 2)]
        )
        plans[1].append([(offset(axis, one(way), across), h, 2) for across in (1, 3, 2)])
        plans[2].append([(offset(axis, one(way), 0), 0, QUARTERS)])
    blocks = collect(
        points.reshape(pieces, rows, width),
        tails,
        after(asked, partial_sums),
        jnp.stack([y, z]).astype(jnp.int32),
        plans[0] + plans[1] + plans[2],
    )
    count = len(DIRECTIONS)

    def send(wait, values):
        return [step(v, d) for v, d in zip(held(wait, values), DIRECTIONS)]

    def held(wait, values):
        first = [after(values[0], *wait[0], *wait[1:])]
        return first + [after(v, w, *wait[1:]) for v, w in zip(values[1:], wait[0][1:])]

    chips = groups // 2

    def along_x(k, block, *gate):
        pairs = [(i, (i + 2 * k) % groups) for i in range(groups)]
        return lax.ppermute(after(block, *gate), "grp", pairs)

    def own_part(first, last, gate, *before):
        return own(after(points, *gate), charges, range(first, last), leaf_size, gamma, before)

    summed = exchange(after(partial_sums, asked))
    own_weight = jnp.sum(after(summed, *blocks).astype(F32), axis=0).astype(BF)
    weights = exchange(spread(own_weight))
    blocks = [after(block, weights) for block in blocks]
    cut = leaf_count * 2 // 3
    got_1 = [step(v, d) for v, d in zip(blocks[:count], DIRECTIONS)]
    x_1 = along_x(1, weights, *blocks[:count])
    total, norms = own_part(0, cut, blocks[:count])
    got_2 = send((got_1, total, x_1), blocks[count : 2 * count])
    x_2 = along_x(2, weights, *got_1)
    total, norms = own_part(cut, leaf_count, got_1, total, norms)
    x_3 = along_x(3, weights, total)
    got_3 = send((got_2, total, x_2, x_3), got_1)
    mine = jnp.concatenate([weights, x_1, x_2, x_3], axis=0)
    other = lax.ppermute(after(mine, *got_2), "grp", [(i, i ^ 1) for i in range(groups)])
    far_ids = coarse_far[0]
    far_alive = (far_ids >= 0).astype(F32)
    ids = jnp.maximum(far_ids, 0)
    group = lax.axis_index("grp")
    from_group, node = ids // members, ids % members
    side = (from_group % 2) != (group % 2)
    at = (group // 2 - from_group // 2) % chips * members
    at = at + node
    sources = jnp.where(side[:, None, None], other[at], mine[at])
    far_terms = lax.dot_general(
        sources, coarse_coupling[0], (((2,), (1,)), ((0,), (0,))), preferred_element_type=F32
    )
    field = jnp.sum(far_terms * far_alive[:, None, None], axis=0).astype(BF)
    got_4 = send((got_3, field), blocks[2 * count :])
    plan_5, plan_6 = [], []
    for axis, way in DIRECTIONS:
        first = 2 * (1 - axis)
        plan_5.append(
            [(first, 4 + way, 1), (first + 1, 4 + way, 1), (4 + first + way, 4, 1)]
        )
        plan_6.append(
            [(first, 2 * way, 2), (first + 1, 2 * way, 2)]
            + [(4 + first, 2 + way, 1), (4 + first + 1, 2 + way, 1)]
        )
    woven = weave([*got_2, *[after(block, field) for block in got_3]], plan_5 + plan_6)
    got_5 = send((got_4, *woven), woven[:count])
    fields = exchange(spread(after(field, *got_4)))
    got_6 = send((got_5, fields), woven[count:])
    add = functools.partial(near, leaf_size=leaf_size, gamma=gamma)
    groups_4, groups_6, groups_7 = [], [], []
    for d, (axis, way) in enumerate(DIRECTIONS):
        groups_4.append(([(count + d, 0), (count + d, 1)], number(offset(axis, 2, 0))))
        for k in range(0, QUARTERS, 2):
            groups_4.append(([(d, k), (d, k + 1)], number(offset(axis, one(way), 0))))
        for k, along in enumerate((1, 3, 2)):
            pair = [(d, 2 * k), (d, 2 * k + 1)]
            groups_6.append((pair, number(offset(1 - axis, along, one(way)))))
            if way == 0:
                groups_7.append(([(d, k), (d + 1, k)], number(offset(1 - axis, along, 2))))
    flat = near_list.reshape(-1)
    owner = jnp.where(flat >= 0, flat // leaf_count, 0)
    back = (y - owner // RING) % RING * RING + (z - owner % RING) % RING
    leaves = jnp.arange(flat.shape[0]) // near_count + 1
    match = (back[None, :] == jnp.arange(members)[:, None]) & (flat >= 0)[None, :]
    target = jnp.sum(jnp.where(match, leaves[None, :], 0), axis=1) - 1
    total = add([*got_4, *got_3], groups_4, target, points, norms, after(total, *got_5))
    got_7 = send((got_6, total), got_5)
    total = add(got_6, groups_6, target, points, norms, total)
    total = finish(fields, parent, transfer, leaf_basis, total)
    return add(got_7, groups_7, target, points, norms, total)


def solution(mesh):
    placed = (
        P(("grp", "sub"), None),
        P(None, ("grp", "sub")),
        P(("grp", "sub"), None),
        P(("grp", "sub"), None, None),
        P(("grp", "sub"), None, None),
        P(("grp", "sub")),
        P(("grp", "sub"), None),
        P(("grp", "sub"), None, None, None),
    )
    return jax.shard_map(
        local, mesh=mesh, in_specs=placed, out_specs=P(None, ("grp", "sub")), check_vma=False
    )
```

```python
import functools

import jax
import jax.numpy as jnp
from jax import lax
from jax.experimental import pallas as pl
from jax.experimental.pallas import tpu as pltpu
from jax.sharding import PartitionSpec as P

BF = jnp.bfloat16
F32 = jnp.float32
LOG2E = 1.4426950408889634
TILE_ROWS = 16
TILE_LANES = 128
RING = 4
QUARTERS = 4
DIRECTIONS = [(axis, way) for axis in range(2) for way in range(2)]
NT = (((1,), (1,)), ((), ()))
MIB = 1024 * 1024


def params(size):
    return pltpu.CompilerParams(vmem_limit_bytes=size * MIB)


def offset(axis, along, across):
    return (along, across) if axis == 0 else (across, along)


def number(steps):
    return steps[0] * RING + steps[1]


def one(way):
    return 1 if way == 0 else RING - 1


def step(block, direction):
    return turn(block, *offset(direction[0], one(direction[1]), 0))


def turn(block, y, z):
    pairs = [
        (d, (d // RING + y) % RING * RING + (d % RING + z) % RING) for d in range(RING * RING)
    ]
    return lax.ppermute(block, "sub", pairs)


def collect(points, tails, asked, place, plans):
    pieces, rows, width = points.shape
    extra = tails.shape[1]
    sizes = [sum(run[2] for run in plan) for plan in plans]
    runs = []
    for number, plan in enumerate(plans):
        at = 0
        for steps, quarter, length in plan:
            runs.append((number, at, steps, quarter, length))
            at += length

    def body(asked, place, points, tails, *rest):
        outs, sems = rest[:-1], rest[-1]

        def wanted(steps):
            y = (place[0] + steps[0]) % RING
            z = (place[1] + steps[1]) % RING
            return asked[y * RING + z]

        def copies(k):
            number, at, steps, quarter, length = runs[k]
            first = jnp.maximum(wanted(steps) - 1, 0) * QUARTERS + quarter
            return (
                pltpu.make_async_copy(
                    points.at[pl.ds(first, length)],
                    outs[number].at[pl.ds(at, length), pl.ds(0, rows)],
                    sems.at[k, 0],
                ),
                pltpu.make_async_copy(
                    tails.at[pl.ds(first, length)],
                    outs[number].at[pl.ds(at, length), pl.ds(rows, extra)],
                    sems.at[k, 1],
                ),
            )

        for k in range(len(runs)):

            @pl.when(wanted(runs[k][2]) > 0)
            def _(k=k):
                for copy in copies(k):
                    copy.start()

        for k in range(len(runs)):

            @pl.when(wanted(runs[k][2]) > 0)
            def _(k=k):
                for copy in copies(k):
                    copy.wait()

    scalar = pl.BlockSpec(memory_space=pltpu.SMEM)
    return pl.pallas_call(
        body,
        in_specs=[scalar, scalar] + [pl.BlockSpec(memory_space=pltpu.VMEM)] * 2,
        out_specs=[pl.BlockSpec(memory_space=pltpu.HBM)] * len(plans),
        out_shape=[jax.ShapeDtypeStruct((n, rows + extra, width), BF) for n in sizes],
        scratch_shapes=[pltpu.SemaphoreType.DMA((len(runs), 2))],
        compiler_params=params(10),
        cost_estimate=pl.CostEstimate(
            flops=0, bytes_accessed=sum(sizes) * rows * width * 4, transcendentals=0
        ),
        name="collect",
    )(asked, place, points, tails)


def weave(sources, plans):
    count = sum(len(plan) for plan in plans)
    shape = sources[0].shape[1:]
    sizes = [sum(run[2] for run in plan) for plan in plans]

    def body(*refs):
        ins, outs, sems = refs[: len(sources)], refs[len(sources) : -1], refs[-1]
        copies = []
        for plan, out in zip(plans, outs):
            at = 0
            for source, first, length in plan:
                copies.append(
                    pltpu.make_async_copy(
                        ins[source].at[pl.ds(first, length)],
                        out.at[pl.ds(at, length)],
                        sems.at[len(copies)],
                    )
                )
                at += length
        for copy in copies:
            copy.start()
        for copy in copies:
            copy.wait()

    return pl.pallas_call(
        body,
        in_specs=[pl.BlockSpec(memory_space=pltpu.VMEM)] * len(sources),
        out_specs=[pl.BlockSpec(memory_space=pltpu.HBM)] * len(plans),
        out_shape=[jax.ShapeDtypeStruct((size, *shape), BF) for size in sizes],
        scratch_shapes=[pltpu.SemaphoreType.DMA((count,))],
        compiler_params=params(14),
        cost_estimate=pl.CostEstimate(
            flops=0,
            bytes_accessed=4 * sum(sizes) * shape[0] * shape[1],
            transcendentals=0,
        ),
        name="weave",
    )(*sources)


def lift(charges, leaf_basis, transfer, slots, requests, width):
    leaf_count, leaf_size, rank = leaf_basis.shape
    columns = charges.shape[0]
    lines, rows = columns // TILE_ROWS, leaf_size // QUARTERS
    members = requests.shape[0]

    def body(slots, requests, charges, basis, transfer, out, tails, sums):
        t = pl.program_id(0)
        tails[...] = jnp.zeros_like(tails)
        for q in range(QUARTERS):
            for g in range(lines):
                tails[q, :, g * rows : (g + 1) * rows] = charges[
                    g * TILE_ROWS : (g + 1) * TILE_ROWS, q * rows : (q + 1) * rows
                ]

        @pl.when(t == 0)
        def _():
            sums[...] = jnp.zeros_like(sums)

        skeleton = jnp.dot(charges[...], basis[0], preferred_element_type=F32).astype(BF)
        sums[slots[t]] += jnp.dot(skeleton, transfer[0], preferred_element_type=F32)

        @pl.when(t == leaf_count - 1)
        def _():
            out[:, 0:columns, :] = sums[...].astype(BF)
            for d in range(members):
                value = requests[d].astype(F32)
                out[d, columns:, :] = jnp.full((TILE_ROWS, rank), value, F32).astype(BF)

    return pl.pallas_call(
        body,
        grid_spec=pltpu.PrefetchScalarGridSpec(
            num_scalar_prefetch=2,
            grid=(leaf_count,),
            in_specs=[
                pl.BlockSpec((columns, leaf_size), lambda t, s, r: (0, t)),
                pl.BlockSpec((1, leaf_size, rank), lambda t, s, r: (t, 0, 0)),
                pl.BlockSpec((1, rank, rank), lambda t, s, r: (t, 0, 0)),
            ],
            out_specs=[
                pl.BlockSpec((members, columns + TILE_ROWS, rank), lambda t, s, r: (0, 0, 0)),
                pl.BlockSpec((QUARTERS, TILE_ROWS, width), lambda t, s, r: (t, 0, 0)),
            ],
            scratch_shapes=[pltpu.VMEM((members, columns, rank), F32)],
        ),
        out_shape=[
            jax.ShapeDtypeStruct((members, columns + TILE_ROWS, rank), BF),
            jax.ShapeDtypeStruct((leaf_count * QUARTERS, TILE_ROWS, width), BF),
        ],
        compiler_params=params(10),
        name="lift",
    )(slots, requests, charges, leaf_basis, transfer)


def finish(fields, slots, transfer, leaf_basis, total):
    leaf_count, leaf_size, rank = leaf_basis.shape
    columns = total.shape[0]

    def body(slots, field, transfer, basis, total, out):
        descended = lax.dot_general(
            field[0], transfer[0], NT, preferred_element_type=F32
        ).astype(BF)
        out[...] = total[...] + lax.dot_general(
            descended, basis[0], NT, preferred_element_type=F32
        )

    return pl.pallas_call(
        body,
        grid_spec=pltpu.PrefetchScalarGridSpec(
            num_scalar_prefetch=1,
            grid=(leaf_count,),
            in_specs=[
                pl.BlockSpec((1, columns, rank), lambda t, s: (s[t], 0, 0)),
                pl.BlockSpec((1, rank, rank), lambda t, s: (t, 0, 0)),
                pl.BlockSpec((1, leaf_size, rank), lambda t, s: (t, 0, 0)),
                pl.BlockSpec((columns, leaf_size), lambda t, s: (0, t)),
            ],
            out_specs=pl.BlockSpec((columns, leaf_size), lambda t, s: (0, t)),
        ),
        out_shape=jax.ShapeDtypeStruct(total.shape, F32),
        compiler_params=params(8),
        name="finish",
    )(slots, fields, transfer, leaf_basis, total)


def gauss(source, source_norms, target, target_norms, scale):
    gram = lax.dot_general(source, target, NT, preferred_element_type=F32)
    return jnp.exp2((2.0 * scale) * gram - (source_norms + target_norms)).astype(BF)


def own_body(scale, leaf_size, first, second, ti, sj, ci, cj, *rest):
    before, (out, rows, col) = rest[:-3], rest[-3:]
    step = pl.program_id(0)
    width = ti.shape[1]
    i0 = pl.multiple_of(first[step] * leaf_size, leaf_size)
    j0 = pl.multiple_of(second[step] * leaf_size, leaf_size)
    ones = jnp.ones((8, width), BF)
    lanes = jnp.ones((width, TILE_LANES), BF)

    @pl.when(step == 0)
    def _():
        if before:
            out[...] = before[0][...]
            rows[...] = before[1][...]
        else:
            out[...] = jnp.zeros_like(out)
            rows[...] = jnp.zeros_like(rows)

    @pl.when(i0 == j0)
    def _():
        wide = sj[...].astype(F32)
        square = wide * wide
        high = square.astype(BF)
        low = (square - high.astype(F32)).astype(BF)
        row = lax.dot_general(ones, high, NT, preferred_element_type=F32) + lax.dot_general(
            ones, low, NT, preferred_element_type=F32
        )
        rows[:, pl.ds(i0, leaf_size)] = scale * row
        column = jnp.dot(high, lanes, preferred_element_type=F32) + jnp.dot(
            low, lanes, preferred_element_type=F32
        )
        col[pl.ds(i0, leaf_size), :] = scale * column

    gram = lax.dot_general(sj[...], ti[...], NT, preferred_element_type=F32)
    norms = col[pl.ds(j0, leaf_size), :][:, :1] + rows[0:1, pl.ds(i0, leaf_size)]
    kernel = jnp.exp2((2.0 * scale) * gram - norms).astype(BF)
    out[:, pl.ds(i0, leaf_size)] += jnp.dot(cj[...], kernel, preferred_element_type=F32)

    @pl.when(i0 != j0)
    def _():
        out[:, pl.ds(j0, leaf_size)] += lax.dot_general(
            ci[...], kernel, NT, preferred_element_type=F32
        )


def own(points, charges, columns_of, leaf_size, gamma, before=()):
    width = points.shape[1]
    columns = charges.shape[0]
    total = points.shape[0]
    pairs = [(i, j) for j in columns_of for i in range(j, -1, -1)]
    first = jnp.array([p[0] for p in pairs], jnp.int32)
    second = jnp.array([p[1] for p in pairs], jnp.int32)
    return pl.pallas_call(
        functools.partial(own_body, gamma * LOG2E, leaf_size),
        grid_spec=pltpu.PrefetchScalarGridSpec(
            num_scalar_prefetch=2,
            grid=(len(pairs),),
            in_specs=[
                pl.BlockSpec((leaf_size, width), lambda s, a, b: (a[s], 0)),
                pl.BlockSpec((leaf_size, width), lambda s, a, b: (b[s], 0)),
                pl.BlockSpec((columns, leaf_size), lambda s, a, b: (0, a[s])),
                pl.BlockSpec((columns, leaf_size), lambda s, a, b: (0, b[s])),
            ]
            + [pl.BlockSpec(b.shape, lambda s, a, b: (0, 0)) for b in before],
            out_specs=[
                pl.BlockSpec((columns, total), lambda s, a, b: (0, 0)),
                pl.BlockSpec((8, total), lambda s, a, b: (0, 0)),
            ],
            scratch_shapes=[pltpu.VMEM((total, TILE_LANES), F32)],
        ),
        out_shape=[
            jax.ShapeDtypeStruct((columns, total), F32),
            jax.ShapeDtypeStruct((8, total), F32),
        ],
        compiler_params=params(14),
        cost_estimate=pl.CostEstimate(
            flops=2 * len(pairs) * leaf_size * leaf_size * (width + 2 * columns),
            bytes_accessed=total * width * 8,
            transcendentals=len(pairs) * leaf_size * leaf_size,
        ),
        name="own",
    )(first, second, points, points, charges, charges, *before)


def near_body(scale, groups, leaf_size, target, points, norms, before, *refs):
    buffers, out = refs[:-1], refs[-1]
    columns = before.shape[0]
    rows = buffers[0].shape[1] - TILE_ROWS
    out[...] = before[...]
    for units, source_steps in groups:
        leaf = target[source_steps]

        @pl.when(leaf >= 0)
        def _(units=units, leaf=leaf):
            source = jnp.concatenate([buffers[b][u, 0:rows, :] for b, u in units], axis=0)
            charges = jnp.concatenate(
                [
                    jnp.concatenate(
                        [
                            buffers[b][u, rows:, g * TILE_LANES : (g + 1) * TILE_LANES]
                            for g in range(columns // TILE_ROWS)
                        ],
                        axis=0,
                    )
                    for b, u in units
                ],
                axis=1,
            )
            wide = source.astype(F32)
            source_norms = scale * jnp.sum(wide * wide, axis=1, keepdims=True)
            start = pl.multiple_of(leaf * leaf_size, leaf_size)
            kernel = gauss(
                source,
                source_norms,
                points[pl.ds(start, leaf_size), :],
                norms[0:1, pl.ds(start, leaf_size)],
                scale,
            )
            out[:, pl.ds(start, leaf_size)] += jnp.dot(
                charges, kernel, preferred_element_type=F32
            )


def near(buffers, groups, target, points, norms, before, leaf_size, gamma):
    width = points.shape[1]
    columns = before.shape[0]
    rows = sum(len(units) for units, _ in groups) * TILE_LANES
    whole = pl.BlockSpec(memory_space=pltpu.VMEM)
    return pl.pallas_call(
        functools.partial(near_body, gamma * LOG2E, groups, leaf_size),
        in_specs=[pl.BlockSpec(memory_space=pltpu.SMEM)] + [whole] * (3 + len(buffers)),
        out_specs=whole,
        out_shape=jax.ShapeDtypeStruct(before.shape, F32),
        compiler_params=params(20),
        cost_estimate=pl.CostEstimate(
            flops=2 * rows * leaf_size * (width + columns),
            bytes_accessed=rows * width * 2 + points.size * 2,
            transcendentals=rows * leaf_size,
        ),
        name="near",
    )(target, points, norms, before, *buffers)


def after(value, *others):
    return lax.optimization_barrier((value, *others))[0]


def local(points, charges, near_list, leaf_basis, transfer, parent, coarse_far, coarse_coupling):
    leaf_count, leaf_size, rank = leaf_basis.shape
    width = points.shape[1]
    columns = charges.shape[0]
    near_count = near_list.shape[1]
    members = lax.axis_size("sub")
    groups = lax.axis_size("grp")
    gamma = 2.0 / width

    def exchange(block):
        return lax.all_to_all(block, "sub", split_axis=0, concat_axis=0, tiled=True)

    def spread(block):
        return jnp.broadcast_to(block[None], (members, *block.shape))

    here = lax.axis_index("sub")
    y, z = here // RING, here % RING

    entries = near_list.reshape(-1)
    wanted = (entries // leaf_count)[None, :] == jnp.arange(members)[:, None]
    wanted = wanted & (entries >= 0)[None, :]
    requests = jnp.sum(jnp.where(wanted, entries[None, :] % leaf_count + 1, 0), axis=1)

    terms, tails = lift(charges, leaf_basis, transfer, parent, requests, width)
    terms = exchange(terms)
    asked = terms[:, columns, 0].astype(F32).astype(jnp.int32)

    pieces, rows = leaf_count * QUARTERS, leaf_size // QUARTERS
    plans = [[], [], []]
    for axis, way in DIRECTIONS:
        h = axis * (QUARTERS // 2)
        plans[0].append(
            [(offset(axis, 2, 0), 2 * way, 2)]
            + [(offset(axis, 2, across), h + way, 1) for across in (1, 3, 2)]
        )
        plans[1].append([(offset(axis, one(way), across), h, 2) for across in (1, 3, 2)])
        plans[2].append([(offset(axis, one(way), 0), 0, QUARTERS)])
    blocks = collect(
        points.reshape(pieces, rows, width),
        tails,
        asked,
        jnp.stack([y, z]).astype(jnp.int32),
        plans[0] + plans[1] + plans[2],
    )
    count = len(DIRECTIONS)

    def send(wait, values):
        return [step(v, d) for v, d in zip(held(wait, values), DIRECTIONS)]

    def held(wait, values):
        first = [after(values[0], *wait[0], *wait[1:])]
        return first + [after(v, w, *wait[1:]) for v, w in zip(values[1:], wait[0][1:])]

    chips = groups // 2

    def along_x(k, block, *gate):
        pairs = [(i, (i + 2 * k) % groups) for i in range(groups)]
        return lax.ppermute(after(block, *gate), "grp", pairs)

    def own_part(first, last, gate, *before):
        return own(after(points, *gate), charges, range(first, last), leaf_size, gamma, before)

    own_weight = jnp.sum(terms[:, :columns].astype(F32), axis=0).astype(BF)
    weights = exchange(spread(own_weight))
    blocks = [after(block, weights) for block in blocks]
    cut = leaf_count * 2 // 3
    got_1 = [step(v, d) for v, d in zip(blocks[:count], DIRECTIONS)]
    x_1 = along_x(1, weights, *blocks[:count])
    total, norms = own_part(0, cut, blocks[:count])
    got_2 = send((got_1, total, x_1), blocks[count : 2 * count])
    x_2 = along_x(2, weights, *got_1)
    total, norms = own_part(cut, leaf_count, got_1, total, norms)
    x_3 = along_x(3, weights, total)
    got_3 = send((got_2, total, x_2, x_3), got_1)
    mine = jnp.concatenate([weights, x_1, x_2, x_3], axis=0)
    other = lax.ppermute(after(mine, *got_2), "grp", [(i, i ^ 1) for i in range(groups)])
    far_ids = coarse_far[0]
    far_alive = (far_ids >= 0).astype(F32)
    ids = jnp.maximum(far_ids, 0)
    group = lax.axis_index("grp")
    from_group, node = ids // members, ids % members
    side = (from_group % 2) != (group % 2)
    at = (group // 2 - from_group // 2) % chips * members
    at = at + node
    sources = jnp.where(side[:, None, None], other[at], mine[at])
    far_terms = lax.dot_general(
        sources, coarse_coupling[0], (((2,), (1,)), ((0,), (0,))), preferred_element_type=F32
    )
    field = jnp.sum(far_terms * far_alive[:, None, None], axis=0).astype(BF)
    got_4 = send((got_3, field), blocks[2 * count :])
    plan_5, plan_6 = [], []
    for axis, way in DIRECTIONS:
        first = 2 * (1 - axis)
        plan_5.append(
            [(first, 4 + way, 1), (first + 1, 4 + way, 1), (4 + first + way, 4, 1)]
        )
        plan_6.append(
            [(first, 2 * way, 2), (first + 1, 2 * way, 2)]
            + [(4 + first, 2 + way, 1), (4 + first + 1, 2 + way, 1)]
        )
    woven = weave([*got_2, *[after(block, field) for block in got_3]], plan_5 + plan_6)
    got_5 = send((got_4, *woven), woven[:count])
    fields = exchange(spread(after(field, *got_4)))
    got_6 = send((got_5, fields), woven[count:])
    add = functools.partial(near, leaf_size=leaf_size, gamma=gamma)
    groups_4, groups_6, groups_7 = [], [], []
    for d, (axis, way) in enumerate(DIRECTIONS):
        groups_4.append(([(count + d, 0), (count + d, 1)], number(offset(axis, 2, 0))))
        for k in range(0, QUARTERS, 2):
            groups_4.append(([(d, k), (d, k + 1)], number(offset(axis, one(way), 0))))
        for k, along in enumerate((1, 3, 2)):
            pair = [(d, 2 * k), (d, 2 * k + 1)]
            groups_6.append((pair, number(offset(1 - axis, along, one(way)))))
            if way == 0:
                groups_7.append(([(d, k), (d + 1, k)], number(offset(1 - axis, along, 2))))
    flat = near_list.reshape(-1)
    owner = jnp.where(flat >= 0, flat // leaf_count, 0)
    back = (y - owner // RING) % RING * RING + (z - owner % RING) % RING
    leaves = jnp.arange(flat.shape[0]) // near_count + 1
    match = (back[None, :] == jnp.arange(members)[:, None]) & (flat >= 0)[None, :]
    target = jnp.sum(jnp.where(match, leaves[None, :], 0), axis=1) - 1
    total = add([*got_4, *got_3], groups_4, target, points, norms, after(total, *got_5))
    got_7 = send((got_6, total), got_5)
    total = add(got_6, groups_6, target, points, norms, total)
    total = finish(fields, parent, transfer, leaf_basis, total)
    return add(got_7, groups_7, target, points, norms, total)


def solution(mesh):
    placed = (
        P(("grp", "sub"), None),
        P(None, ("grp", "sub")),
        P(("grp", "sub"), None),
        P(("grp", "sub"), None, None),
        P(("grp", "sub"), None, None),
        P(("grp", "sub")),
        P(("grp", "sub"), None),
        P(("grp", "sub"), None, None, None),
    )
    return jax.shard_map(
        local, mesh=mesh, in_specs=placed, out_specs=P(None, ("grp", "sub")), check_vma=False
    )
```

```python
import functools

import jax
import jax.numpy as jnp
from jax import lax
from jax.experimental import pallas as pl
from jax.experimental.pallas import tpu as pltpu
from jax.sharding import PartitionSpec as P

BF = jnp.bfloat16
F32 = jnp.float32
LOG2E = 1.4426950408889634
TILE_ROWS = 16
TILE_LANES = 128
RING = 4
QUARTERS = 4
DIRECTIONS = [(axis, way) for axis in range(2) for way in range(2)]
NT = (((1,), (1,)), ((), ()))
MIB = 1024 * 1024


def params(size):
    return pltpu.CompilerParams(vmem_limit_bytes=size * MIB)


def offset(axis, along, across):
    return (along, across) if axis == 0 else (across, along)


def number(steps):
    return steps[0] * RING + steps[1]


def one(way):
    return 1 if way == 0 else RING - 1


def step(block, direction):
    return turn(block, *offset(direction[0], one(direction[1]), 0))


def turn(block, y, z):
    pairs = [
        (d, (d // RING + y) % RING * RING + (d % RING + z) % RING) for d in range(RING * RING)
    ]
    return lax.ppermute(block, "sub", pairs)


def collect(points, tails, asked, place, plans):
    pieces, rows, width = points.shape
    extra = tails.shape[1]
    sizes = [sum(run[2] for run in plan) for plan in plans]
    runs = []
    for number, plan in enumerate(plans):
        at = 0
        for steps, quarter, length in plan:
            runs.append((number, at, steps, quarter, length))
            at += length

    def body(asked, place, points, tails, *rest):
        outs, sems = rest[:-1], rest[-1]

        def wanted(steps):
            y = (place[0] + steps[0]) % RING
            z = (place[1] + steps[1]) % RING
            return asked[y * RING + z]

        def copies(k):
            number, at, steps, quarter, length = runs[k]
            first = jnp.maximum(wanted(steps) - 1, 0) * QUARTERS + quarter
            return (
                pltpu.make_async_copy(
                    points.at[pl.ds(first, length)],
                    outs[number].at[pl.ds(at, length), pl.ds(0, rows)],
                    sems.at[k, 0],
                ),
                pltpu.make_async_copy(
                    tails.at[pl.ds(first, length)],
                    outs[number].at[pl.ds(at, length), pl.ds(rows, extra)],
                    sems.at[k, 1],
                ),
            )

        for k in range(len(runs)):

            @pl.when(wanted(runs[k][2]) > 0)
            def _(k=k):
                for copy in copies(k):
                    copy.start()

        for k in range(len(runs)):

            @pl.when(wanted(runs[k][2]) > 0)
            def _(k=k):
                for copy in copies(k):
                    copy.wait()

    scalar = pl.BlockSpec(memory_space=pltpu.SMEM)
    return pl.pallas_call(
        body,
        in_specs=[scalar, scalar] + [pl.BlockSpec(memory_space=pltpu.VMEM)] * 2,
        out_specs=[pl.BlockSpec(memory_space=pltpu.HBM)] * len(plans),
        out_shape=[jax.ShapeDtypeStruct((n, rows + extra, width), BF) for n in sizes],
        scratch_shapes=[pltpu.SemaphoreType.DMA((len(runs), 2))],
        compiler_params=params(56),
        cost_estimate=pl.CostEstimate(
            flops=0, bytes_accessed=sum(sizes) * rows * width * 4, transcendentals=0
        ),
        name="collect",
    )(asked, place, points, tails)


def weave(sources, plans):
    count = sum(len(plan) for plan in plans)
    shape = sources[0].shape[1:]
    sizes = [sum(run[2] for run in plan) for plan in plans]

    def body(*refs):
        ins, outs, sems = refs[: len(sources)], refs[len(sources) : -1], refs[-1]
        copies = []
        for plan, out in zip(plans, outs):
            at = 0
            for source, first, length in plan:
                copies.append(
                    pltpu.make_async_copy(
                        ins[source].at[pl.ds(first, length)],
                        out.at[pl.ds(at, length)],
                        sems.at[len(copies)],
                    )
                )
                at += length
        for copy in copies:
            copy.start()
        for copy in copies:
            copy.wait()

    return pl.pallas_call(
        body,
        in_specs=[pl.BlockSpec(memory_space=pltpu.VMEM)] * len(sources),
        out_specs=[pl.BlockSpec(memory_space=pltpu.HBM)] * len(plans),
        out_shape=[jax.ShapeDtypeStruct((size, *shape), BF) for size in sizes],
        scratch_shapes=[pltpu.SemaphoreType.DMA((count,))],
        compiler_params=params(14),
        cost_estimate=pl.CostEstimate(
            flops=0,
            bytes_accessed=4 * sum(sizes) * shape[0] * shape[1],
            transcendentals=0,
        ),
        name="weave",
    )(*sources)


def lift(charges, leaf_basis, transfer, slots, requests, width):
    leaf_count, leaf_size, rank = leaf_basis.shape
    columns = charges.shape[0]
    lines, rows = columns // TILE_ROWS, leaf_size // QUARTERS
    members = requests.shape[0]

    def body(slots, requests, charges, basis, transfer, out, tails, sums):
        t = pl.program_id(0)
        tails[...] = jnp.zeros_like(tails)
        for q in range(QUARTERS):
            for g in range(lines):
                tails[q, :, g * rows : (g + 1) * rows] = charges[
                    g * TILE_ROWS : (g + 1) * TILE_ROWS, q * rows : (q + 1) * rows
                ]

        @pl.when(t == 0)
        def _():
            sums[...] = jnp.zeros_like(sums)

        skeleton = jnp.dot(charges[...], basis[0], preferred_element_type=F32).astype(BF)
        sums[slots[t]] += jnp.dot(skeleton, transfer[0], preferred_element_type=F32)

        @pl.when(t == leaf_count - 1)
        def _():
            out[:, 0:columns, :] = sums[...].astype(BF)
            for d in range(members):
                value = requests[d].astype(F32)
                out[d, columns:, :] = jnp.full((TILE_ROWS, rank), value, F32).astype(BF)

    return pl.pallas_call(
        body,
        grid_spec=pltpu.PrefetchScalarGridSpec(
            num_scalar_prefetch=2,
            grid=(leaf_count,),
            in_specs=[
                pl.BlockSpec((columns, leaf_size), lambda t, s, r: (0, t)),
                pl.BlockSpec((1, leaf_size, rank), lambda t, s, r: (t, 0, 0)),
                pl.BlockSpec((1, rank, rank), lambda t, s, r: (t, 0, 0)),
            ],
            out_specs=[
                pl.BlockSpec((members, columns + TILE_ROWS, rank), lambda t, s, r: (0, 0, 0)),
                pl.BlockSpec((QUARTERS, TILE_ROWS, width), lambda t, s, r: (t, 0, 0)),
            ],
            scratch_shapes=[pltpu.VMEM((members, columns, rank), F32)],
        ),
        out_shape=[
            jax.ShapeDtypeStruct((members, columns + TILE_ROWS, rank), BF),
            jax.ShapeDtypeStruct((leaf_count * QUARTERS, TILE_ROWS, width), BF),
        ],
        compiler_params=params(10),
        name="lift",
    )(slots, requests, charges, leaf_basis, transfer)


def finish(fields, slots, transfer, leaf_basis, total):
    leaf_count, leaf_size, rank = leaf_basis.shape
    columns = total.shape[0]

    def body(slots, field, transfer, basis, total, out):
        descended = lax.dot_general(
            field[0], transfer[0], NT, preferred_element_type=F32
        ).astype(BF)
        out[...] = total[...] + lax.dot_general(
            descended, basis[0], NT, preferred_element_type=F32
        )

    return pl.pallas_call(
        body,
        grid_spec=pltpu.PrefetchScalarGridSpec(
            num_scalar_prefetch=1,
            grid=(leaf_count,),
            in_specs=[
                pl.BlockSpec((1, columns, rank), lambda t, s: (s[t], 0, 0)),
                pl.BlockSpec((1, rank, rank), lambda t, s: (t, 0, 0)),
                pl.BlockSpec((1, leaf_size, rank), lambda t, s: (t, 0, 0)),
                pl.BlockSpec((columns, leaf_size), lambda t, s: (0, t)),
            ],
            out_specs=pl.BlockSpec((columns, leaf_size), lambda t, s: (0, t)),
        ),
        out_shape=jax.ShapeDtypeStruct(total.shape, F32),
        compiler_params=params(8),
        name="finish",
    )(slots, fields, transfer, leaf_basis, total)


def gauss(source, source_norms, target, target_norms, scale):
    gram = lax.dot_general(source, target, NT, preferred_element_type=F32)
    return jnp.exp2((2.0 * scale) * gram - (source_norms + target_norms)).astype(BF)


def own_body(scale, leaf_size, first, second, ti, sj, ci, cj, *rest):
    before, (out, rows, col) = rest[:-3], rest[-3:]
    step = pl.program_id(0)
    width = ti.shape[1]
    i0 = pl.multiple_of(first[step] * leaf_size, leaf_size)
    j0 = pl.multiple_of(second[step] * leaf_size, leaf_size)
    ones = jnp.ones((8, width), BF)
    lanes = jnp.ones((width, TILE_LANES), BF)

    @pl.when(step == 0)
    def _():
        if before:
            out[...] = before[0][...]
            rows[...] = before[1][...]
        else:
            out[...] = jnp.zeros_like(out)
            rows[...] = jnp.zeros_like(rows)

    @pl.when(i0 == j0)
    def _():
        wide = sj[...].astype(F32)
        square = wide * wide
        high = square.astype(BF)
        low = (square - high.astype(F32)).astype(BF)
        row = lax.dot_general(ones, high, NT, preferred_element_type=F32) + lax.dot_general(
            ones, low, NT, preferred_element_type=F32
        )
        rows[:, pl.ds(i0, leaf_size)] = scale * row
        column = jnp.dot(high, lanes, preferred_element_type=F32) + jnp.dot(
            low, lanes, preferred_element_type=F32
        )
        col[pl.ds(i0, leaf_size), :] = scale * column

    gram = lax.dot_general(sj[...], ti[...], NT, preferred_element_type=F32)
    norms = col[pl.ds(j0, leaf_size), :][:, :1] + rows[0:1, pl.ds(i0, leaf_size)]
    kernel = jnp.exp2((2.0 * scale) * gram - norms).astype(BF)
    out[:, pl.ds(i0, leaf_size)] += jnp.dot(cj[...], kernel, preferred_element_type=F32)

    @pl.when(i0 != j0)
    def _():
        out[:, pl.ds(j0, leaf_size)] += lax.dot_general(
            ci[...], kernel, NT, preferred_element_type=F32
        )


def own(points, charges, columns_of, leaf_size, gamma, before=()):
    width = points.shape[1]
    columns = charges.shape[0]
    total = points.shape[0]
    pairs = [(i, j) for j in columns_of for i in range(j, -1, -1)]
    first = jnp.array([p[0] for p in pairs], jnp.int32)
    second = jnp.array([p[1] for p in pairs], jnp.int32)
    return pl.pallas_call(
        functools.partial(own_body, gamma * LOG2E, leaf_size),
        grid_spec=pltpu.PrefetchScalarGridSpec(
            num_scalar_prefetch=2,
            grid=(len(pairs),),
            in_specs=[
                pl.BlockSpec((leaf_size, width), lambda s, a, b: (a[s], 0)),
                pl.BlockSpec((leaf_size, width), lambda s, a, b: (b[s], 0)),
                pl.BlockSpec((columns, leaf_size), lambda s, a, b: (0, a[s])),
                pl.BlockSpec((columns, leaf_size), lambda s, a, b: (0, b[s])),
            ]
            + [pl.BlockSpec(b.shape, lambda s, a, b: (0, 0)) for b in before],
            out_specs=[
                pl.BlockSpec((columns, total), lambda s, a, b: (0, 0)),
                pl.BlockSpec((8, total), lambda s, a, b: (0, 0)),
            ],
            scratch_shapes=[pltpu.VMEM((total, TILE_LANES), F32)],
        ),
        out_shape=[
            jax.ShapeDtypeStruct((columns, total), F32),
            jax.ShapeDtypeStruct((8, total), F32),
        ],
        compiler_params=params(14),
        cost_estimate=pl.CostEstimate(
            flops=2 * len(pairs) * leaf_size * leaf_size * (width + 2 * columns),
            bytes_accessed=total * width * 8,
            transcendentals=len(pairs) * leaf_size * leaf_size,
        ),
        name="own",
    )(first, second, points, points, charges, charges, *before)


def near_body(scale, groups, leaf_size, target, points, norms, before, *refs):
    buffers, out = refs[:-1], refs[-1]
    columns = before.shape[0]
    rows = buffers[0].shape[1] - TILE_ROWS
    out[...] = before[...]
    for units, source_steps in groups:
        leaf = target[source_steps]

        @pl.when(leaf >= 0)
        def _(units=units, leaf=leaf):
            source = jnp.concatenate([buffers[b][u, 0:rows, :] for b, u in units], axis=0)
            charges = jnp.concatenate(
                [
                    jnp.concatenate(
                        [
                            buffers[b][u, rows:, g * TILE_LANES : (g + 1) * TILE_LANES]
                            for g in range(columns // TILE_ROWS)
                        ],
                        axis=0,
                    )
                    for b, u in units
                ],
                axis=1,
            )
            wide = source.astype(F32)
            source_norms = scale * jnp.sum(wide * wide, axis=1, keepdims=True)
            start = pl.multiple_of(leaf * leaf_size, leaf_size)
            kernel = gauss(
                source,
                source_norms,
                points[pl.ds(start, leaf_size), :],
                norms[0:1, pl.ds(start, leaf_size)],
                scale,
            )
            out[:, pl.ds(start, leaf_size)] += jnp.dot(
                charges, kernel, preferred_element_type=F32
            )


def near(buffers, groups, target, points, norms, before, leaf_size, gamma):
    width = points.shape[1]
    columns = before.shape[0]
    rows = sum(len(units) for units, _ in groups) * TILE_LANES
    whole = pl.BlockSpec(memory_space=pltpu.VMEM)
    return pl.pallas_call(
        functools.partial(near_body, gamma * LOG2E, groups, leaf_size),
        in_specs=[pl.BlockSpec(memory_space=pltpu.SMEM)] + [whole] * (3 + len(buffers)),
        out_specs=whole,
        out_shape=jax.ShapeDtypeStruct(before.shape, F32),
        compiler_params=params(20),
        cost_estimate=pl.CostEstimate(
            flops=2 * rows * leaf_size * (width + columns),
            bytes_accessed=rows * width * 2 + points.size * 2,
            transcendentals=rows * leaf_size,
        ),
        name="near",
    )(target, points, norms, before, *buffers)


def after(value, *others):
    return lax.optimization_barrier((value, *others))[0]


def local(points, charges, near_list, leaf_basis, transfer, parent, coarse_far, coarse_coupling):
    leaf_count, leaf_size, rank = leaf_basis.shape
    width = points.shape[1]
    columns = charges.shape[0]
    near_count = near_list.shape[1]
    members = lax.axis_size("sub")
    groups = lax.axis_size("grp")
    gamma = 2.0 / width

    def exchange(block):
        return lax.all_to_all(block, "sub", split_axis=0, concat_axis=0, tiled=True)

    def spread(block):
        return jnp.broadcast_to(block[None], (members, *block.shape))

    here = lax.axis_index("sub")
    y, z = here // RING, here % RING

    entries = near_list.reshape(-1)
    wanted = (entries // leaf_count)[None, :] == jnp.arange(members)[:, None]
    wanted = wanted & (entries >= 0)[None, :]
    requests = jnp.sum(jnp.where(wanted, entries[None, :] % leaf_count + 1, 0), axis=1)

    terms, tails = lift(charges, leaf_basis, transfer, parent, requests, width)
    terms = exchange(terms)
    asked = terms[:, columns, 0].astype(F32).astype(jnp.int32)

    pieces, rows = leaf_count * QUARTERS, leaf_size // QUARTERS
    plans = [[], [], []]
    for axis, way in DIRECTIONS:
        h = axis * (QUARTERS // 2)
        plans[0].append(
            [(offset(axis, 2, 0), 2 * way, 2)]
            + [(offset(axis, 2, across), h + way, 1) for across in (1, 3, 2)]
        )
        plans[1].append([(offset(axis, one(way), across), h, 2) for across in (1, 3, 2)])
        plans[2].append([(offset(axis, one(way), 0), 0, QUARTERS)])
    blocks = collect(
        points.reshape(pieces, rows, width),
        tails,
        asked,
        jnp.stack([y, z]).astype(jnp.int32),
        plans[0] + plans[1] + plans[2],
    )
    count = len(DIRECTIONS)

    def send(wait, values):
        return [step(v, d) for v, d in zip(held(wait, values), DIRECTIONS)]

    def held(wait, values):
        first = [after(values[0], *wait[0], *wait[1:])]
        return first + [after(v, w, *wait[1:]) for v, w in zip(values[1:], wait[0][1:])]

    chips = groups // 2

    def along_x(k, block, *gate):
        pairs = [(i, (i + 2 * k) % groups) for i in range(groups)]
        return lax.ppermute(after(block, *gate), "grp", pairs)

    def own_part(first, last, gate, *before):
        return own(after(points, *gate), charges, range(first, last), leaf_size, gamma, before)

    own_weight = jnp.sum(terms[:, :columns].astype(F32), axis=0).astype(BF)
    weights = exchange(spread(own_weight))
    blocks = [after(block, weights) for block in blocks]
    cut = leaf_count * 2 // 3
    got_1 = [step(v, d) for v, d in zip(blocks[:count], DIRECTIONS)]
    x_1 = along_x(1, weights, *blocks[:count])
    total, norms = own_part(0, cut, blocks[:count])
    got_2 = send((got_1, total, x_1), blocks[count : 2 * count])
    x_2 = along_x(2, weights, *got_1)
    total, norms = own_part(cut, leaf_count, got_1, total, norms)
    got_3 = send((got_2, total, x_2), got_1)
    x_3 = along_x(3, weights, *got_2, total)
    mine = jnp.concatenate([weights, x_1, x_2, x_3], axis=0)
    got_4 = send((got_3, x_3), blocks[2 * count :])
    swap = [(i, i ^ 1) for i in range(groups)]
    other = lax.ppermute(after(mine, *got_3), "grp", swap)
    plan_5, plan_6 = [], []
    for axis, way in DIRECTIONS:
        first = 2 * (1 - axis)
        plan_5.append(
            [(first, 4 + way, 1), (first + 1, 4 + way, 1), (4 + first + way, 4, 1)]
        )
        plan_6.append(
            [(first, 2 * way, 2), (first + 1, 2 * way, 2)]
            + [(4 + first, 2 + way, 1), (4 + first + 1, 2 + way, 1)]
        )
    woven = weave([*got_2, *got_3], plan_5 + plan_6)
    got_5 = send((got_4, *woven, other), woven[:count])
    far_ids = coarse_far[0]
    far_alive = (far_ids >= 0).astype(F32)
    ids = jnp.maximum(far_ids, 0)
    group = lax.axis_index("grp")
    from_group, node = ids // members, ids % members
    side = (from_group % 2) != (group % 2)
    at = (group // 2 - from_group // 2) % chips * members
    at = at + node
    crossed = after(other, *got_4)
    sources = jnp.where(side[:, None, None], crossed[at], mine[at])
    far_terms = lax.dot_general(
        sources, coarse_coupling[0], (((2,), (1,)), ((0,), (0,))), preferred_element_type=F32
    )
    field = jnp.sum(far_terms * far_alive[:, None, None], axis=0).astype(BF)
    fields = exchange(spread(field))
    got_6 = send((got_5, fields), woven[count:])
    add = functools.partial(near, leaf_size=leaf_size, gamma=gamma)
    groups_4, groups_6, groups_7 = [], [], []
    for d, (axis, way) in enumerate(DIRECTIONS):
        groups_4.append(([(count + d, 0), (count + d, 1)], number(offset(axis, 2, 0))))
        for k in range(0, QUARTERS, 2):
            groups_4.append(([(d, k), (d, k + 1)], number(offset(axis, one(way), 0))))
        for k, along in enumerate((1, 3, 2)):
            pair = [(d, 2 * k), (d, 2 * k + 1)]
            groups_6.append((pair, number(offset(1 - axis, along, one(way)))))
            if way == 0:
                groups_7.append(([(d, k), (d + 1, k)], number(offset(1 - axis, along, 2))))
    flat = near_list.reshape(-1)
    owner = jnp.where(flat >= 0, flat // leaf_count, 0)
    back = (y - owner // RING) % RING * RING + (z - owner % RING) % RING
    leaves = jnp.arange(flat.shape[0]) // near_count + 1
    match = (back[None, :] == jnp.arange(members)[:, None]) & (flat >= 0)[None, :]
    target = jnp.sum(jnp.where(match, leaves[None, :], 0), axis=1) - 1
    total = add([*got_4, *got_3], groups_4, target, points, norms, after(total, *got_5))
    got_7 = send((got_6, total), got_5)
    total = add(got_6, groups_6, target, points, norms, total)
    total = finish(fields, parent, transfer, leaf_basis, total)
    return add(got_7, groups_7, target, points, norms, total)


def solution(mesh):
    placed = (
        P(("grp", "sub"), None),
        P(None, ("grp", "sub")),
        P(("grp", "sub"), None),
        P(("grp", "sub"), None, None),
        P(("grp", "sub"), None, None),
        P(("grp", "sub")),
        P(("grp", "sub"), None),
        P(("grp", "sub"), None, None, None),
    )
    return jax.shard_map(
        local, mesh=mesh, in_specs=placed, out_specs=P(None, ("grp", "sub")), check_vma=False
    )
```

```python
import functools

import jax
import jax.numpy as jnp
from jax import lax
from jax.experimental import pallas as pl
from jax.experimental.pallas import tpu as pltpu
from jax.sharding import PartitionSpec as P

BF = jnp.bfloat16
F32 = jnp.float32
LOG2E = 1.4426950408889634
TILE_ROWS = 16
TILE_LANES = 128
RING = 4
QUARTERS = 4
DIRECTIONS = [(axis, way) for axis in range(2) for way in range(2)]
NT = (((1,), (1,)), ((), ()))
MIB = 1024 * 1024


def params(size):
    return pltpu.CompilerParams(vmem_limit_bytes=size * MIB)


def offset(axis, along, across):
    return (along, across) if axis == 0 else (across, along)


def number(steps):
    return steps[0] * RING + steps[1]


def one(way):
    return 1 if way == 0 else RING - 1


def step(block, direction):
    return turn(block, *offset(direction[0], one(direction[1]), 0))


def turn(block, y, z):
    pairs = [
        (d, (d // RING + y) % RING * RING + (d % RING + z) % RING) for d in range(RING * RING)
    ]
    return lax.ppermute(block, "sub", pairs)


def collect(points, tails, asked, place, plans):
    pieces, rows, width = points.shape
    extra = tails.shape[1]
    sizes = [sum(run[2] for run in plan) for plan in plans]
    runs = []
    for number, plan in enumerate(plans):
        at = 0
        for steps, quarter, length in plan:
            runs.append((number, at, steps, quarter, length))
            at += length

    def body(asked, place, points, tails, *rest):
        outs, sems = rest[:-1], rest[-1]

        def wanted(steps):
            y = (place[0] + steps[0]) % RING
            z = (place[1] + steps[1]) % RING
            return asked[y * RING + z]

        def copies(k):
            number, at, steps, quarter, length = runs[k]
            first = jnp.maximum(wanted(steps) - 1, 0) * QUARTERS + quarter
            return (
                pltpu.make_async_copy(
                    points.at[pl.ds(first, length)],
                    outs[number].at[pl.ds(at, length), pl.ds(0, rows)],
                    sems.at[k, 0],
                ),
                pltpu.make_async_copy(
                    tails.at[pl.ds(first, length)],
                    outs[number].at[pl.ds(at, length), pl.ds(rows, extra)],
                    sems.at[k, 1],
                ),
            )

        for k in range(len(runs)):

            @pl.when(wanted(runs[k][2]) > 0)
            def _(k=k):
                for copy in copies(k):
                    copy.start()

        for k in range(len(runs)):

            @pl.when(wanted(runs[k][2]) > 0)
            def _(k=k):
                for copy in copies(k):
                    copy.wait()

    scalar = pl.BlockSpec(memory_space=pltpu.SMEM)
    return pl.pallas_call(
        body,
        in_specs=[scalar, scalar] + [pl.BlockSpec(memory_space=pltpu.VMEM)] * 2,
        out_specs=[pl.BlockSpec(memory_space=pltpu.HBM)] * len(plans),
        out_shape=[jax.ShapeDtypeStruct((n, rows + extra, width), BF) for n in sizes],
        scratch_shapes=[pltpu.SemaphoreType.DMA((len(runs), 2))],
        compiler_params=params(63),
        cost_estimate=pl.CostEstimate(
            flops=0, bytes_accessed=sum(sizes) * rows * width * 4, transcendentals=0
        ),
        name="collect",
    )(asked, place, points, tails)


def weave(sources, plans):
    shape = sources[0].shape[1:]
    sizes = [sum(run[2] for run in plan) for plan in plans]
    runs = []
    for place, plan in enumerate(plans):
        at = 0
        for source, first, length in plan:
            runs.append((source, first, length, place, at, sum(sizes[:place]) + at))
            at += length

    def body(*refs):
        ins = refs[: len(sources)]
        outs = refs[len(sources) : -3]
        held, loads, stores = refs[-3:]
        first_leg, second_leg = [], []
        for k, (source, first, length, place, at, row) in enumerate(runs):
            staged = held.at[pl.ds(row, length)]
            first_leg.append(
                pltpu.make_async_copy(
                    ins[source].at[pl.ds(first, length)], staged, loads.at[k]
                )
            )
            second_leg.append(
                pltpu.make_async_copy(staged, outs[place].at[pl.ds(at, length)], stores.at[k])
            )
        for copy in first_leg:
            copy.start()
        for load, store in zip(first_leg, second_leg):
            load.wait()
            store.start()
        for copy in second_leg:
            copy.wait()

    return pl.pallas_call(
        body,
        in_specs=[pl.BlockSpec(memory_space=pl.ANY)] * len(sources),
        out_specs=[pl.BlockSpec(memory_space=pltpu.HBM)] * len(plans),
        out_shape=[jax.ShapeDtypeStruct((size, *shape), BF) for size in sizes],
        scratch_shapes=[
            pltpu.VMEM((sum(sizes), *shape), BF),
            pltpu.SemaphoreType.DMA((len(runs),)),
            pltpu.SemaphoreType.DMA((len(runs),)),
        ],
        compiler_params=params(63),
        cost_estimate=pl.CostEstimate(
            flops=0,
            bytes_accessed=4 * sum(sizes) * shape[0] * shape[1],
            transcendentals=0,
        ),
        name="weave",
    )(*sources)


def lift(charges, leaf_basis, transfer, slots, requests, width):
    leaf_count, leaf_size, rank = leaf_basis.shape
    columns = charges.shape[0]
    lines, rows = columns // TILE_ROWS, leaf_size // QUARTERS
    members = requests.shape[0]

    def body(slots, requests, charges, basis, transfer, out, tails, sums):
        t = pl.program_id(0)
        tails[...] = jnp.zeros_like(tails)
        for q in range(QUARTERS):
            for g in range(lines):
                tails[q, :, g * rows : (g + 1) * rows] = charges[
                    g * TILE_ROWS : (g + 1) * TILE_ROWS, q * rows : (q + 1) * rows
                ]

        @pl.when(t == 0)
        def _():
            sums[...] = jnp.zeros_like(sums)

        skeleton = jnp.dot(charges[...], basis[0], preferred_element_type=F32).astype(BF)
        sums[slots[t]] += jnp.dot(skeleton, transfer[0], preferred_element_type=F32)

        @pl.when(t == leaf_count - 1)
        def _():
            out[:, 0:columns, :] = sums[...].astype(BF)
            for d in range(members):
                value = requests[d].astype(F32)
                out[d, columns:, :] = jnp.full((TILE_ROWS, rank), value, F32).astype(BF)

    return pl.pallas_call(
        body,
        grid_spec=pltpu.PrefetchScalarGridSpec(
            num_scalar_prefetch=2,
            grid=(leaf_count,),
            in_specs=[
                pl.BlockSpec((columns, leaf_size), lambda t, s, r: (0, t)),
                pl.BlockSpec((1, leaf_size, rank), lambda t, s, r: (t, 0, 0)),
                pl.BlockSpec((1, rank, rank), lambda t, s, r: (t, 0, 0)),
            ],
            out_specs=[
                pl.BlockSpec((members, columns + TILE_ROWS, rank), lambda t, s, r: (0, 0, 0)),
                pl.BlockSpec((QUARTERS, TILE_ROWS, width), lambda t, s, r: (t, 0, 0)),
            ],
            scratch_shapes=[pltpu.VMEM((members, columns, rank), F32)],
        ),
        out_shape=[
            jax.ShapeDtypeStruct((members, columns + TILE_ROWS, rank), BF),
            jax.ShapeDtypeStruct((leaf_count * QUARTERS, TILE_ROWS, width), BF),
        ],
        compiler_params=params(63),
        name="lift",
    )(slots, requests, charges, leaf_basis, transfer)


def finish(fields, slots, transfer, leaf_basis, total):
    leaf_count, leaf_size, rank = leaf_basis.shape
    columns = total.shape[0]

    def body(slots, field, transfer, basis, total, out):
        descended = lax.dot_general(
            field[0], transfer[0], NT, preferred_element_type=F32
        ).astype(BF)
        out[...] = total[...] + lax.dot_general(
            descended, basis[0], NT, preferred_element_type=F32
        )

    return pl.pallas_call(
        body,
        grid_spec=pltpu.PrefetchScalarGridSpec(
            num_scalar_prefetch=1,
            grid=(leaf_count,),
            in_specs=[
                pl.BlockSpec((1, columns, rank), lambda t, s: (s[t], 0, 0)),
                pl.BlockSpec((1, rank, rank), lambda t, s: (t, 0, 0)),
                pl.BlockSpec((1, leaf_size, rank), lambda t, s: (t, 0, 0)),
                pl.BlockSpec((columns, leaf_size), lambda t, s: (0, t)),
            ],
            out_specs=pl.BlockSpec((columns, leaf_size), lambda t, s: (0, t)),
        ),
        out_shape=jax.ShapeDtypeStruct(total.shape, F32),
        compiler_params=params(8),
        name="finish",
    )(slots, fields, transfer, leaf_basis, total)


def gauss(source, source_norms, target, target_norms, scale):
    gram = lax.dot_general(source, target, NT, preferred_element_type=F32)
    return jnp.exp2((2.0 * scale) * gram - (source_norms + target_norms)).astype(BF)


def own_body(scale, leaf_size, first, second, ti, sj, ci, cj, *rest):
    before, (out, rows, col) = rest[:-3], rest[-3:]
    step = pl.program_id(0)
    width = ti.shape[1]
    i0 = pl.multiple_of(first[step] * leaf_size, leaf_size)
    j0 = pl.multiple_of(second[step] * leaf_size, leaf_size)
    ones = jnp.ones((8, width), BF)
    lanes = jnp.ones((width, TILE_LANES), BF)

    @pl.when(step == 0)
    def _():
        if before:
            out[...] = before[0][...]
            rows[...] = before[1][...]
        else:
            out[...] = jnp.zeros_like(out)
            rows[...] = jnp.zeros_like(rows)

    @pl.when(i0 == j0)
    def _():
        wide = sj[...].astype(F32)
        square = wide * wide
        high = square.astype(BF)
        low = (square - high.astype(F32)).astype(BF)
        row = lax.dot_general(ones, high, NT, preferred_element_type=F32) + lax.dot_general(
            ones, low, NT, preferred_element_type=F32
        )
        rows[:, pl.ds(i0, leaf_size)] = scale * row
        column = jnp.dot(high, lanes, preferred_element_type=F32) + jnp.dot(
            low, lanes, preferred_element_type=F32
        )
        col[pl.ds(i0, leaf_size), :] = scale * column

    gram = lax.dot_general(sj[...], ti[...], NT, preferred_element_type=F32)
    norms = col[pl.ds(j0, leaf_size), :][:, :1] + rows[0:1, pl.ds(i0, leaf_size)]
    kernel = jnp.exp2((2.0 * scale) * gram - norms).astype(BF)
    out[:, pl.ds(i0, leaf_size)] += jnp.dot(cj[...], kernel, preferred_element_type=F32)

    @pl.when(i0 != j0)
    def _():
        out[:, pl.ds(j0, leaf_size)] += lax.dot_general(
            ci[...], kernel, NT, preferred_element_type=F32
        )


def own(points, charges, columns_of, leaf_size, gamma, before=()):
    width = points.shape[1]
    columns = charges.shape[0]
    total = points.shape[0]
    pairs = [(i, j) for j in columns_of for i in range(j, -1, -1)]
    first = jnp.array([p[0] for p in pairs], jnp.int32)
    second = jnp.array([p[1] for p in pairs], jnp.int32)
    return pl.pallas_call(
        functools.partial(own_body, gamma * LOG2E, leaf_size),
        grid_spec=pltpu.PrefetchScalarGridSpec(
            num_scalar_prefetch=2,
            grid=(len(pairs),),
            in_specs=[
                pl.BlockSpec((leaf_size, width), lambda s, a, b: (a[s], 0)),
                pl.BlockSpec((leaf_size, width), lambda s, a, b: (b[s], 0)),
                pl.BlockSpec((columns, leaf_size), lambda s, a, b: (0, a[s])),
                pl.BlockSpec((columns, leaf_size), lambda s, a, b: (0, b[s])),
            ]
            + [pl.BlockSpec(b.shape, lambda s, a, b: (0, 0)) for b in before],
            out_specs=[
                pl.BlockSpec((columns, total), lambda s, a, b: (0, 0)),
                pl.BlockSpec((8, total), lambda s, a, b: (0, 0)),
            ],
            scratch_shapes=[pltpu.VMEM((total, TILE_LANES), F32)],
        ),
        out_shape=[
            jax.ShapeDtypeStruct((columns, total), F32),
            jax.ShapeDtypeStruct((8, total), F32),
        ],
        compiler_params=params(63),
        cost_estimate=pl.CostEstimate(
            flops=2 * len(pairs) * leaf_size * leaf_size * (width + 2 * columns),
            bytes_accessed=total * width * 8,
            transcendentals=len(pairs) * leaf_size * leaf_size,
        ),
        name="own",
    )(first, second, points, points, charges, charges, *before)


def near_body(scale, groups, leaf_size, target, points, norms, before, *refs):
    buffers, out = refs[:-1], refs[-1]
    columns = before.shape[0]
    rows = buffers[0].shape[1] - TILE_ROWS
    out[...] = before[...]
    for units, source_steps in groups:
        leaf = target[source_steps]

        @pl.when(leaf >= 0)
        def _(units=units, leaf=leaf):
            source = jnp.concatenate([buffers[b][u, 0:rows, :] for b, u in units], axis=0)
            charges = jnp.concatenate(
                [
                    jnp.concatenate(
                        [
                            buffers[b][u, rows:, g * TILE_LANES : (g + 1) * TILE_LANES]
                            for g in range(columns // TILE_ROWS)
                        ],
                        axis=0,
                    )
                    for b, u in units
                ],
                axis=1,
            )
            wide = source.astype(F32)
            source_norms = scale * jnp.sum(wide * wide, axis=1, keepdims=True)
            start = pl.multiple_of(leaf * leaf_size, leaf_size)
            kernel = gauss(
                source,
                source_norms,
                points[pl.ds(start, leaf_size), :],
                norms[0:1, pl.ds(start, leaf_size)],
                scale,
            )
            out[:, pl.ds(start, leaf_size)] += jnp.dot(
                charges, kernel, preferred_element_type=F32
            )


def near(buffers, groups, target, points, norms, before, leaf_size, gamma):
    width = points.shape[1]
    columns = before.shape[0]
    rows = sum(len(units) for units, _ in groups) * TILE_LANES
    whole = pl.BlockSpec(memory_space=pltpu.VMEM)
    return pl.pallas_call(
        functools.partial(near_body, gamma * LOG2E, groups, leaf_size),
        in_specs=[pl.BlockSpec(memory_space=pltpu.SMEM)] + [whole] * (3 + len(buffers)),
        out_specs=whole,
        out_shape=jax.ShapeDtypeStruct(before.shape, F32),
        compiler_params=params(20),
        cost_estimate=pl.CostEstimate(
            flops=2 * rows * leaf_size * (width + columns),
            bytes_accessed=rows * width * 2 + points.size * 2,
            transcendentals=rows * leaf_size,
        ),
        name="near",
    )(target, points, norms, before, *buffers)


def after(value, *others):
    return lax.optimization_barrier((value, *others))[0]


def local(points, charges, near_list, leaf_basis, transfer, parent, coarse_far, coarse_coupling):
    leaf_count, leaf_size, rank = leaf_basis.shape
    width = points.shape[1]
    columns = charges.shape[0]
    near_count = near_list.shape[1]
    members = lax.axis_size("sub")
    groups = lax.axis_size("grp")
    gamma = 2.0 / width

    def exchange(block):
        return lax.all_to_all(block, "sub", split_axis=0, concat_axis=0, tiled=True)

    def spread(block):
        return jnp.broadcast_to(block[None], (members, *block.shape))

    here = lax.axis_index("sub")
    y, z = here // RING, here % RING

    entries = near_list.reshape(-1)
    wanted = (entries // leaf_count)[None, :] == jnp.arange(members)[:, None]
    wanted = wanted & (entries >= 0)[None, :]
    requests = jnp.sum(jnp.where(wanted, entries[None, :] % leaf_count + 1, 0), axis=1)

    terms, tails = lift(charges, leaf_basis, transfer, parent, requests, width)
    terms = exchange(terms)
    asked = terms[:, columns, 0].astype(F32).astype(jnp.int32)

    own_weight = jnp.sum(terms[:, :columns].astype(F32), axis=0).astype(BF)
    weights = exchange(spread(own_weight))
    pieces, rows = leaf_count * QUARTERS, leaf_size // QUARTERS
    plans = [[], [], []]
    for axis, way in DIRECTIONS:
        h = axis * (QUARTERS // 2)
        plans[0].append(
            [(offset(axis, 2, 0), 2 * way, 2)]
            + [(offset(axis, 2, across), h + way, 1) for across in (1, 3, 2)]
        )
        plans[1].append([(offset(axis, one(way), across), h, 2) for across in (1, 3, 2)])
        plans[2].append([(offset(axis, one(way), 0), 0, QUARTERS)])
    blocks = collect(
        points.reshape(pieces, rows, width),
        tails,
        after(asked, own_weight),
        jnp.stack([y, z]).astype(jnp.int32),
        plans[0] + plans[1] + plans[2],
    )
    count = len(DIRECTIONS)

    def send(wait, values):
        return [step(v, d) for v, d in zip(held(wait, values), DIRECTIONS)]

    def held(wait, values):
        first = [after(values[0], *wait[0], *wait[1:])]
        return first + [after(v, w, *wait[1:]) for v, w in zip(values[1:], wait[0][1:])]

    chips = groups // 2

    def along_x(k, block, *gate):
        pairs = [(i, (i + 2 * k) % groups) for i in range(groups)]
        return lax.ppermute(after(block, *gate), "grp", pairs)

    def own_part(first, last, gate, *before):
        return own(after(points, *gate), charges, range(first, last), leaf_size, gamma, before)

    blocks = [after(block, weights) for block in blocks]
    cut = leaf_count * 2 // 3
    got_1 = [step(v, d) for v, d in zip(blocks[:count], DIRECTIONS)]
    x_1 = along_x(1, weights, *blocks[:count])
    total, norms = own_part(0, cut, blocks[:count])
    got_2 = send((got_1, total, x_1), blocks[count : 2 * count])
    x_2 = along_x(2, weights, *got_1)
    total, norms = own_part(cut, leaf_count, got_1, total, norms)
    got_3 = send((got_2, total, x_2), got_1)
    x_3 = along_x(3, weights, *got_2, total)
    mine = jnp.concatenate([weights, x_1, x_2, x_3], axis=0)
    got_4 = send((got_3, x_3), blocks[2 * count :])
    swap = [(i, i ^ 1) for i in range(groups)]
    other = lax.ppermute(after(mine, *got_3), "grp", swap)
    plan_5, plan_6 = [], []
    for axis, way in DIRECTIONS:
        first = 2 * (1 - axis)
        plan_5.append(
            [(first, 4 + way, 1), (first + 1, 4 + way, 1), (4 + first + way, 4, 1)]
        )
        plan_6.append(
            [(first, 2 * way, 2), (first + 1, 2 * way, 2)]
            + [(4 + first, 2 + way, 1), (4 + first + 1, 2 + way, 1)]
        )
    woven = weave([*got_2, *got_3], plan_5 + plan_6)
    far_ids = coarse_far[0]
    far_alive = (far_ids >= 0).astype(F32)
    ids = jnp.maximum(far_ids, 0)
    group = lax.axis_index("grp")
    from_group, node = ids // members, ids % members
    side = (from_group % 2) != (group % 2)
    at = (group // 2 - from_group // 2) % chips * members
    at = at + node
    sources = jnp.where(side[:, None, None], other[at], mine[at])
    far_terms = lax.dot_general(
        sources, coarse_coupling[0], (((2,), (1,)), ((0,), (0,))), preferred_element_type=F32
    )
    field = jnp.sum(far_terms * far_alive[:, None, None], axis=0).astype(BF)
    fields = exchange(spread(after(field, woven[0])))
    got_5 = send((got_4, *woven, fields), woven[:count])
    got_6 = send((got_5, fields), woven[count:])
    add = functools.partial(near, leaf_size=leaf_size, gamma=gamma)
    groups_4, groups_6, groups_7 = [], [], []
    for d, (axis, way) in enumerate(DIRECTIONS):
        groups_4.append(([(count + d, 0), (count + d, 1)], number(offset(axis, 2, 0))))
        for k in range(0, QUARTERS, 2):
            groups_4.append(([(d, k), (d, k + 1)], number(offset(axis, one(way), 0))))
        for k, along in enumerate((1, 3, 2)):
            pair = [(d, 2 * k), (d, 2 * k + 1)]
            groups_6.append((pair, number(offset(1 - axis, along, one(way)))))
            if way == 0:
                groups_7.append(([(d, k), (d + 1, k)], number(offset(1 - axis, along, 2))))
    flat = near_list.reshape(-1)
    owner = jnp.where(flat >= 0, flat // leaf_count, 0)
    back = (y - owner // RING) % RING * RING + (z - owner % RING) % RING
    leaves = jnp.arange(flat.shape[0]) // near_count + 1
    match = (back[None, :] == jnp.arange(members)[:, None]) & (flat >= 0)[None, :]
    target = jnp.sum(jnp.where(match, leaves[None, :], 0), axis=1) - 1
    total = add([*got_4, *got_3], groups_4, target, points, norms, after(total, *got_5))
    got_7 = send((got_6, total), got_5)
    total = add(got_6, groups_6, target, points, norms, total)
    total = finish(fields, parent, transfer, leaf_basis, total)
    return add(got_7, groups_7, target, points, norms, total)


def solution(mesh):
    placed = (
        P(("grp", "sub"), None),
        P(None, ("grp", "sub")),
        P(("grp", "sub"), None),
        P(("grp", "sub"), None, None),
        P(("grp", "sub"), None, None),
        P(("grp", "sub")),
        P(("grp", "sub"), None),
        P(("grp", "sub"), None, None, None),
    )
    return jax.shard_map(
        local, mesh=mesh, in_specs=placed, out_specs=P(None, ("grp", "sub")), check_vma=False
    )
```

```python
import functools

import jax
import jax.numpy as jnp
from jax import lax
from jax.experimental import pallas as pl
from jax.experimental.pallas import tpu as pltpu
from jax.sharding import PartitionSpec as P

BF = jnp.bfloat16
F32 = jnp.float32
LOG2E = 1.4426950408889634
TILE_ROWS = 16
TILE_LANES = 128
RING = 4
QUARTERS = 4
DIRECTIONS = [(axis, way) for axis in range(2) for way in range(2)]
NT = (((1,), (1,)), ((), ()))
MIB = 1024 * 1024


def params(size):
    return pltpu.CompilerParams(vmem_limit_bytes=size * MIB)


def offset(axis, along, across):
    return (along, across) if axis == 0 else (across, along)


def number(steps):
    return steps[0] * RING + steps[1]


def one(way):
    return 1 if way == 0 else RING - 1


def step(block, direction):
    return turn(block, *offset(direction[0], one(direction[1]), 0))


def turn(block, y, z):
    pairs = [
        (d, (d // RING + y) % RING * RING + (d % RING + z) % RING) for d in range(RING * RING)
    ]
    return lax.ppermute(block, "sub", pairs)


def collect(points, tails, asked, place, plans):
    pieces, rows, width = points.shape
    extra = tails.shape[1]
    sizes = [sum(run[2] for run in plan) for plan in plans]
    runs = []
    for number, plan in enumerate(plans):
        at = 0
        for steps, quarter, length in plan:
            runs.append((number, at, steps, quarter, length))
            at += length

    def body(asked, place, points, tails, *rest):
        outs, sems = rest[:-1], rest[-1]

        def wanted(steps):
            y = (place[0] + steps[0]) % RING
            z = (place[1] + steps[1]) % RING
            return asked[y * RING + z]

        def copies(k):
            number, at, steps, quarter, length = runs[k]
            first = jnp.maximum(wanted(steps) - 1, 0) * QUARTERS + quarter
            return (
                pltpu.make_async_copy(
                    points.at[pl.ds(first, length)],
                    outs[number].at[pl.ds(at, length), pl.ds(0, rows)],
                    sems.at[k, 0],
                ),
                pltpu.make_async_copy(
                    tails.at[pl.ds(first, length)],
                    outs[number].at[pl.ds(at, length), pl.ds(rows, extra)],
                    sems.at[k, 1],
                ),
            )

        for k in range(len(runs)):

            @pl.when(wanted(runs[k][2]) > 0)
            def _(k=k):
                for copy in copies(k):
                    copy.start()

        for k in range(len(runs)):

            @pl.when(wanted(runs[k][2]) > 0)
            def _(k=k):
                for copy in copies(k):
                    copy.wait()

    scalar = pl.BlockSpec(memory_space=pltpu.SMEM)
    return pl.pallas_call(
        body,
        in_specs=[scalar, scalar] + [pl.BlockSpec(memory_space=pltpu.VMEM)] * 2,
        out_specs=[pl.BlockSpec(memory_space=pltpu.HBM)] * len(plans),
        out_shape=[jax.ShapeDtypeStruct((n, rows + extra, width), BF) for n in sizes],
        scratch_shapes=[pltpu.SemaphoreType.DMA((len(runs), 2))],
        compiler_params=params(63),
        cost_estimate=pl.CostEstimate(
            flops=0, bytes_accessed=sum(sizes) * rows * width * 4, transcendentals=0
        ),
        name="collect",
    )(asked, place, points, tails)


def weave(sources, plans):
    shape = sources[0].shape[1:]
    sizes = [sum(run[2] for run in plan) for plan in plans]
    runs = []
    for place, plan in enumerate(plans):
        at = 0
        for source, first, length in plan:
            runs.append((source, first, length, place, at, sum(sizes[:place]) + at))
            at += length

    def body(*refs):
        ins = refs[: len(sources)]
        outs = refs[len(sources) : -3]
        held, loads, stores = refs[-3:]
        first_leg, second_leg = [], []
        for k, (source, first, length, place, at, row) in enumerate(runs):
            staged = held.at[pl.ds(row, length)]
            first_leg.append(
                pltpu.make_async_copy(
                    ins[source].at[pl.ds(first, length)], staged, loads.at[k]
                )
            )
            second_leg.append(
                pltpu.make_async_copy(staged, outs[place].at[pl.ds(at, length)], stores.at[k])
            )
        for copy in first_leg:
            copy.start()
        for load, store in zip(first_leg, second_leg):
            load.wait()
            store.start()
        for copy in second_leg:
            copy.wait()

    return pl.pallas_call(
        body,
        in_specs=[pl.BlockSpec(memory_space=pl.ANY)] * len(sources),
        out_specs=[pl.BlockSpec(memory_space=pltpu.HBM)] * len(plans),
        out_shape=[jax.ShapeDtypeStruct((size, *shape), BF) for size in sizes],
        scratch_shapes=[
            pltpu.VMEM((sum(sizes), *shape), BF),
            pltpu.SemaphoreType.DMA((len(runs),)),
            pltpu.SemaphoreType.DMA((len(runs),)),
        ],
        compiler_params=params(63),
        cost_estimate=pl.CostEstimate(
            flops=0,
            bytes_accessed=4 * sum(sizes) * shape[0] * shape[1],
            transcendentals=0,
        ),
        name="weave",
    )(*sources)


def lift(charges, leaf_basis, transfer, slots, requests, width):
    leaf_count, leaf_size, rank = leaf_basis.shape
    columns = charges.shape[0]
    lines, rows = columns // TILE_ROWS, leaf_size // QUARTERS
    members = requests.shape[0]

    def body(slots, requests, charges, basis, transfer, out, tails, sums):
        t = pl.program_id(0)
        tails[...] = jnp.zeros_like(tails)
        for q in range(QUARTERS):
            for g in range(lines):
                tails[q, :, g * rows : (g + 1) * rows] = charges[
                    g * TILE_ROWS : (g + 1) * TILE_ROWS, q * rows : (q + 1) * rows
                ]

        @pl.when(t == 0)
        def _():
            sums[...] = jnp.zeros_like(sums)

        skeleton = jnp.dot(charges[...], basis[0], preferred_element_type=F32).astype(BF)
        sums[slots[t]] += jnp.dot(skeleton, transfer[0], preferred_element_type=F32)

        @pl.when(t == leaf_count - 1)
        def _():
            out[:, 0:columns, :] = sums[...].astype(BF)
            for d in range(members):
                value = requests[d].astype(F32)
                out[d, columns:, :] = jnp.full((TILE_ROWS, rank), value, F32).astype(BF)

    return pl.pallas_call(
        body,
        grid_spec=pltpu.PrefetchScalarGridSpec(
            num_scalar_prefetch=2,
            grid=(leaf_count,),
            in_specs=[
                pl.BlockSpec((columns, leaf_size), lambda t, s, r: (0, t)),
                pl.BlockSpec((1, leaf_size, rank), lambda t, s, r: (t, 0, 0)),
                pl.BlockSpec((1, rank, rank), lambda t, s, r: (t, 0, 0)),
            ],
            out_specs=[
                pl.BlockSpec((members, columns + TILE_ROWS, rank), lambda t, s, r: (0, 0, 0)),
                pl.BlockSpec((QUARTERS, TILE_ROWS, width), lambda t, s, r: (t, 0, 0)),
            ],
            scratch_shapes=[pltpu.VMEM((members, columns, rank), F32)],
        ),
        out_shape=[
            jax.ShapeDtypeStruct((members, columns + TILE_ROWS, rank), BF),
            jax.ShapeDtypeStruct((leaf_count * QUARTERS, TILE_ROWS, width), BF),
        ],
        compiler_params=params(63),
        name="lift",
    )(slots, requests, charges, leaf_basis, transfer)


def finish(fields, slots, transfer, leaf_basis, total):
    leaf_count, leaf_size, rank = leaf_basis.shape
    columns = total.shape[0]

    def body(slots, field, transfer, basis, total, out):
        descended = lax.dot_general(
            field[0], transfer[0], NT, preferred_element_type=F32
        ).astype(BF)
        out[...] = total[...] + lax.dot_general(
            descended, basis[0], NT, preferred_element_type=F32
        )

    return pl.pallas_call(
        body,
        grid_spec=pltpu.PrefetchScalarGridSpec(
            num_scalar_prefetch=1,
            grid=(leaf_count,),
            in_specs=[
                pl.BlockSpec((1, columns, rank), lambda t, s: (s[t], 0, 0)),
                pl.BlockSpec((1, rank, rank), lambda t, s: (t, 0, 0)),
                pl.BlockSpec((1, leaf_size, rank), lambda t, s: (t, 0, 0)),
                pl.BlockSpec((columns, leaf_size), lambda t, s: (0, t)),
            ],
            out_specs=pl.BlockSpec((columns, leaf_size), lambda t, s: (0, t)),
        ),
        out_shape=jax.ShapeDtypeStruct(total.shape, F32),
        compiler_params=params(8),
        name="finish",
    )(slots, fields, transfer, leaf_basis, total)


def gauss(source, source_norms, target, target_norms, scale):
    gram = lax.dot_general(source, target, NT, preferred_element_type=F32)
    return jnp.exp2((2.0 * scale) * gram - (source_norms + target_norms)).astype(BF)


def own_body(scale, leaf_size, first, second, ti, sj, ci, cj, *rest):
    before, (out, rows, col) = rest[:-3], rest[-3:]
    step = pl.program_id(0)
    width = ti.shape[1]
    i0 = pl.multiple_of(first[step] * leaf_size, leaf_size)
    j0 = pl.multiple_of(second[step] * leaf_size, leaf_size)
    ones = jnp.ones((8, width), BF)
    lanes = jnp.ones((width, TILE_LANES), BF)

    @pl.when(step == 0)
    def _():
        if before:
            out[...] = before[0][...]
            rows[...] = before[1][...]
        else:
            out[...] = jnp.zeros_like(out)
            rows[...] = jnp.zeros_like(rows)

    @pl.when(i0 == j0)
    def _():
        wide = sj[...].astype(F32)
        square = wide * wide
        high = square.astype(BF)
        low = (square - high.astype(F32)).astype(BF)
        row = lax.dot_general(ones, high, NT, preferred_element_type=F32) + lax.dot_general(
            ones, low, NT, preferred_element_type=F32
        )
        rows[:, pl.ds(i0, leaf_size)] = scale * row
        column = jnp.dot(high, lanes, preferred_element_type=F32) + jnp.dot(
            low, lanes, preferred_element_type=F32
        )
        col[pl.ds(i0, leaf_size), :] = scale * column

    gram = lax.dot_general(sj[...], ti[...], NT, preferred_element_type=F32)
    norms = col[pl.ds(j0, leaf_size), :][:, :1] + rows[0:1, pl.ds(i0, leaf_size)]
    kernel = jnp.exp2((2.0 * scale) * gram - norms).astype(BF)
    out[:, pl.ds(i0, leaf_size)] += jnp.dot(cj[...], kernel, preferred_element_type=F32)

    @pl.when(i0 != j0)
    def _():
        out[:, pl.ds(j0, leaf_size)] += lax.dot_general(
            ci[...], kernel, NT, preferred_element_type=F32
        )


def own(points, charges, columns_of, leaf_size, gamma, before=()):
    width = points.shape[1]
    columns = charges.shape[0]
    total = points.shape[0]
    pairs = [(i, j) for j in columns_of for i in range(j, -1, -1)]
    first = jnp.array([p[0] for p in pairs], jnp.int32)
    second = jnp.array([p[1] for p in pairs], jnp.int32)
    return pl.pallas_call(
        functools.partial(own_body, gamma * LOG2E, leaf_size),
        grid_spec=pltpu.PrefetchScalarGridSpec(
            num_scalar_prefetch=2,
            grid=(len(pairs),),
            in_specs=[
                pl.BlockSpec((leaf_size, width), lambda s, a, b: (a[s], 0)),
                pl.BlockSpec((leaf_size, width), lambda s, a, b: (b[s], 0)),
                pl.BlockSpec((columns, leaf_size), lambda s, a, b: (0, a[s])),
                pl.BlockSpec((columns, leaf_size), lambda s, a, b: (0, b[s])),
            ]
            + [pl.BlockSpec(b.shape, lambda s, a, b: (0, 0)) for b in before],
            out_specs=[
                pl.BlockSpec((columns, total), lambda s, a, b: (0, 0)),
                pl.BlockSpec((8, total), lambda s, a, b: (0, 0)),
            ],
            scratch_shapes=[pltpu.VMEM((total, TILE_LANES), F32)],
        ),
        out_shape=[
            jax.ShapeDtypeStruct((columns, total), F32),
            jax.ShapeDtypeStruct((8, total), F32),
        ],
        compiler_params=params(63),
        cost_estimate=pl.CostEstimate(
            flops=2 * len(pairs) * leaf_size * leaf_size * (width + 2 * columns),
            bytes_accessed=total * width * 8,
            transcendentals=len(pairs) * leaf_size * leaf_size,
        ),
        name="own",
    )(first, second, points, points, charges, charges, *before)


def near_body(scale, groups, leaf_size, target, points, norms, before, *refs):
    buffers, out = refs[:-1], refs[-1]
    columns = before.shape[0]
    rows = buffers[0].shape[1] - TILE_ROWS
    out[...] = before[...]
    for units, source_steps in groups:
        leaf = target[source_steps]

        @pl.when(leaf >= 0)
        def _(units=units, leaf=leaf):
            source = jnp.concatenate([buffers[b][u, 0:rows, :] for b, u in units], axis=0)
            charges = jnp.concatenate(
                [
                    jnp.concatenate(
                        [
                            buffers[b][u, rows:, g * TILE_LANES : (g + 1) * TILE_LANES]
                            for g in range(columns // TILE_ROWS)
                        ],
                        axis=0,
                    )
                    for b, u in units
                ],
                axis=1,
            )
            wide = source.astype(F32)
            source_norms = scale * jnp.sum(wide * wide, axis=1, keepdims=True)
            start = pl.multiple_of(leaf * leaf_size, leaf_size)
            kernel = gauss(
                source,
                source_norms,
                points[pl.ds(start, leaf_size), :],
                norms[0:1, pl.ds(start, leaf_size)],
                scale,
            )
            out[:, pl.ds(start, leaf_size)] += jnp.dot(
                charges, kernel, preferred_element_type=F32
            )


def near(buffers, groups, target, points, norms, before, leaf_size, gamma):
    width = points.shape[1]
    columns = before.shape[0]
    rows = sum(len(units) for units, _ in groups) * TILE_LANES
    whole = pl.BlockSpec(memory_space=pltpu.VMEM)
    return pl.pallas_call(
        functools.partial(near_body, gamma * LOG2E, groups, leaf_size),
        in_specs=[pl.BlockSpec(memory_space=pltpu.SMEM)] + [whole] * (3 + len(buffers)),
        out_specs=whole,
        out_shape=jax.ShapeDtypeStruct(before.shape, F32),
        compiler_params=params(20),
        cost_estimate=pl.CostEstimate(
            flops=2 * rows * leaf_size * (width + columns),
            bytes_accessed=rows * width * 2 + points.size * 2,
            transcendentals=rows * leaf_size,
        ),
        name="near",
    )(target, points, norms, before, *buffers)


def after(value, *others):
    return lax.optimization_barrier((value, *others))[0]


def local(points, charges, near_list, leaf_basis, transfer, parent, coarse_far, coarse_coupling):
    leaf_count, leaf_size, rank = leaf_basis.shape
    width = points.shape[1]
    columns = charges.shape[0]
    near_count = near_list.shape[1]
    members = lax.axis_size("sub")
    groups = lax.axis_size("grp")
    gamma = 2.0 / width

    def exchange(block):
        return lax.all_to_all(block, "sub", split_axis=0, concat_axis=0, tiled=True)

    def spread(block):
        return jnp.broadcast_to(block[None], (members, *block.shape))

    here = lax.axis_index("sub")
    y, z = here // RING, here % RING

    entries = near_list.reshape(-1)
    inner = entries[None, :] - (jnp.arange(members) * leaf_count)[:, None]
    wanted = (inner >= 0) & (inner < leaf_count)
    requests = jnp.sum(jnp.where(wanted, inner + 1, 0), axis=1)

    terms, tails = lift(charges, leaf_basis, transfer, parent, requests, width)
    terms = exchange(terms)
    asked = terms[:, columns, 0].astype(F32).astype(jnp.int32)

    own_weight = jnp.sum(terms[:, :columns].astype(F32), axis=0).astype(BF)
    weights = exchange(spread(own_weight))
    pieces, rows = leaf_count * QUARTERS, leaf_size // QUARTERS
    plans = [[], [], []]
    for axis, way in DIRECTIONS:
        h = axis * (QUARTERS // 2)
        plans[0].append(
            [(offset(axis, 2, 0), 2 * way, 2)]
            + [(offset(axis, 2, across), h + way, 1) for across in (1, 3, 2)]
        )
        plans[1].append([(offset(axis, one(way), across), h, 2) for across in (1, 3, 2)])
        plans[2].append([(offset(axis, one(way), 0), 0, QUARTERS)])
    blocks = collect(
        points.reshape(pieces, rows, width),
        tails,
        after(asked, own_weight),
        jnp.stack([y, z]).astype(jnp.int32),
        plans[0] + plans[1] + plans[2],
    )
    count = len(DIRECTIONS)

    def send(wait, values):
        return [step(v, d) for v, d in zip(held(wait, values), DIRECTIONS)]

    def held(wait, values):
        first = [after(values[0], *wait[0], *wait[1:])]
        return first + [after(v, w, *wait[1:]) for v, w in zip(values[1:], wait[0][1:])]

    chips = groups // 2

    def along_x(k, block, *gate):
        pairs = [(i, (i + 2 * k) % groups) for i in range(groups)]
        return lax.ppermute(after(block, *gate), "grp", pairs)

    def own_part(first, last, gate, *before):
        return own(after(points, *gate), charges, range(first, last), leaf_size, gamma, before)

    blocks = [after(block, weights) for block in blocks]
    cut_1, cut_2 = leaf_count - 2, leaf_count - 1
    got_1 = [step(v, d) for v, d in zip(blocks[:count], DIRECTIONS)]
    x_1 = along_x(1, weights, *blocks[:count])
    total, norms = own_part(0, cut_1, blocks[:count])
    got_2 = send((got_1, total, x_1), blocks[count : 2 * count])
    x_2 = along_x(2, weights, *got_1)
    total, norms = own_part(cut_1, cut_2, got_1, total, norms)
    x_3 = along_x(3, weights, total)
    got_3 = send((got_2, total, x_2, x_3), got_1)
    mine = jnp.concatenate([weights, x_1, x_2, x_3], axis=0)
    swap = [(i, i ^ 1) for i in range(groups)]
    other = lax.ppermute(after(mine, *got_2), "grp", swap)
    total, norms = own_part(cut_2, leaf_count, got_2, total, norms)
    far_ids = coarse_far[0]
    far_alive = (far_ids >= 0).astype(F32)
    ids = jnp.maximum(far_ids, 0)
    group = lax.axis_index("grp")
    from_group, node = ids // members, ids % members
    side = (from_group % 2) != (group % 2)
    at = (group // 2 - from_group // 2) % chips * members
    at = at + node
    sources = jnp.where(side[:, None, None], other[at], mine[at])
    far_terms = lax.dot_general(
        sources, coarse_coupling[0], (((2,), (1,)), ((0,), (0,))), preferred_element_type=F32
    )
    field = jnp.sum(far_terms * far_alive[:, None, None], axis=0).astype(BF)
    fields = exchange(spread(after(field, *got_3)))
    got_4 = send((got_3, total, field), blocks[2 * count :])
    plan_5, plan_6 = [], []
    for axis, way in DIRECTIONS:
        first = 2 * (1 - axis)
        plan_5.append(
            [(first, 4 + way, 1), (first + 1, 4 + way, 1), (4 + first + way, 4, 1)]
        )
        plan_6.append(
            [(first, 2 * way, 2), (first + 1, 2 * way, 2)]
            + [(4 + first, 2 + way, 1), (4 + first + 1, 2 + way, 1)]
        )
    woven = weave([*got_2, *got_3], plan_5 + plan_6)
    got_5 = send((got_4, *woven, fields), woven[:count])
    got_6 = send((got_5, fields), woven[count:])
    add = functools.partial(near, leaf_size=leaf_size, gamma=gamma)
    groups_4, groups_6, groups_7 = [], [], []
    for d, (axis, way) in enumerate(DIRECTIONS):
        groups_4.append(([(count + d, 0), (count + d, 1)], number(offset(axis, 2, 0))))
        for k in range(0, QUARTERS, 2):
            groups_4.append(([(d, k), (d, k + 1)], number(offset(axis, one(way), 0))))
        for k, along in enumerate((1, 3, 2)):
            pair = [(d, 2 * k), (d, 2 * k + 1)]
            groups_6.append((pair, number(offset(1 - axis, along, one(way)))))
            if way == 0:
                groups_7.append(([(d, k), (d + 1, k)], number(offset(1 - axis, along, 2))))
    flat = near_list.reshape(-1)
    owner = jnp.where(flat >= 0, flat // leaf_count, 0)
    back = (y - owner // RING) % RING * RING + (z - owner % RING) % RING
    leaves = jnp.arange(flat.shape[0]) // near_count + 1
    match = (back[None, :] == jnp.arange(members)[:, None]) & (flat >= 0)[None, :]
    target = jnp.sum(jnp.where(match, leaves[None, :], 0), axis=1) - 1
    total = add([*got_4, *got_3], groups_4, target, points, norms, after(total, *got_5))
    total = finish(fields, parent, transfer, leaf_basis, total)
    got_7 = send((got_6, total), got_5)
    total = add(got_6, groups_6, target, points, norms, total)
    return add(got_7, groups_7, target, points, norms, total)


def solution(mesh):
    placed = (
        P(("grp", "sub"), None),
        P(None, ("grp", "sub")),
        P(("grp", "sub"), None),
        P(("grp", "sub"), None, None),
        P(("grp", "sub"), None, None),
        P(("grp", "sub")),
        P(("grp", "sub"), None),
        P(("grp", "sub"), None, None, None),
    )
    return jax.shard_map(
        local, mesh=mesh, in_specs=placed, out_specs=P(None, ("grp", "sub")), check_vma=False
    )
```

```python
import functools

import jax
import jax.numpy as jnp
from jax import lax
from jax.experimental import pallas as pl
from jax.experimental.pallas import tpu as pltpu
from jax.sharding import PartitionSpec as P

BF = jnp.bfloat16
F32 = jnp.float32
LOG2E = 1.4426950408889634
TILE_ROWS = 16
TILE_LANES = 128
RING = 4
QUARTERS = 4
DIRECTIONS = [(axis, way) for axis in range(2) for way in range(2)]
NT = (((1,), (1,)), ((), ()))
MIB = 1024 * 1024


def params(size):
    return pltpu.CompilerParams(vmem_limit_bytes=size * MIB)


def offset(axis, along, across):
    return (along, across) if axis == 0 else (across, along)


def number(steps):
    return steps[0] * RING + steps[1]


def one(way):
    return 1 if way == 0 else RING - 1


def step(block, direction):
    return turn(block, *offset(direction[0], one(direction[1]), 0))


def turn(block, y, z):
    pairs = [
        (d, (d // RING + y) % RING * RING + (d % RING + z) % RING) for d in range(RING * RING)
    ]
    return lax.ppermute(block, "sub", pairs)


def collect(points, tails, asked, place, plans):
    pieces, rows, width = points.shape
    extra = tails.shape[1]
    sizes = [sum(run[2] for run in plan) for plan in plans]
    runs = []
    for number, plan in enumerate(plans):
        at = 0
        for steps, quarter, length in plan:
            runs.append((number, at, steps, quarter, length))
            at += length

    def body(asked, place, points, tails, *rest):
        outs, sems = rest[:-1], rest[-1]

        def wanted(steps):
            y = (place[0] + steps[0]) % RING
            z = (place[1] + steps[1]) % RING
            return asked[y * RING + z]

        def copies(k):
            number, at, steps, quarter, length = runs[k]
            first = jnp.maximum(wanted(steps) - 1, 0) * QUARTERS + quarter
            return (
                pltpu.make_async_copy(
                    points.at[pl.ds(first, length)],
                    outs[number].at[pl.ds(at, length), pl.ds(0, rows)],
                    sems.at[k, 0],
                ),
                pltpu.make_async_copy(
                    tails.at[pl.ds(first, length)],
                    outs[number].at[pl.ds(at, length), pl.ds(rows, extra)],
                    sems.at[k, 1],
                ),
            )

        for k in range(len(runs)):

            @pl.when(wanted(runs[k][2]) > 0)
            def _(k=k):
                for copy in copies(k):
                    copy.start()

        for k in range(len(runs)):

            @pl.when(wanted(runs[k][2]) > 0)
            def _(k=k):
                for copy in copies(k):
                    copy.wait()

    scalar = pl.BlockSpec(memory_space=pltpu.SMEM)
    return pl.pallas_call(
        body,
        in_specs=[scalar, scalar] + [pl.BlockSpec(memory_space=pltpu.VMEM)] * 2,
        out_specs=[pl.BlockSpec(memory_space=pltpu.HBM)] * len(plans),
        out_shape=[jax.ShapeDtypeStruct((n, rows + extra, width), BF) for n in sizes],
        scratch_shapes=[pltpu.SemaphoreType.DMA((len(runs), 2))],
        compiler_params=params(63),
        cost_estimate=pl.CostEstimate(
            flops=0, bytes_accessed=sum(sizes) * rows * width * 4, transcendentals=0
        ),
        name="collect",
    )(asked, place, points, tails)


def weave(sources, plans):
    shape = sources[0].shape[1:]
    sizes = [sum(run[2] for run in plan) for plan in plans]
    runs = []
    for place, plan in enumerate(plans):
        at = 0
        for source, first, length in plan:
            runs.append((source, first, length, place, at, sum(sizes[:place]) + at))
            at += length

    def body(*refs):
        ins = refs[: len(sources)]
        outs = refs[len(sources) : -3]
        held, loads, stores = refs[-3:]
        first_leg, second_leg = [], []
        for k, (source, first, length, place, at, row) in enumerate(runs):
            staged = held.at[pl.ds(row, length)]
            first_leg.append(
                pltpu.make_async_copy(
                    ins[source].at[pl.ds(first, length)], staged, loads.at[k]
                )
            )
            second_leg.append(
                pltpu.make_async_copy(staged, outs[place].at[pl.ds(at, length)], stores.at[k])
            )
        for copy in first_leg:
            copy.start()
        for load, store in zip(first_leg, second_leg):
            load.wait()
            store.start()
        for copy in second_leg:
            copy.wait()

    return pl.pallas_call(
        body,
        in_specs=[pl.BlockSpec(memory_space=pl.ANY)] * len(sources),
        out_specs=[pl.BlockSpec(memory_space=pltpu.HBM)] * len(plans),
        out_shape=[jax.ShapeDtypeStruct((size, *shape), BF) for size in sizes],
        scratch_shapes=[
            pltpu.VMEM((sum(sizes), *shape), BF),
            pltpu.SemaphoreType.DMA((len(runs),)),
            pltpu.SemaphoreType.DMA((len(runs),)),
        ],
        compiler_params=params(63),
        cost_estimate=pl.CostEstimate(
            flops=0,
            bytes_accessed=4 * sum(sizes) * shape[0] * shape[1],
            transcendentals=0,
        ),
        name="weave",
    )(*sources)


def lift(charges, leaf_basis, transfer, slots, requests, width):
    leaf_count, leaf_size, rank = leaf_basis.shape
    columns = charges.shape[0]
    lines, rows = columns // TILE_ROWS, leaf_size // QUARTERS
    members = requests.shape[0]

    def body(slots, requests, charges, basis, transfer, out, tails, sums):
        t = pl.program_id(0)
        tails[...] = jnp.zeros_like(tails)
        for q in range(QUARTERS):
            for g in range(lines):
                tails[q, :, g * rows : (g + 1) * rows] = charges[
                    g * TILE_ROWS : (g + 1) * TILE_ROWS, q * rows : (q + 1) * rows
                ]

        @pl.when(t == 0)
        def _():
            sums[...] = jnp.zeros_like(sums)

        skeleton = jnp.dot(charges[...], basis[0], preferred_element_type=F32).astype(BF)
        sums[slots[t]] += jnp.dot(skeleton, transfer[0], preferred_element_type=F32)

        @pl.when(t == leaf_count - 1)
        def _():
            out[:, 0:columns, :] = sums[...].astype(BF)
            for d in range(members):
                value = requests[d].astype(F32)
                out[d, columns:, :] = jnp.full((TILE_ROWS, rank), value, F32).astype(BF)

    return pl.pallas_call(
        body,
        grid_spec=pltpu.PrefetchScalarGridSpec(
            num_scalar_prefetch=2,
            grid=(leaf_count,),
            in_specs=[
                pl.BlockSpec((columns, leaf_size), lambda t, s, r: (0, t)),
                pl.BlockSpec((1, leaf_size, rank), lambda t, s, r: (t, 0, 0)),
                pl.BlockSpec((1, rank, rank), lambda t, s, r: (t, 0, 0)),
            ],
            out_specs=[
                pl.BlockSpec((members, columns + TILE_ROWS, rank), lambda t, s, r: (0, 0, 0)),
                pl.BlockSpec((QUARTERS, TILE_ROWS, width), lambda t, s, r: (t, 0, 0)),
            ],
            scratch_shapes=[pltpu.VMEM((members, columns, rank), F32)],
        ),
        out_shape=[
            jax.ShapeDtypeStruct((members, columns + TILE_ROWS, rank), BF),
            jax.ShapeDtypeStruct((leaf_count * QUARTERS, TILE_ROWS, width), BF),
        ],
        compiler_params=params(63),
        name="lift",
    )(slots, requests, charges, leaf_basis, transfer)


def finish(fields, slots, transfer, leaf_basis, total):
    leaf_count, leaf_size, rank = leaf_basis.shape
    columns = total.shape[0]

    def body(slots, field, transfer, basis, total, out):
        descended = lax.dot_general(
            field[0], transfer[0], NT, preferred_element_type=F32
        ).astype(BF)
        out[...] = total[...] + lax.dot_general(
            descended, basis[0], NT, preferred_element_type=F32
        )

    return pl.pallas_call(
        body,
        grid_spec=pltpu.PrefetchScalarGridSpec(
            num_scalar_prefetch=1,
            grid=(leaf_count,),
            in_specs=[
                pl.BlockSpec((1, columns, rank), lambda t, s: (s[t], 0, 0)),
                pl.BlockSpec((1, rank, rank), lambda t, s: (t, 0, 0)),
                pl.BlockSpec((1, leaf_size, rank), lambda t, s: (t, 0, 0)),
                pl.BlockSpec((columns, leaf_size), lambda t, s: (0, t)),
            ],
            out_specs=pl.BlockSpec((columns, leaf_size), lambda t, s: (0, t)),
        ),
        out_shape=jax.ShapeDtypeStruct(total.shape, F32),
        compiler_params=params(8),
        name="finish",
    )(slots, fields, transfer, leaf_basis, total)


def gauss(source, source_norms, target, target_norms, scale):
    gram = lax.dot_general(source, target, NT, preferred_element_type=F32)
    return jnp.exp2((2.0 * scale) * gram - (source_norms + target_norms)).astype(BF)


def own_body(scale, leaf_size, first, second, ti, sj, ci, cj, *rest):
    before, (out, rows, col) = rest[:-3], rest[-3:]
    step = pl.program_id(0)
    width = ti.shape[1]
    i0 = pl.multiple_of(first[step] * leaf_size, leaf_size)
    j0 = pl.multiple_of(second[step] * leaf_size, leaf_size)
    ones = jnp.ones((8, width), BF)
    lanes = jnp.ones((width, TILE_LANES), BF)

    @pl.when(step == 0)
    def _():
        if before:
            out[...] = before[0][...]
            rows[...] = before[1][...]
        else:
            out[...] = jnp.zeros_like(out)
            rows[...] = jnp.zeros_like(rows)

    @pl.when(i0 == j0)
    def _():
        wide = sj[...].astype(F32)
        square = wide * wide
        high = square.astype(BF)
        low = (square - high.astype(F32)).astype(BF)
        row = lax.dot_general(ones, high, NT, preferred_element_type=F32) + lax.dot_general(
            ones, low, NT, preferred_element_type=F32
        )
        rows[:, pl.ds(i0, leaf_size)] = scale * row
        column = jnp.dot(high, lanes, preferred_element_type=F32) + jnp.dot(
            low, lanes, preferred_element_type=F32
        )
        col[pl.ds(i0, leaf_size), :] = scale * column

    gram = lax.dot_general(sj[...], ti[...], NT, preferred_element_type=F32)
    norms = col[pl.ds(j0, leaf_size), :][:, :1] + rows[0:1, pl.ds(i0, leaf_size)]
    kernel = jnp.exp2((2.0 * scale) * gram - norms).astype(BF)
    out[:, pl.ds(i0, leaf_size)] += jnp.dot(cj[...], kernel, preferred_element_type=F32)

    @pl.when(i0 != j0)
    def _():
        out[:, pl.ds(j0, leaf_size)] += lax.dot_general(
            ci[...], kernel, NT, preferred_element_type=F32
        )


def own(points, charges, columns_of, leaf_size, gamma, before=()):
    width = points.shape[1]
    columns = charges.shape[0]
    total = points.shape[0]
    pairs = [(i, j) for j in columns_of for i in range(j, -1, -1)]
    first = jnp.array([p[0] for p in pairs], jnp.int32)
    second = jnp.array([p[1] for p in pairs], jnp.int32)
    return pl.pallas_call(
        functools.partial(own_body, gamma * LOG2E, leaf_size),
        grid_spec=pltpu.PrefetchScalarGridSpec(
            num_scalar_prefetch=2,
            grid=(len(pairs),),
            in_specs=[
                pl.BlockSpec((leaf_size, width), lambda s, a, b: (a[s], 0)),
                pl.BlockSpec((leaf_size, width), lambda s, a, b: (b[s], 0)),
                pl.BlockSpec((columns, leaf_size), lambda s, a, b: (0, a[s])),
                pl.BlockSpec((columns, leaf_size), lambda s, a, b: (0, b[s])),
            ]
            + [pl.BlockSpec(b.shape, lambda s, a, b: (0, 0)) for b in before],
            out_specs=[
                pl.BlockSpec((columns, total), lambda s, a, b: (0, 0)),
                pl.BlockSpec((8, total), lambda s, a, b: (0, 0)),
            ],
            scratch_shapes=[pltpu.VMEM((total, TILE_LANES), F32)],
        ),
        out_shape=[
            jax.ShapeDtypeStruct((columns, total), F32),
            jax.ShapeDtypeStruct((8, total), F32),
        ],
        compiler_params=params(63),
        cost_estimate=pl.CostEstimate(
            flops=2 * len(pairs) * leaf_size * leaf_size * (width + 2 * columns),
            bytes_accessed=total * width * 8,
            transcendentals=len(pairs) * leaf_size * leaf_size,
        ),
        name="own",
    )(first, second, points, points, charges, charges, *before)


def near_body(scale, groups, leaf_size, target, points, norms, before, *refs):
    buffers, out = refs[:-1], refs[-1]
    columns = before.shape[0]
    rows = buffers[0].shape[1] - TILE_ROWS
    out[...] = before[...]
    for units, source_steps in groups:
        leaf = target[source_steps]

        @pl.when(leaf >= 0)
        def _(units=units, leaf=leaf):
            source = jnp.concatenate([buffers[b][u, 0:rows, :] for b, u in units], axis=0)
            charges = jnp.concatenate(
                [
                    jnp.concatenate(
                        [
                            buffers[b][u, rows:, g * TILE_LANES : (g + 1) * TILE_LANES]
                            for g in range(columns // TILE_ROWS)
                        ],
                        axis=0,
                    )
                    for b, u in units
                ],
                axis=1,
            )
            wide = source.astype(F32)
            source_norms = scale * jnp.sum(wide * wide, axis=1, keepdims=True)
            start = pl.multiple_of(leaf * leaf_size, leaf_size)
            kernel = gauss(
                source,
                source_norms,
                points[pl.ds(start, leaf_size), :],
                norms[0:1, pl.ds(start, leaf_size)],
                scale,
            )
            out[:, pl.ds(start, leaf_size)] += jnp.dot(
                charges, kernel, preferred_element_type=F32
            )


def near(buffers, groups, target, points, norms, before, leaf_size, gamma):
    width = points.shape[1]
    columns = before.shape[0]
    rows = sum(len(units) for units, _ in groups) * TILE_LANES
    whole = pl.BlockSpec(memory_space=pltpu.VMEM)
    return pl.pallas_call(
        functools.partial(near_body, gamma * LOG2E, groups, leaf_size),
        in_specs=[pl.BlockSpec(memory_space=pltpu.SMEM)] + [whole] * (3 + len(buffers)),
        out_specs=whole,
        out_shape=jax.ShapeDtypeStruct(before.shape, F32),
        compiler_params=params(20),
        cost_estimate=pl.CostEstimate(
            flops=2 * rows * leaf_size * (width + columns),
            bytes_accessed=rows * width * 2 + points.size * 2,
            transcendentals=rows * leaf_size,
        ),
        name="near",
    )(target, points, norms, before, *buffers)


def after(value, *others):
    return lax.optimization_barrier((value, *others))[0]


def local(points, charges, near_list, leaf_basis, transfer, parent, coarse_far, coarse_coupling):
    leaf_count, leaf_size, rank = leaf_basis.shape
    width = points.shape[1]
    columns = charges.shape[0]
    near_count = near_list.shape[1]
    members = lax.axis_size("sub")
    groups = lax.axis_size("grp")
    gamma = 2.0 / width

    def exchange(block):
        return lax.all_to_all(block, "sub", split_axis=0, concat_axis=0, tiled=True)

    def spread(block):
        return jnp.broadcast_to(block[None], (members, *block.shape))

    here = lax.axis_index("sub")
    y, z = here // RING, here % RING

    entries = near_list.reshape(-1)
    inner = entries[None, :] - (jnp.arange(members) * leaf_count)[:, None]
    wanted = (inner >= 0) & (inner < leaf_count)
    requests = jnp.sum(jnp.where(wanted, inner + 1, 0), axis=1)

    terms, tails = lift(charges, leaf_basis, transfer, parent, requests, width)
    terms = exchange(terms)
    asked = terms[:, columns, 0].astype(F32).astype(jnp.int32)

    own_weight = jnp.sum(terms[:, :columns].astype(F32), axis=0).astype(BF)
    weights = exchange(spread(own_weight))
    pieces, rows = leaf_count * QUARTERS, leaf_size // QUARTERS
    plans = [[], [], []]
    for axis, way in DIRECTIONS:
        h = axis * (QUARTERS // 2)
        plans[0].append(
            [(offset(axis, 2, 0), 2 * way, 2)]
            + [(offset(axis, 2, across), h + way, 1) for across in (1, 3, 2)]
        )
        plans[1].append([(offset(axis, one(way), across), h, 2) for across in (1, 3, 2)])
        plans[2].append([(offset(axis, one(way), 0), 0, QUARTERS)])
    blocks = collect(
        points.reshape(pieces, rows, width),
        tails,
        after(asked, own_weight),
        jnp.stack([y, z]).astype(jnp.int32),
        plans[0] + plans[1] + plans[2],
    )
    count = len(DIRECTIONS)

    def send(wait, values):
        return [step(v, d) for v, d in zip(held(wait, values), DIRECTIONS)]

    def held(wait, values):
        first = [after(values[0], *wait[0], *wait[1:])]
        return first + [after(v, w, *wait[1:]) for v, w in zip(values[1:], wait[0][1:])]

    chips = groups // 2

    def along_x(k, block, *gate):
        pairs = [(i, (i + 2 * k) % groups) for i in range(groups)]
        return lax.ppermute(after(block, *gate), "grp", pairs)

    def own_part(first, last, gate, *before):
        return own(after(points, *gate), charges, range(first, last), leaf_size, gamma, before)

    blocks = [after(block, weights) for block in blocks]
    cut = leaf_count * 2 // 3
    got_1 = [step(v, d) for v, d in zip(blocks[:count], DIRECTIONS)]
    x_1 = along_x(1, weights, *blocks[:count])
    total, norms = own_part(0, cut, blocks[:count])
    got_2 = send((got_1, total, x_1), blocks[count : 2 * count])
    x_2 = along_x(2, weights, *got_1)
    total, norms = own_part(cut, leaf_count, got_1, total, norms)
    got_3 = send((got_2, total, x_2), got_1)
    x_3 = along_x(3, weights, *got_2, total)
    mine = jnp.concatenate([weights, x_1, x_2, x_3], axis=0)
    got_4 = send((got_3, x_3), blocks[2 * count :])
    swap = [(i, i ^ 1) for i in range(groups)]
    other = lax.ppermute(after(mine, *got_3), "grp", swap)
    plan_5, plan_6 = [], []
    for axis, way in DIRECTIONS:
        first = 2 * (1 - axis)
        plan_5.append(
            [(first, 4 + way, 1), (first + 1, 4 + way, 1), (4 + first + way, 4, 1)]
        )
        plan_6.append(
            [(first, 2 * way, 2), (first + 1, 2 * way, 2)]
            + [(4 + first, 2 + way, 1), (4 + first + 1, 2 + way, 1)]
        )
    woven = weave([*got_2, *got_3], plan_5 + plan_6)
    far_ids = coarse_far[0]
    far_alive = (far_ids >= 0).astype(F32)
    ids = jnp.maximum(far_ids, 0)
    group = lax.axis_index("grp")
    from_group, node = ids // members, ids % members
    side = (from_group % 2) != (group % 2)
    at = (group // 2 - from_group // 2) % chips * members
    at = at + node
    sources = jnp.where(side[:, None, None], other[at], mine[at])
    far_terms = lax.dot_general(
        sources, coarse_coupling[0], (((2,), (1,)), ((0,), (0,))), preferred_element_type=F32
    )
    field = jnp.sum(far_terms * far_alive[:, None, None], axis=0).astype(BF)
    fields = exchange(spread(after(field, woven[0])))
    got_5 = send((got_4, *woven, fields), woven[:count])
    got_6 = send((got_5, fields), woven[count:])
    add = functools.partial(near, leaf_size=leaf_size, gamma=gamma)
    groups_4, groups_6, groups_7 = [], [], []
    for d, (axis, way) in enumerate(DIRECTIONS):
        groups_4.append(([(count + d, 0), (count + d, 1)], number(offset(axis, 2, 0))))
        for k in range(0, QUARTERS, 2):
            groups_4.append(([(d, k), (d, k + 1)], number(offset(axis, one(way), 0))))
        for k, along in enumerate((1, 3, 2)):
            pair = [(d, 2 * k), (d, 2 * k + 1)]
            groups_6.append((pair, number(offset(1 - axis, along, one(way)))))
            if way == 0:
                groups_7.append(([(d, k), (d + 1, k)], number(offset(1 - axis, along, 2))))
    flat = near_list.reshape(-1)
    owner = jnp.where(flat >= 0, flat // leaf_count, 0)
    back = (y - owner // RING) % RING * RING + (z - owner % RING) % RING
    leaves = jnp.arange(flat.shape[0]) // near_count + 1
    match = (back[None, :] == jnp.arange(members)[:, None]) & (flat >= 0)[None, :]
    target = jnp.sum(jnp.where(match, leaves[None, :], 0), axis=1) - 1
    total = add([*got_4, *got_3], groups_4, target, points, norms, after(total, *got_5))
    total = finish(fields, parent, transfer, leaf_basis, total)
    got_7 = send((got_6, total), got_5)
    total = add(got_6, groups_6, target, points, norms, total)
    return add(got_7, groups_7, target, points, norms, total)


def solution(mesh):
    placed = (
        P(("grp", "sub"), None),
        P(None, ("grp", "sub")),
        P(("grp", "sub"), None),
        P(("grp", "sub"), None, None),
        P(("grp", "sub"), None, None),
        P(("grp", "sub")),
        P(("grp", "sub"), None),
        P(("grp", "sub"), None, None, None),
    )
    return jax.shard_map(
        local, mesh=mesh, in_specs=placed, out_specs=P(None, ("grp", "sub")), check_vma=False
    )
```

```python
import functools

import jax
import jax.numpy as jnp
from jax import lax
from jax.experimental import pallas as pl
from jax.experimental.pallas import tpu as pltpu
from jax.sharding import PartitionSpec as P

BF = jnp.bfloat16
F32 = jnp.float32
LOG2E = 1.4426950408889634
TILE_ROWS = 16
TILE_LANES = 128
RING = 4
QUARTERS = 4
DIRECTIONS = [(axis, way) for axis in range(2) for way in range(2)]
NT = (((1,), (1,)), ((), ()))
MIB = 1024 * 1024


def params(size):
    return pltpu.CompilerParams(vmem_limit_bytes=size * MIB)


def offset(axis, along, across):
    return (along, across) if axis == 0 else (across, along)


def number(steps):
    return steps[0] * RING + steps[1]


def one(way):
    return 1 if way == 0 else RING - 1


def step(block, direction):
    return turn(block, *offset(direction[0], one(direction[1]), 0))


def turn(block, y, z):
    pairs = [
        (d, (d // RING + y) % RING * RING + (d % RING + z) % RING) for d in range(RING * RING)
    ]
    return lax.ppermute(block, "sub", pairs)


def collect(points, tails, asked, place, plans):
    pieces, rows, width = points.shape
    extra = tails.shape[1]
    sizes = [sum(run[2] for run in plan) for plan in plans]
    runs = []
    for number, plan in enumerate(plans):
        at = 0
        for steps, quarter, length in plan:
            runs.append((number, at, steps, quarter, length))
            at += length

    def body(asked, place, points, tails, *rest):
        outs, sems = rest[:-1], rest[-1]

        def wanted(steps):
            y = (place[0] + steps[0]) % RING
            z = (place[1] + steps[1]) % RING
            return asked[y * RING + z]

        def copies(k):
            number, at, steps, quarter, length = runs[k]
            first = jnp.maximum(wanted(steps) - 1, 0) * QUARTERS + quarter
            return (
                pltpu.make_async_copy(
                    points.at[pl.ds(first, length)],
                    outs[number].at[pl.ds(at, length), pl.ds(0, rows)],
                    sems.at[k, 0],
                ),
                pltpu.make_async_copy(
                    tails.at[pl.ds(first, length)],
                    outs[number].at[pl.ds(at, length), pl.ds(rows, extra)],
                    sems.at[k, 1],
                ),
            )

        for k in range(len(runs)):

            @pl.when(wanted(runs[k][2]) > 0)
            def _(k=k):
                for copy in copies(k):
                    copy.start()

        for k in range(len(runs)):

            @pl.when(wanted(runs[k][2]) > 0)
            def _(k=k):
                for copy in copies(k):
                    copy.wait()

    scalar = pl.BlockSpec(memory_space=pltpu.SMEM)
    return pl.pallas_call(
        body,
        in_specs=[scalar, scalar] + [pl.BlockSpec(memory_space=pltpu.VMEM)] * 2,
        out_specs=[pl.BlockSpec(memory_space=pltpu.HBM)] * len(plans),
        out_shape=[jax.ShapeDtypeStruct((n, rows + extra, width), BF) for n in sizes],
        scratch_shapes=[pltpu.SemaphoreType.DMA((len(runs), 2))],
        compiler_params=params(63),
        cost_estimate=pl.CostEstimate(
            flops=0, bytes_accessed=sum(sizes) * rows * width * 4, transcendentals=0
        ),
        name="collect",
    )(asked, place, points, tails)


def weave(sources, plans):
    shape = sources[0].shape[1:]
    sizes = [sum(run[2] for run in plan) for plan in plans]
    runs = []
    for place, plan in enumerate(plans):
        at = 0
        for source, first, length in plan:
            runs.append((source, first, length, place, at, sum(sizes[:place]) + at))
            at += length

    def body(*refs):
        ins = refs[: len(sources)]
        outs = refs[len(sources) : -3]
        held, loads, stores = refs[-3:]
        first_leg, second_leg = [], []
        for k, (source, first, length, place, at, row) in enumerate(runs):
            staged = held.at[pl.ds(row, length)]
            first_leg.append(
                pltpu.make_async_copy(
                    ins[source].at[pl.ds(first, length)], staged, loads.at[k]
                )
            )
            second_leg.append(
                pltpu.make_async_copy(staged, outs[place].at[pl.ds(at, length)], stores.at[k])
            )
        for copy in first_leg:
            copy.start()
        for load, store in zip(first_leg, second_leg):
            load.wait()
            store.start()
        for copy in second_leg:
            copy.wait()

    return pl.pallas_call(
        body,
        in_specs=[pl.BlockSpec(memory_space=pl.ANY)] * len(sources),
        out_specs=[pl.BlockSpec(memory_space=pltpu.HBM)] * len(plans),
        out_shape=[jax.ShapeDtypeStruct((size, *shape), BF) for size in sizes],
        scratch_shapes=[
            pltpu.VMEM((sum(sizes), *shape), BF),
            pltpu.SemaphoreType.DMA((len(runs),)),
            pltpu.SemaphoreType.DMA((len(runs),)),
        ],
        compiler_params=params(63),
        cost_estimate=pl.CostEstimate(
            flops=0,
            bytes_accessed=4 * sum(sizes) * shape[0] * shape[1],
            transcendentals=0,
        ),
        name="weave",
    )(*sources)


def lift(charges, leaf_basis, transfer, slots, requests, width):
    leaf_count, leaf_size, rank = leaf_basis.shape
    columns = charges.shape[0]
    lines, rows = columns // TILE_ROWS, leaf_size // QUARTERS
    members = requests.shape[0]

    def body(slots, requests, charges, basis, transfer, out, tails, sums):
        t = pl.program_id(0)
        tails[...] = jnp.zeros_like(tails)
        for q in range(QUARTERS):
            for g in range(lines):
                tails[q, :, g * rows : (g + 1) * rows] = charges[
                    g * TILE_ROWS : (g + 1) * TILE_ROWS, q * rows : (q + 1) * rows
                ]

        @pl.when(t == 0)
        def _():
            sums[...] = jnp.zeros_like(sums)

        skeleton = jnp.dot(charges[...], basis[0], preferred_element_type=F32).astype(BF)
        sums[slots[t]] += jnp.dot(skeleton, transfer[0], preferred_element_type=F32)

        @pl.when(t == leaf_count - 1)
        def _():
            out[:, 0:columns, :] = sums[...].astype(BF)
            for d in range(members):
                value = requests[d].astype(F32)
                out[d, columns:, :] = jnp.full((TILE_ROWS, rank), value, F32).astype(BF)

    return pl.pallas_call(
        body,
        grid_spec=pltpu.PrefetchScalarGridSpec(
            num_scalar_prefetch=2,
            grid=(leaf_count,),
            in_specs=[
                pl.BlockSpec((columns, leaf_size), lambda t, s, r: (0, t)),
                pl.BlockSpec((1, leaf_size, rank), lambda t, s, r: (t, 0, 0)),
                pl.BlockSpec((1, rank, rank), lambda t, s, r: (t, 0, 0)),
            ],
            out_specs=[
                pl.BlockSpec((members, columns + TILE_ROWS, rank), lambda t, s, r: (0, 0, 0)),
                pl.BlockSpec((QUARTERS, TILE_ROWS, width), lambda t, s, r: (t, 0, 0)),
            ],
            scratch_shapes=[pltpu.VMEM((members, columns, rank), F32)],
        ),
        out_shape=[
            jax.ShapeDtypeStruct((members, columns + TILE_ROWS, rank), BF),
            jax.ShapeDtypeStruct((leaf_count * QUARTERS, TILE_ROWS, width), BF),
        ],
        compiler_params=params(63),
        name="lift",
    )(slots, requests, charges, leaf_basis, transfer)


def finish(fields, slots, transfer, leaf_basis, total):
    leaf_count, leaf_size, rank = leaf_basis.shape
    columns = total.shape[0]

    def body(slots, field, transfer, basis, total, out):
        descended = lax.dot_general(
            field[0], transfer[0], NT, preferred_element_type=F32
        ).astype(BF)
        out[...] = total[...] + lax.dot_general(
            descended, basis[0], NT, preferred_element_type=F32
        )

    return pl.pallas_call(
        body,
        grid_spec=pltpu.PrefetchScalarGridSpec(
            num_scalar_prefetch=1,
            grid=(leaf_count,),
            in_specs=[
                pl.BlockSpec((1, columns, rank), lambda t, s: (s[t], 0, 0)),
                pl.BlockSpec((1, rank, rank), lambda t, s: (t, 0, 0)),
                pl.BlockSpec((1, leaf_size, rank), lambda t, s: (t, 0, 0)),
                pl.BlockSpec((columns, leaf_size), lambda t, s: (0, t)),
            ],
            out_specs=pl.BlockSpec((columns, leaf_size), lambda t, s: (0, t)),
        ),
        out_shape=jax.ShapeDtypeStruct(total.shape, F32),
        compiler_params=params(8),
        name="finish",
    )(slots, fields, transfer, leaf_basis, total)


def gauss(source, source_norms, target, target_norms, scale):
    gram = lax.dot_general(source, target, NT, preferred_element_type=F32)
    return jnp.exp2((2.0 * scale) * gram - (source_norms + target_norms)).astype(BF)


def own_body(scale, leaf_size, first, second, ti, sj, ci, cj, *rest):
    before, (out, rows, col) = rest[:-3], rest[-3:]
    step = pl.program_id(0)
    width = ti.shape[1]
    i0 = pl.multiple_of(first[step] * leaf_size, leaf_size)
    j0 = pl.multiple_of(second[step] * leaf_size, leaf_size)
    ones = jnp.ones((8, width), BF)
    lanes = jnp.ones((width, TILE_LANES), BF)

    @pl.when(step == 0)
    def _():
        if before:
            out[...] = before[0][...]
            rows[...] = before[1][...]
        else:
            out[...] = jnp.zeros_like(out)
            rows[...] = jnp.zeros_like(rows)

    @pl.when(i0 == j0)
    def _():
        wide = sj[...].astype(F32)
        square = wide * wide
        high = square.astype(BF)
        low = (square - high.astype(F32)).astype(BF)
        row = lax.dot_general(ones, high, NT, preferred_element_type=F32) + lax.dot_general(
            ones, low, NT, preferred_element_type=F32
        )
        rows[:, pl.ds(i0, leaf_size)] = scale * row
        column = jnp.dot(high, lanes, preferred_element_type=F32) + jnp.dot(
            low, lanes, preferred_element_type=F32
        )
        col[pl.ds(i0, leaf_size), :] = scale * column

    gram = lax.dot_general(sj[...], ti[...], NT, preferred_element_type=F32)
    norms = col[pl.ds(j0, leaf_size), :][:, :1] + rows[0:1, pl.ds(i0, leaf_size)]
    kernel = jnp.exp2((2.0 * scale) * gram - norms).astype(BF)
    out[:, pl.ds(i0, leaf_size)] += jnp.dot(cj[...], kernel, preferred_element_type=F32)

    @pl.when(i0 != j0)
    def _():
        out[:, pl.ds(j0, leaf_size)] += lax.dot_general(
            ci[...], kernel, NT, preferred_element_type=F32
        )


def own(points, charges, columns_of, leaf_size, gamma, before=()):
    width = points.shape[1]
    columns = charges.shape[0]
    total = points.shape[0]
    pairs = [(i, j) for j in columns_of for i in range(j, -1, -1)]
    first = jnp.array([p[0] for p in pairs], jnp.int32)
    second = jnp.array([p[1] for p in pairs], jnp.int32)
    return pl.pallas_call(
        functools.partial(own_body, gamma * LOG2E, leaf_size),
        grid_spec=pltpu.PrefetchScalarGridSpec(
            num_scalar_prefetch=2,
            grid=(len(pairs),),
            in_specs=[
                pl.BlockSpec((leaf_size, width), lambda s, a, b: (a[s], 0)),
                pl.BlockSpec((leaf_size, width), lambda s, a, b: (b[s], 0)),
                pl.BlockSpec((columns, leaf_size), lambda s, a, b: (0, a[s])),
                pl.BlockSpec((columns, leaf_size), lambda s, a, b: (0, b[s])),
            ]
            + [pl.BlockSpec(b.shape, lambda s, a, b: (0, 0)) for b in before],
            out_specs=[
                pl.BlockSpec((columns, total), lambda s, a, b: (0, 0)),
                pl.BlockSpec((8, total), lambda s, a, b: (0, 0)),
            ],
            scratch_shapes=[pltpu.VMEM((total, TILE_LANES), F32)],
        ),
        out_shape=[
            jax.ShapeDtypeStruct((columns, total), F32),
            jax.ShapeDtypeStruct((8, total), F32),
        ],
        compiler_params=params(63),
        cost_estimate=pl.CostEstimate(
            flops=2 * len(pairs) * leaf_size * leaf_size * (width + 2 * columns),
            bytes_accessed=total * width * 8,
            transcendentals=len(pairs) * leaf_size * leaf_size,
        ),
        name="own",
    )(first, second, points, points, charges, charges, *before)


def near_body(scale, groups, leaf_size, target, points, norms, before, *refs):
    buffers, out = refs[:-1], refs[-1]
    columns = before.shape[0]
    rows = buffers[0].shape[1] - TILE_ROWS
    out[...] = before[...]
    for units, source_steps in groups:
        leaf = target[source_steps]

        @pl.when(leaf >= 0)
        def _(units=units, leaf=leaf):
            source = jnp.concatenate([buffers[b][u, 0:rows, :] for b, u in units], axis=0)
            charges = jnp.concatenate(
                [
                    jnp.concatenate(
                        [
                            buffers[b][u, rows:, g * TILE_LANES : (g + 1) * TILE_LANES]
                            for g in range(columns // TILE_ROWS)
                        ],
                        axis=0,
                    )
                    for b, u in units
                ],
                axis=1,
            )
            wide = source.astype(F32)
            source_norms = scale * jnp.sum(wide * wide, axis=1, keepdims=True)
            start = pl.multiple_of(leaf * leaf_size, leaf_size)
            kernel = gauss(
                source,
                source_norms,
                points[pl.ds(start, leaf_size), :],
                norms[0:1, pl.ds(start, leaf_size)],
                scale,
            )
            out[:, pl.ds(start, leaf_size)] += jnp.dot(
                charges, kernel, preferred_element_type=F32
            )


def near(buffers, groups, target, points, norms, before, leaf_size, gamma):
    width = points.shape[1]
    columns = before.shape[0]
    rows = sum(len(units) for units, _ in groups) * TILE_LANES
    whole = pl.BlockSpec(memory_space=pltpu.VMEM)
    return pl.pallas_call(
        functools.partial(near_body, gamma * LOG2E, groups, leaf_size),
        in_specs=[pl.BlockSpec(memory_space=pltpu.SMEM)] + [whole] * (3 + len(buffers)),
        out_specs=whole,
        out_shape=jax.ShapeDtypeStruct(before.shape, F32),
        compiler_params=params(20),
        cost_estimate=pl.CostEstimate(
            flops=2 * rows * leaf_size * (width + columns),
            bytes_accessed=rows * width * 2 + points.size * 2,
            transcendentals=rows * leaf_size,
        ),
        name="near",
    )(target, points, norms, before, *buffers)


def after(value, *others):
    return lax.optimization_barrier((value, *others))[0]


def local(points, charges, near_list, leaf_basis, transfer, parent, coarse_far, coarse_coupling):
    leaf_count, leaf_size, rank = leaf_basis.shape
    width = points.shape[1]
    columns = charges.shape[0]
    near_count = near_list.shape[1]
    members = lax.axis_size("sub")
    groups = lax.axis_size("grp")
    gamma = 2.0 / width

    def exchange(block):
        return lax.all_to_all(block, "sub", split_axis=0, concat_axis=0, tiled=True)

    def spread(block):
        return jnp.broadcast_to(block[None], (members, *block.shape))

    here = lax.axis_index("sub")
    y, z = here // RING, here % RING

    entries = near_list.reshape(-1)
    inner = entries[None, :] - (jnp.arange(members) * leaf_count)[:, None]
    wanted = (inner >= 0) & (inner < leaf_count)
    requests = jnp.sum(jnp.where(wanted, inner + 1, 0), axis=1)

    terms, tails = lift(charges, leaf_basis, transfer, parent, requests, width)
    terms = exchange(terms)
    asked = terms[:, columns, 0].astype(F32).astype(jnp.int32)

    own_weight = jnp.sum(terms[:, :columns].astype(F32), axis=0).astype(BF)
    weights = exchange(spread(own_weight))
    pieces, rows = leaf_count * QUARTERS, leaf_size // QUARTERS
    plans = [[], [], []]
    for axis, way in DIRECTIONS:
        h = axis * (QUARTERS // 2)
        plans[0].append(
            [(offset(axis, 2, 0), 2 * way, 2)]
            + [(offset(axis, 2, across), h + way, 1) for across in (1, 3, 2)]
        )
        plans[1].append([(offset(axis, one(way), across), h, 2) for across in (1, 3, 2)])
        plans[2].append([(offset(axis, one(way), 0), 0, QUARTERS)])
    blocks = collect(
        points.reshape(pieces, rows, width),
        tails,
        after(asked, own_weight),
        jnp.stack([y, z]).astype(jnp.int32),
        plans[0] + plans[1] + plans[2],
    )
    count = len(DIRECTIONS)

    def send(wait, values):
        return [step(v, d) for v, d in zip(held(wait, values), DIRECTIONS)]

    def held(wait, values):
        first = [after(values[0], *wait[0], *wait[1:])]
        return first + [after(v, w, *wait[1:]) for v, w in zip(values[1:], wait[0][1:])]

    chips = groups // 2

    def along_x(k, block, *gate):
        pairs = [(i, (i + 2 * k) % groups) for i in range(groups)]
        return lax.ppermute(after(block, *gate), "grp", pairs)

    def own_part(first, last, gate, *before):
        return own(after(points, *gate), charges, range(first, last), leaf_size, gamma, before)

    blocks = [after(block, weights) for block in blocks]
    cut = leaf_count * 2 // 3
    got_1 = [step(v, d) for v, d in zip(blocks[:count], DIRECTIONS)]
    x_1 = along_x(1, weights, *blocks[:count])
    total, norms = own_part(0, cut, blocks[:count])
    got_2 = send((got_1, total, x_1), blocks[count : 2 * count])
    x_2 = along_x(2, weights, *got_1)
    total, norms = own_part(cut, leaf_count, got_1, total, norms)
    got_3 = send((got_2, total, x_2), got_1)
    x_3 = along_x(3, weights, *got_2, total)
    mine = jnp.concatenate([weights, x_1, x_2, x_3], axis=0)
    got_4 = send((got_3, x_3), blocks[2 * count :])
    swap = [(i, i ^ 1) for i in range(groups)]
    other = lax.ppermute(after(mine, *got_3), "grp", swap)
    plan_5, plan_6 = [], []
    for axis, way in DIRECTIONS:
        first = 2 * (1 - axis)
        plan_5.append(
            [(first, 4 + way, 1), (first + 1, 4 + way, 1), (4 + first + way, 4, 1)]
        )
        plan_6.append(
            [(first, 2 * way, 2), (first + 1, 2 * way, 2)]
            + [(4 + first, 2 + way, 1), (4 + first + 1, 2 + way, 1)]
        )
    woven = weave([*got_2, *got_3], plan_5 + plan_6)
    far_ids = coarse_far[0]
    far_alive = (far_ids >= 0).astype(F32)
    ids = jnp.maximum(far_ids, 0)
    group = lax.axis_index("grp")
    from_group, node = ids // members, ids % members
    side = (from_group % 2) != (group % 2)
    at = (group // 2 - from_group // 2) % chips * members
    at = at + node
    sources = jnp.where(side[:, None, None], other[at], mine[at])
    far_terms = lax.dot_general(
        sources, coarse_coupling[0], (((2,), (1,)), ((0,), (0,))), preferred_element_type=F32
    )
    field = jnp.sum(far_terms * far_alive[:, None, None], axis=0).astype(BF)
    fields = exchange(spread(field))
    got_5 = send((got_4, *woven, fields), woven[:count])
    got_6 = send((got_5, fields), woven[count:])
    add = functools.partial(near, leaf_size=leaf_size, gamma=gamma)
    groups_4, groups_6, groups_7 = [], [], []
    for d, (axis, way) in enumerate(DIRECTIONS):
        groups_4.append(([(count + d, 0), (count + d, 1)], number(offset(axis, 2, 0))))
        for k in range(0, QUARTERS, 2):
            groups_4.append(([(d, k), (d, k + 1)], number(offset(axis, one(way), 0))))
        for k, along in enumerate((1, 3, 2)):
            pair = [(d, 2 * k), (d, 2 * k + 1)]
            groups_6.append((pair, number(offset(1 - axis, along, one(way)))))
            if way == 0:
                groups_7.append(([(d, k), (d + 1, k)], number(offset(1 - axis, along, 2))))
    flat = near_list.reshape(-1)
    owner = jnp.where(flat >= 0, flat // leaf_count, 0)
    back = (y - owner // RING) % RING * RING + (z - owner % RING) % RING
    leaves = jnp.arange(flat.shape[0]) // near_count + 1
    match = (back[None, :] == jnp.arange(members)[:, None]) & (flat >= 0)[None, :]
    target = jnp.sum(jnp.where(match, leaves[None, :], 0), axis=1) - 1
    total = add([*got_4, *got_3], groups_4, target, points, norms, after(total, *got_5))
    total = finish(fields, parent, transfer, leaf_basis, total)
    got_7 = send((got_6, total), got_5)
    total = add(got_6, groups_6, target, points, norms, total)
    return add(got_7, groups_7, target, points, norms, total)


def solution(mesh):
    placed = (
        P(("grp", "sub"), None),
        P(None, ("grp", "sub")),
        P(("grp", "sub"), None),
        P(("grp", "sub"), None, None),
        P(("grp", "sub"), None, None),
        P(("grp", "sub")),
        P(("grp", "sub"), None),
        P(("grp", "sub"), None, None, None),
    )
    return jax.shard_map(
        local, mesh=mesh, in_specs=placed, out_specs=P(None, ("grp", "sub")), check_vma=False
    )
```

```python
import functools

import jax
import jax.numpy as jnp
from jax import lax
from jax.experimental import pallas as pl
from jax.experimental.pallas import tpu as pltpu
from jax.sharding import PartitionSpec as P

BF = jnp.bfloat16
F32 = jnp.float32
LOG2E = 1.4426950408889634
TILE_ROWS = 16
TILE_LANES = 128
RING = 4
QUARTERS = 4
DIRECTIONS = [(axis, way) for axis in range(2) for way in range(2)]
NT = (((1,), (1,)), ((), ()))
MIB = 1024 * 1024


def params(size):
    return pltpu.CompilerParams(vmem_limit_bytes=size * MIB)


def offset(axis, along, across):
    return (along, across) if axis == 0 else (across, along)


def number(steps):
    return steps[0] * RING + steps[1]


def one(way):
    return 1 if way == 0 else RING - 1


def step(block, direction):
    return turn(block, *offset(direction[0], one(direction[1]), 0))


def turn(block, y, z):
    pairs = [
        (d, (d // RING + y) % RING * RING + (d % RING + z) % RING) for d in range(RING * RING)
    ]
    return lax.ppermute(block, "sub", pairs)


def collect(points, tails, asked, place, plans):
    pieces, rows, width = points.shape
    extra = tails.shape[1]
    sizes = [sum(run[2] for run in plan) for plan in plans]
    runs = []
    for number, plan in enumerate(plans):
        at = 0
        for steps, quarter, length in plan:
            runs.append((number, at, steps, quarter, length))
            at += length

    def body(asked, place, points, tails, *rest):
        outs, sems = rest[:-1], rest[-1]

        def wanted(steps):
            y = (place[0] + steps[0]) % RING
            z = (place[1] + steps[1]) % RING
            return asked[y * RING + z]

        def copies(k):
            number, at, steps, quarter, length = runs[k]
            first = jnp.maximum(wanted(steps) - 1, 0) * QUARTERS + quarter
            return (
                pltpu.make_async_copy(
                    points.at[pl.ds(first, length)],
                    outs[number].at[pl.ds(at, length), pl.ds(0, rows)],
                    sems.at[k, 0],
                ),
                pltpu.make_async_copy(
                    tails.at[pl.ds(first, length)],
                    outs[number].at[pl.ds(at, length), pl.ds(rows, extra)],
                    sems.at[k, 1],
                ),
            )

        for k in range(len(runs)):

            @pl.when(wanted(runs[k][2]) > 0)
            def _(k=k):
                for copy in copies(k):
                    copy.start()

        for k in range(len(runs)):

            @pl.when(wanted(runs[k][2]) > 0)
            def _(k=k):
                for copy in copies(k):
                    copy.wait()

    scalar = pl.BlockSpec(memory_space=pltpu.SMEM)
    return pl.pallas_call(
        body,
        in_specs=[scalar, scalar] + [pl.BlockSpec(memory_space=pltpu.VMEM)] * 2,
        out_specs=[pl.BlockSpec(memory_space=pltpu.HBM)] * len(plans),
        out_shape=[jax.ShapeDtypeStruct((n, rows + extra, width), BF) for n in sizes],
        scratch_shapes=[pltpu.SemaphoreType.DMA((len(runs), 2))],
        compiler_params=params(63),
        cost_estimate=pl.CostEstimate(
            flops=0, bytes_accessed=sum(sizes) * rows * width * 4, transcendentals=0
        ),
        name="collect",
    )(asked, place, points, tails)


def weave(sources, plans):
    shape = sources[0].shape[1:]
    sizes = [sum(run[2] for run in plan) for plan in plans]
    runs = []
    for place, plan in enumerate(plans):
        at = 0
        for source, first, length in plan:
            runs.append((source, first, length, place, at, sum(sizes[:place]) + at))
            at += length

    def body(*refs):
        ins = refs[: len(sources)]
        outs = refs[len(sources) : -3]
        held, loads, stores = refs[-3:]
        first_leg, second_leg = [], []
        for k, (source, first, length, place, at, row) in enumerate(runs):
            staged = held.at[pl.ds(row, length)]
            first_leg.append(
                pltpu.make_async_copy(
                    ins[source].at[pl.ds(first, length)], staged, loads.at[k]
                )
            )
            second_leg.append(
                pltpu.make_async_copy(staged, outs[place].at[pl.ds(at, length)], stores.at[k])
            )
        for copy in first_leg:
            copy.start()
        for load, store in zip(first_leg, second_leg):
            load.wait()
            store.start()
        for copy in second_leg:
            copy.wait()

    return pl.pallas_call(
        body,
        in_specs=[pl.BlockSpec(memory_space=pl.ANY)] * len(sources),
        out_specs=[pl.BlockSpec(memory_space=pltpu.HBM)] * len(plans),
        out_shape=[jax.ShapeDtypeStruct((size, *shape), BF) for size in sizes],
        scratch_shapes=[
            pltpu.VMEM((sum(sizes), *shape), BF),
            pltpu.SemaphoreType.DMA((len(runs),)),
            pltpu.SemaphoreType.DMA((len(runs),)),
        ],
        compiler_params=params(63),
        cost_estimate=pl.CostEstimate(
            flops=0,
            bytes_accessed=4 * sum(sizes) * shape[0] * shape[1],
            transcendentals=0,
        ),
        name="weave",
    )(*sources)


def lift(charges, leaf_basis, transfer, slots, requests, width):
    leaf_count, leaf_size, rank = leaf_basis.shape
    columns = charges.shape[0]
    lines, rows = columns // TILE_ROWS, leaf_size // QUARTERS
    members = requests.shape[0]

    def body(slots, requests, charges, basis, transfer, out, tails, sums):
        t = pl.program_id(0)
        tails[...] = jnp.zeros_like(tails)
        for q in range(QUARTERS):
            for g in range(lines):
                tails[q, :, g * rows : (g + 1) * rows] = charges[
                    g * TILE_ROWS : (g + 1) * TILE_ROWS, q * rows : (q + 1) * rows
                ]

        @pl.when(t == 0)
        def _():
            sums[...] = jnp.zeros_like(sums)

        skeleton = jnp.dot(charges[...], basis[0], preferred_element_type=F32).astype(BF)
        sums[slots[t]] += jnp.dot(skeleton, transfer[0], preferred_element_type=F32)

        @pl.when(t == leaf_count - 1)
        def _():
            out[:, 0:columns, :] = sums[...].astype(BF)
            for d in range(members):
                value = requests[d].astype(F32)
                out[d, columns:, :] = jnp.full((TILE_ROWS, rank), value, F32).astype(BF)

    return pl.pallas_call(
        body,
        grid_spec=pltpu.PrefetchScalarGridSpec(
            num_scalar_prefetch=2,
            grid=(leaf_count,),
            in_specs=[
                pl.BlockSpec((columns, leaf_size), lambda t, s, r: (0, t)),
                pl.BlockSpec((1, leaf_size, rank), lambda t, s, r: (t, 0, 0)),
                pl.BlockSpec((1, rank, rank), lambda t, s, r: (t, 0, 0)),
            ],
            out_specs=[
                pl.BlockSpec((members, columns + TILE_ROWS, rank), lambda t, s, r: (0, 0, 0)),
                pl.BlockSpec((QUARTERS, TILE_ROWS, width), lambda t, s, r: (t, 0, 0)),
            ],
            scratch_shapes=[pltpu.VMEM((members, columns, rank), F32)],
        ),
        out_shape=[
            jax.ShapeDtypeStruct((members, columns + TILE_ROWS, rank), BF),
            jax.ShapeDtypeStruct((leaf_count * QUARTERS, TILE_ROWS, width), BF),
        ],
        compiler_params=params(63),
        name="lift",
    )(slots, requests, charges, leaf_basis, transfer)


def finish(fields, slots, transfer, leaf_basis, total):
    leaf_count, leaf_size, rank = leaf_basis.shape
    columns = total.shape[0]

    def body(slots, field, transfer, basis, total, out):
        descended = lax.dot_general(
            field[0], transfer[0], NT, preferred_element_type=F32
        ).astype(BF)
        out[...] = total[...] + lax.dot_general(
            descended, basis[0], NT, preferred_element_type=F32
        )

    return pl.pallas_call(
        body,
        grid_spec=pltpu.PrefetchScalarGridSpec(
            num_scalar_prefetch=1,
            grid=(leaf_count,),
            in_specs=[
                pl.BlockSpec((1, columns, rank), lambda t, s: (s[t], 0, 0)),
                pl.BlockSpec((1, rank, rank), lambda t, s: (t, 0, 0)),
                pl.BlockSpec((1, leaf_size, rank), lambda t, s: (t, 0, 0)),
                pl.BlockSpec((columns, leaf_size), lambda t, s: (0, t)),
            ],
            out_specs=pl.BlockSpec((columns, leaf_size), lambda t, s: (0, t)),
        ),
        out_shape=jax.ShapeDtypeStruct(total.shape, F32),
        compiler_params=params(8),
        name="finish",
    )(slots, fields, transfer, leaf_basis, total)


def gauss(source, source_norms, target, target_norms, scale):
    gram = lax.dot_general(source, target, NT, preferred_element_type=F32)
    return jnp.exp2((2.0 * scale) * gram - (source_norms + target_norms)).astype(BF)


def own_body(scale, leaf_size, first, second, ti, sj, ci, cj, *rest):
    before, (out, rows, col) = rest[:-3], rest[-3:]
    step = pl.program_id(0)
    width = ti.shape[1]
    i0 = pl.multiple_of(first[step] * leaf_size, leaf_size)
    j0 = pl.multiple_of(second[step] * leaf_size, leaf_size)
    ones = jnp.ones((8, width), BF)
    lanes = jnp.ones((width, TILE_LANES), BF)

    @pl.when(step == 0)
    def _():
        if before:
            out[...] = before[0][...]
            rows[...] = before[1][...]
        else:
            out[...] = jnp.zeros_like(out)
            rows[...] = jnp.zeros_like(rows)

    @pl.when(i0 == j0)
    def _():
        wide = sj[...].astype(F32)
        square = wide * wide
        high = square.astype(BF)
        low = (square - high.astype(F32)).astype(BF)
        row = lax.dot_general(ones, high, NT, preferred_element_type=F32) + lax.dot_general(
            ones, low, NT, preferred_element_type=F32
        )
        rows[:, pl.ds(i0, leaf_size)] = scale * row
        column = jnp.dot(high, lanes, preferred_element_type=F32) + jnp.dot(
            low, lanes, preferred_element_type=F32
        )
        col[pl.ds(i0, leaf_size), :] = scale * column

    gram = lax.dot_general(sj[...], ti[...], NT, preferred_element_type=F32)
    norms = col[pl.ds(j0, leaf_size), :][:, :1] + rows[0:1, pl.ds(i0, leaf_size)]
    kernel = jnp.exp2((2.0 * scale) * gram - norms).astype(BF)
    out[:, pl.ds(i0, leaf_size)] += jnp.dot(cj[...], kernel, preferred_element_type=F32)

    @pl.when(i0 != j0)
    def _():
        out[:, pl.ds(j0, leaf_size)] += lax.dot_general(
            ci[...], kernel, NT, preferred_element_type=F32
        )


def own(points, charges, columns_of, leaf_size, gamma, before=()):
    width = points.shape[1]
    columns = charges.shape[0]
    total = points.shape[0]
    pairs = [(i, j) for j in columns_of for i in range(j, -1, -1)]
    first = jnp.array([p[0] for p in pairs], jnp.int32)
    second = jnp.array([p[1] for p in pairs], jnp.int32)
    return pl.pallas_call(
        functools.partial(own_body, gamma * LOG2E, leaf_size),
        grid_spec=pltpu.PrefetchScalarGridSpec(
            num_scalar_prefetch=2,
            grid=(len(pairs),),
            in_specs=[
                pl.BlockSpec((leaf_size, width), lambda s, a, b: (a[s], 0)),
                pl.BlockSpec((leaf_size, width), lambda s, a, b: (b[s], 0)),
                pl.BlockSpec((columns, leaf_size), lambda s, a, b: (0, a[s])),
                pl.BlockSpec((columns, leaf_size), lambda s, a, b: (0, b[s])),
            ]
            + [pl.BlockSpec(b.shape, lambda s, a, b: (0, 0)) for b in before],
            out_specs=[
                pl.BlockSpec((columns, total), lambda s, a, b: (0, 0)),
                pl.BlockSpec((8, total), lambda s, a, b: (0, 0)),
            ],
            scratch_shapes=[pltpu.VMEM((total, TILE_LANES), F32)],
        ),
        out_shape=[
            jax.ShapeDtypeStruct((columns, total), F32),
            jax.ShapeDtypeStruct((8, total), F32),
        ],
        compiler_params=params(63),
        cost_estimate=pl.CostEstimate(
            flops=2 * len(pairs) * leaf_size * leaf_size * (width + 2 * columns),
            bytes_accessed=total * width * 8,
            transcendentals=len(pairs) * leaf_size * leaf_size,
        ),
        name="own",
    )(first, second, points, points, charges, charges, *before)


def near_body(scale, groups, leaf_size, target, points, norms, before, *refs):
    buffers, out = refs[:-1], refs[-1]
    columns = before.shape[0]
    rows = buffers[0].shape[1] - TILE_ROWS
    out[...] = before[...]
    for units, source_steps in groups:
        leaf = target[source_steps]

        @pl.when(leaf >= 0)
        def _(units=units, leaf=leaf):
            source = jnp.concatenate([buffers[b][u, 0:rows, :] for b, u in units], axis=0)
            charges = jnp.concatenate(
                [
                    jnp.concatenate(
                        [
                            buffers[b][u, rows:, g * TILE_LANES : (g + 1) * TILE_LANES]
                            for g in range(columns // TILE_ROWS)
                        ],
                        axis=0,
                    )
                    for b, u in units
                ],
                axis=1,
            )
            wide = source.astype(F32)
            source_norms = scale * jnp.sum(wide * wide, axis=1, keepdims=True)
            start = pl.multiple_of(leaf * leaf_size, leaf_size)
            kernel = gauss(
                source,
                source_norms,
                points[pl.ds(start, leaf_size), :],
                norms[0:1, pl.ds(start, leaf_size)],
                scale,
            )
            out[:, pl.ds(start, leaf_size)] += jnp.dot(
                charges, kernel, preferred_element_type=F32
            )


def near(buffers, groups, target, points, norms, before, leaf_size, gamma):
    width = points.shape[1]
    columns = before.shape[0]
    rows = sum(len(units) for units, _ in groups) * TILE_LANES
    whole = pl.BlockSpec(memory_space=pltpu.VMEM)
    return pl.pallas_call(
        functools.partial(near_body, gamma * LOG2E, groups, leaf_size),
        in_specs=[pl.BlockSpec(memory_space=pltpu.SMEM)] + [whole] * (3 + len(buffers)),
        out_specs=whole,
        out_shape=jax.ShapeDtypeStruct(before.shape, F32),
        compiler_params=params(20),
        cost_estimate=pl.CostEstimate(
            flops=2 * rows * leaf_size * (width + columns),
            bytes_accessed=rows * width * 2 + points.size * 2,
            transcendentals=rows * leaf_size,
        ),
        name="near",
    )(target, points, norms, before, *buffers)


def after(value, *others):
    return lax.optimization_barrier((value, *others))[0]


def local(points, charges, near_list, leaf_basis, transfer, parent, coarse_far, coarse_coupling):
    leaf_count, leaf_size, rank = leaf_basis.shape
    width = points.shape[1]
    columns = charges.shape[0]
    near_count = near_list.shape[1]
    members = lax.axis_size("sub")
    groups = lax.axis_size("grp")
    gamma = 2.0 / width

    def exchange(block):
        return lax.all_to_all(block, "sub", split_axis=0, concat_axis=0, tiled=True)

    def spread(block):
        return jnp.broadcast_to(block[None], (members, *block.shape))

    here = lax.axis_index("sub")
    y, z = here // RING, here % RING

    entries = near_list.reshape(-1)
    inner = entries[None, :] - (jnp.arange(members) * leaf_count)[:, None]
    wanted = (inner >= 0) & (inner < leaf_count)
    requests = jnp.sum(jnp.where(wanted, inner + 1, 0), axis=1)

    terms, tails = lift(charges, leaf_basis, transfer, parent, requests, width)
    terms = exchange(terms)
    asked = terms[:, columns, 0].astype(F32).astype(jnp.int32)

    own_weight = jnp.sum(terms[:, :columns].astype(F32), axis=0).astype(BF)
    weights = exchange(spread(own_weight))
    pieces, rows = leaf_count * QUARTERS, leaf_size // QUARTERS
    plans = [[], [], []]
    for axis, way in DIRECTIONS:
        h = axis * (QUARTERS // 2)
        plans[0].append(
            [(offset(axis, 2, 0), 2 * way, 2)]
            + [(offset(axis, 2, across), h + way, 1) for across in (1, 3, 2)]
        )
        plans[1].append([(offset(axis, one(way), across), h, 2) for across in (1, 3, 2)])
        plans[2].append([(offset(axis, one(way), 0), 0, QUARTERS)])
    blocks = collect(
        points.reshape(pieces, rows, width),
        tails,
        after(asked, own_weight),
        jnp.stack([y, z]).astype(jnp.int32),
        plans[0] + plans[1] + plans[2],
    )
    count = len(DIRECTIONS)

    def send(wait, values):
        return [step(v, d) for v, d in zip(held(wait, values), DIRECTIONS)]

    def held(wait, values):
        return [after(v, w, *wait[1:]) for v, w in zip(values, wait[0])]

    chips = groups // 2

    def along_x(k, block, *gate):
        pairs = [(i, (i + 2 * k) % groups) for i in range(groups)]
        return lax.ppermute(after(block, *gate), "grp", pairs)

    def own_part(first, last, gate, *before):
        return own(after(points, *gate), charges, range(first, last), leaf_size, gamma, before)

    blocks = [after(block, weights) for block in blocks]
    cut = leaf_count * 2 // 3
    got_1 = [step(v, d) for v, d in zip(blocks[:count], DIRECTIONS)]
    x_1 = along_x(1, weights, *blocks[:count])
    total, norms = own_part(0, cut, blocks[:count])
    got_2 = send((got_1, total, x_1), blocks[count : 2 * count])
    x_2 = along_x(2, weights, *got_1)
    total, norms = own_part(cut, leaf_count, got_1, total, norms)
    got_3 = send((got_2, total, x_2), got_1)
    x_3 = along_x(3, weights, *got_2, total)
    mine = jnp.concatenate([weights, x_1, x_2, x_3], axis=0)
    got_4 = send((got_3, x_3), blocks[2 * count :])
    swap = [(i, i ^ 1) for i in range(groups)]
    other = lax.ppermute(after(mine, *got_3), "grp", swap)
    plan_5, plan_6 = [], []
    for axis, way in DIRECTIONS:
        first = 2 * (1 - axis)
        plan_5.append(
            [(first, 4 + way, 1), (first + 1, 4 + way, 1), (4 + first + way, 4, 1)]
        )
        plan_6.append(
            [(first, 2 * way, 2), (first + 1, 2 * way, 2)]
            + [(4 + first, 2 + way, 1), (4 + first + 1, 2 + way, 1)]
        )
    woven = weave([*got_2, *got_3], plan_5 + plan_6)
    far_ids = coarse_far[0]
    far_alive = (far_ids >= 0).astype(F32)
    ids = jnp.maximum(far_ids, 0)
    group = lax.axis_index("grp")
    from_group, node = ids // members, ids % members
    side = (from_group % 2) != (group % 2)
    at = (group // 2 - from_group // 2) % chips * members
    at = at + node
    sources = jnp.where(side[:, None, None], other[at], mine[at])
    far_terms = lax.dot_general(
        sources, coarse_coupling[0], (((2,), (1,)), ((0,), (0,))), preferred_element_type=F32
    )
    field = jnp.sum(far_terms * far_alive[:, None, None], axis=0).astype(BF)
    fields = exchange(spread(field))
    got_5 = send((got_4, *woven, fields), woven[:count])
    got_6 = send((got_5, fields), woven[count:])
    add = functools.partial(near, leaf_size=leaf_size, gamma=gamma)
    groups_4, groups_6, groups_7 = [], [], []
    for d, (axis, way) in enumerate(DIRECTIONS):
        groups_4.append(([(count + d, 0), (count + d, 1)], number(offset(axis, 2, 0))))
        for k in range(0, QUARTERS, 2):
            groups_4.append(([(d, k), (d, k + 1)], number(offset(axis, one(way), 0))))
        for k, along in enumerate((1, 3, 2)):
            pair = [(d, 2 * k), (d, 2 * k + 1)]
            groups_6.append((pair, number(offset(1 - axis, along, one(way)))))
            if way == 0:
                groups_7.append(([(d, k), (d + 1, k)], number(offset(1 - axis, along, 2))))
    flat = near_list.reshape(-1)
    owner = jnp.where(flat >= 0, flat // leaf_count, 0)
    back = (y - owner // RING) % RING * RING + (z - owner % RING) % RING
    leaves = jnp.arange(flat.shape[0]) // near_count + 1
    match = (back[None, :] == jnp.arange(members)[:, None]) & (flat >= 0)[None, :]
    target = jnp.sum(jnp.where(match, leaves[None, :], 0), axis=1) - 1
    total = add([*got_4, *got_3], groups_4, target, points, norms, after(total, *got_5))
    total = finish(fields, parent, transfer, leaf_basis, total)
    got_7 = send((got_6, total), got_5)
    total = add(got_6, groups_6, target, points, norms, total)
    return add(got_7, groups_7, target, points, norms, total)


def solution(mesh):
    placed = (
        P(("grp", "sub"), None),
        P(None, ("grp", "sub")),
        P(("grp", "sub"), None),
        P(("grp", "sub"), None, None),
        P(("grp", "sub"), None, None),
        P(("grp", "sub")),
        P(("grp", "sub"), None),
        P(("grp", "sub"), None, None, None),
    )
    return jax.shard_map(
        local, mesh=mesh, in_specs=placed, out_specs=P(None, ("grp", "sub")), check_vma=False
    )
```

```python
import functools

import jax
import jax.numpy as jnp
from jax import lax
from jax.experimental import pallas as pl
from jax.experimental.pallas import tpu as pltpu
from jax.sharding import PartitionSpec as P

BF = jnp.bfloat16
F32 = jnp.float32
LOG2E = 1.4426950408889634
TILE_ROWS = 16
TILE_LANES = 128
RING = 4
QUARTERS = 4
DIRECTIONS = [(axis, way) for way in range(2) for axis in range(2)]
NT = (((1,), (1,)), ((), ()))
MIB = 1024 * 1024


def params(size):
    return pltpu.CompilerParams(vmem_limit_bytes=size * MIB)


def offset(axis, along, across):
    return (along, across) if axis == 0 else (across, along)


def number(steps):
    return steps[0] * RING + steps[1]


def one(way):
    return 1 if way == 0 else RING - 1


def step(block, direction):
    return turn(block, *offset(direction[0], one(direction[1]), 0))


def turn(block, y, z):
    pairs = [
        (d, (d // RING + y) % RING * RING + (d % RING + z) % RING) for d in range(RING * RING)
    ]
    return lax.ppermute(block, "sub", pairs)


def collect(points, tails, asked, place, plans):
    pieces, rows, width = points.shape
    extra = tails.shape[1]
    sizes = [sum(run[2] for run in plan) for plan in plans]
    runs = []
    for number, plan in enumerate(plans):
        at = 0
        for steps, quarter, length in plan:
            runs.append((number, at, steps, quarter, length))
            at += length

    def body(asked, place, points, tails, *rest):
        outs, sems = rest[:-1], rest[-1]

        def wanted(steps):
            y = (place[0] + steps[0]) % RING
            z = (place[1] + steps[1]) % RING
            return asked[y * RING + z]

        def copies(k):
            number, at, steps, quarter, length = runs[k]
            first = jnp.maximum(wanted(steps) - 1, 0) * QUARTERS + quarter
            return (
                pltpu.make_async_copy(
                    points.at[pl.ds(first, length)],
                    outs[number].at[pl.ds(at, length), pl.ds(0, rows)],
                    sems.at[k, 0],
                ),
                pltpu.make_async_copy(
                    tails.at[pl.ds(first, length)],
                    outs[number].at[pl.ds(at, length), pl.ds(rows, extra)],
                    sems.at[k, 1],
                ),
            )

        for k in range(len(runs)):

            @pl.when(wanted(runs[k][2]) > 0)
            def _(k=k):
                for copy in copies(k):
                    copy.start()

        for k in range(len(runs)):

            @pl.when(wanted(runs[k][2]) > 0)
            def _(k=k):
                for copy in copies(k):
                    copy.wait()

    scalar = pl.BlockSpec(memory_space=pltpu.SMEM)
    return pl.pallas_call(
        body,
        in_specs=[scalar, scalar] + [pl.BlockSpec(memory_space=pltpu.VMEM)] * 2,
        out_specs=[pl.BlockSpec(memory_space=pltpu.HBM)] * len(plans),
        out_shape=[jax.ShapeDtypeStruct((n, rows + extra, width), BF) for n in sizes],
        scratch_shapes=[pltpu.SemaphoreType.DMA((len(runs), 2))],
        compiler_params=params(63),
        cost_estimate=pl.CostEstimate(
            flops=0, bytes_accessed=sum(sizes) * rows * width * 4, transcendentals=0
        ),
        name="collect",
    )(asked, place, points, tails)


def weave(sources, plans):
    shape = sources[0].shape[1:]
    sizes = [sum(run[2] for run in plan) for plan in plans]
    runs = []
    for place, plan in enumerate(plans):
        at = 0
        for source, first, length in plan:
            runs.append((source, first, length, place, at, sum(sizes[:place]) + at))
            at += length

    def body(*refs):
        ins = refs[: len(sources)]
        outs = refs[len(sources) : -3]
        held, loads, stores = refs[-3:]
        first_leg, second_leg = [], []
        for k, (source, first, length, place, at, row) in enumerate(runs):
            staged = held.at[pl.ds(row, length)]
            first_leg.append(
                pltpu.make_async_copy(
                    ins[source].at[pl.ds(first, length)], staged, loads.at[k]
                )
            )
            second_leg.append(
                pltpu.make_async_copy(staged, outs[place].at[pl.ds(at, length)], stores.at[k])
            )
        for copy in first_leg:
            copy.start()
        for load, store in zip(first_leg, second_leg):
            load.wait()
            store.start()
        for copy in second_leg:
            copy.wait()

    return pl.pallas_call(
        body,
        in_specs=[pl.BlockSpec(memory_space=pl.ANY)] * len(sources),
        out_specs=[pl.BlockSpec(memory_space=pltpu.HBM)] * len(plans),
        out_shape=[jax.ShapeDtypeStruct((size, *shape), BF) for size in sizes],
        scratch_shapes=[
            pltpu.VMEM((sum(sizes), *shape), BF),
            pltpu.SemaphoreType.DMA((len(runs),)),
            pltpu.SemaphoreType.DMA((len(runs),)),
        ],
        compiler_params=params(63),
        cost_estimate=pl.CostEstimate(
            flops=0,
            bytes_accessed=4 * sum(sizes) * shape[0] * shape[1],
            transcendentals=0,
        ),
        name="weave",
    )(*sources)


def lift(charges, leaf_basis, transfer, slots, requests, width):
    leaf_count, leaf_size, rank = leaf_basis.shape
    columns = charges.shape[0]
    lines, rows = columns // TILE_ROWS, leaf_size // QUARTERS
    members = requests.shape[0]

    def body(slots, requests, charges, basis, transfer, out, tails, sums):
        t = pl.program_id(0)
        tails[...] = jnp.zeros_like(tails)
        for q in range(QUARTERS):
            for g in range(lines):
                tails[q, :, g * rows : (g + 1) * rows] = charges[
                    g * TILE_ROWS : (g + 1) * TILE_ROWS, q * rows : (q + 1) * rows
                ]

        @pl.when(t == 0)
        def _():
            sums[...] = jnp.zeros_like(sums)

        skeleton = jnp.dot(charges[...], basis[0], preferred_element_type=F32).astype(BF)
        sums[slots[t]] += jnp.dot(skeleton, transfer[0], preferred_element_type=F32)

        @pl.when(t == leaf_count - 1)
        def _():
            out[:, 0:columns, :] = sums[...].astype(BF)
            for d in range(members):
                value = requests[d].astype(F32)
                out[d, columns:, :] = jnp.full((TILE_ROWS, rank), value, F32).astype(BF)

    return pl.pallas_call(
        body,
        grid_spec=pltpu.PrefetchScalarGridSpec(
            num_scalar_prefetch=2,
            grid=(leaf_count,),
            in_specs=[
                pl.BlockSpec((columns, leaf_size), lambda t, s, r: (0, t)),
                pl.BlockSpec((1, leaf_size, rank), lambda t, s, r: (t, 0, 0)),
                pl.BlockSpec((1, rank, rank), lambda t, s, r: (t, 0, 0)),
            ],
            out_specs=[
                pl.BlockSpec((members, columns + TILE_ROWS, rank), lambda t, s, r: (0, 0, 0)),
                pl.BlockSpec((QUARTERS, TILE_ROWS, width), lambda t, s, r: (t, 0, 0)),
            ],
            scratch_shapes=[pltpu.VMEM((members, columns, rank), F32)],
        ),
        out_shape=[
            jax.ShapeDtypeStruct((members, columns + TILE_ROWS, rank), BF),
            jax.ShapeDtypeStruct((leaf_count * QUARTERS, TILE_ROWS, width), BF),
        ],
        compiler_params=params(63),
        name="lift",
    )(slots, requests, charges, leaf_basis, transfer)


def finish(fields, slots, transfer, leaf_basis, total):
    leaf_count, leaf_size, rank = leaf_basis.shape
    columns = total.shape[0]

    def body(slots, field, transfer, basis, total, out):
        descended = lax.dot_general(
            field[0], transfer[0], NT, preferred_element_type=F32
        ).astype(BF)
        out[...] = total[...] + lax.dot_general(
            descended, basis[0], NT, preferred_element_type=F32
        )

    return pl.pallas_call(
        body,
        grid_spec=pltpu.PrefetchScalarGridSpec(
            num_scalar_prefetch=1,
            grid=(leaf_count,),
            in_specs=[
                pl.BlockSpec((1, columns, rank), lambda t, s: (s[t], 0, 0)),
                pl.BlockSpec((1, rank, rank), lambda t, s: (t, 0, 0)),
                pl.BlockSpec((1, leaf_size, rank), lambda t, s: (t, 0, 0)),
                pl.BlockSpec((columns, leaf_size), lambda t, s: (0, t)),
            ],
            out_specs=pl.BlockSpec((columns, leaf_size), lambda t, s: (0, t)),
        ),
        out_shape=jax.ShapeDtypeStruct(total.shape, F32),
        compiler_params=params(8),
        name="finish",
    )(slots, fields, transfer, leaf_basis, total)


def gauss(source, source_norms, target, target_norms, scale):
    gram = lax.dot_general(source, target, NT, preferred_element_type=F32)
    return jnp.exp2((2.0 * scale) * gram - (source_norms + target_norms)).astype(BF)


def own_body(scale, leaf_size, first, second, ti, sj, ci, cj, *rest):
    before, (out, rows, col) = rest[:-3], rest[-3:]
    step = pl.program_id(0)
    width = ti.shape[1]
    i0 = pl.multiple_of(first[step] * leaf_size, leaf_size)
    j0 = pl.multiple_of(second[step] * leaf_size, leaf_size)
    ones = jnp.ones((8, width), BF)
    lanes = jnp.ones((width, TILE_LANES), BF)

    @pl.when(step == 0)
    def _():
        if before:
            out[...] = before[0][...]
            rows[...] = before[1][...]
        else:
            out[...] = jnp.zeros_like(out)
            rows[...] = jnp.zeros_like(rows)

    @pl.when(i0 == j0)
    def _():
        wide = sj[...].astype(F32)
        square = wide * wide
        high = square.astype(BF)
        low = (square - high.astype(F32)).astype(BF)
        row = lax.dot_general(ones, high, NT, preferred_element_type=F32) + lax.dot_general(
            ones, low, NT, preferred_element_type=F32
        )
        rows[:, pl.ds(i0, leaf_size)] = scale * row
        column = jnp.dot(high, lanes, preferred_element_type=F32) + jnp.dot(
            low, lanes, preferred_element_type=F32
        )
        col[pl.ds(i0, leaf_size), :] = scale * column

    gram = lax.dot_general(sj[...], ti[...], NT, preferred_element_type=F32)
    norms = col[pl.ds(j0, leaf_size), :][:, :1] + rows[0:1, pl.ds(i0, leaf_size)]
    kernel = jnp.exp2((2.0 * scale) * gram - norms).astype(BF)
    out[:, pl.ds(i0, leaf_size)] += jnp.dot(cj[...], kernel, preferred_element_type=F32)

    @pl.when(i0 != j0)
    def _():
        out[:, pl.ds(j0, leaf_size)] += lax.dot_general(
            ci[...], kernel, NT, preferred_element_type=F32
        )


def own(points, charges, columns_of, leaf_size, gamma, before=()):
    width = points.shape[1]
    columns = charges.shape[0]
    total = points.shape[0]
    pairs = [(i, j) for j in columns_of for i in range(j, -1, -1)]
    first = jnp.array([p[0] for p in pairs], jnp.int32)
    second = jnp.array([p[1] for p in pairs], jnp.int32)
    return pl.pallas_call(
        functools.partial(own_body, gamma * LOG2E, leaf_size),
        grid_spec=pltpu.PrefetchScalarGridSpec(
            num_scalar_prefetch=2,
            grid=(len(pairs),),
            in_specs=[
                pl.BlockSpec((leaf_size, width), lambda s, a, b: (a[s], 0)),
                pl.BlockSpec((leaf_size, width), lambda s, a, b: (b[s], 0)),
                pl.BlockSpec((columns, leaf_size), lambda s, a, b: (0, a[s])),
                pl.BlockSpec((columns, leaf_size), lambda s, a, b: (0, b[s])),
            ]
            + [pl.BlockSpec(b.shape, lambda s, a, b: (0, 0)) for b in before],
            out_specs=[
                pl.BlockSpec((columns, total), lambda s, a, b: (0, 0)),
                pl.BlockSpec((8, total), lambda s, a, b: (0, 0)),
            ],
            scratch_shapes=[pltpu.VMEM((total, TILE_LANES), F32)],
        ),
        out_shape=[
            jax.ShapeDtypeStruct((columns, total), F32),
            jax.ShapeDtypeStruct((8, total), F32),
        ],
        compiler_params=params(63),
        cost_estimate=pl.CostEstimate(
            flops=2 * len(pairs) * leaf_size * leaf_size * (width + 2 * columns),
            bytes_accessed=total * width * 8,
            transcendentals=len(pairs) * leaf_size * leaf_size,
        ),
        name="own",
    )(first, second, points, points, charges, charges, *before)


def near_body(scale, groups, leaf_size, target, points, norms, before, *refs):
    buffers, out = refs[:-1], refs[-1]
    columns = before.shape[0]
    rows = buffers[0].shape[1] - TILE_ROWS
    out[...] = before[...]
    for units, source_steps in groups:
        leaf = target[source_steps]

        @pl.when(leaf >= 0)
        def _(units=units, leaf=leaf):
            source = jnp.concatenate([buffers[b][u, 0:rows, :] for b, u in units], axis=0)
            charges = jnp.concatenate(
                [
                    jnp.concatenate(
                        [
                            buffers[b][u, rows:, g * TILE_LANES : (g + 1) * TILE_LANES]
                            for g in range(columns // TILE_ROWS)
                        ],
                        axis=0,
                    )
                    for b, u in units
                ],
                axis=1,
            )
            wide = source.astype(F32)
            source_norms = scale * jnp.sum(wide * wide, axis=1, keepdims=True)
            start = pl.multiple_of(leaf * leaf_size, leaf_size)
            kernel = gauss(
                source,
                source_norms,
                points[pl.ds(start, leaf_size), :],
                norms[0:1, pl.ds(start, leaf_size)],
                scale,
            )
            out[:, pl.ds(start, leaf_size)] += jnp.dot(
                charges, kernel, preferred_element_type=F32
            )


def near(buffers, groups, target, points, norms, before, leaf_size, gamma):
    width = points.shape[1]
    columns = before.shape[0]
    rows = sum(len(units) for units, _ in groups) * TILE_LANES
    whole = pl.BlockSpec(memory_space=pltpu.VMEM)
    return pl.pallas_call(
        functools.partial(near_body, gamma * LOG2E, groups, leaf_size),
        in_specs=[pl.BlockSpec(memory_space=pltpu.SMEM)] + [whole] * (3 + len(buffers)),
        out_specs=whole,
        out_shape=jax.ShapeDtypeStruct(before.shape, F32),
        compiler_params=params(20),
        cost_estimate=pl.CostEstimate(
            flops=2 * rows * leaf_size * (width + columns),
            bytes_accessed=rows * width * 2 + points.size * 2,
            transcendentals=rows * leaf_size,
        ),
        name="near",
    )(target, points, norms, before, *buffers)


def after(value, *others):
    return lax.optimization_barrier((value, *others))[0]


def local(points, charges, near_list, leaf_basis, transfer, parent, coarse_far, coarse_coupling):
    leaf_count, leaf_size, rank = leaf_basis.shape
    width = points.shape[1]
    columns = charges.shape[0]
    near_count = near_list.shape[1]
    members = lax.axis_size("sub")
    groups = lax.axis_size("grp")
    gamma = 2.0 / width

    def exchange(block):
        return lax.all_to_all(block, "sub", split_axis=0, concat_axis=0, tiled=True)

    def spread(block):
        return jnp.broadcast_to(block[None], (members, *block.shape))

    here = lax.axis_index("sub")
    y, z = here // RING, here % RING

    entries = near_list.reshape(-1)
    inner = entries[None, :] - (jnp.arange(members) * leaf_count)[:, None]
    wanted = (inner >= 0) & (inner < leaf_count)
    requests = jnp.sum(jnp.where(wanted, inner + 1, 0), axis=1)

    terms, tails = lift(charges, leaf_basis, transfer, parent, requests, width)
    terms = exchange(terms)
    asked = terms[:, columns, 0].astype(F32).astype(jnp.int32)

    own_weight = jnp.sum(terms[:, :columns].astype(F32), axis=0).astype(BF)
    weights = exchange(spread(own_weight))
    pieces, rows = leaf_count * QUARTERS, leaf_size // QUARTERS
    plans = [[], [], []]
    for axis, way in DIRECTIONS:
        h = axis * (QUARTERS // 2)
        plans[0].append(
            [(offset(axis, 2, 0), 2 * way, 2)]
            + [(offset(axis, 2, across), h + way, 1) for across in (1, 3, 2)]
        )
        plans[1].append([(offset(axis, one(way), across), h, 2) for across in (1, 3, 2)])
        plans[2].append([(offset(axis, one(way), 0), 0, QUARTERS)])
    blocks = collect(
        points.reshape(pieces, rows, width),
        tails,
        after(asked, own_weight),
        jnp.stack([y, z]).astype(jnp.int32),
        plans[0] + plans[1] + plans[2],
    )
    count = len(DIRECTIONS)

    def send(wait, values):
        return [step(v, d) for v, d in zip(held(wait, values), DIRECTIONS)]

    def held(wait, values):
        return [after(v, w, *wait[1:]) for v, w in zip(values, wait[0])]

    chips = groups // 2

    def along_x(k, block, *gate):
        pairs = [(i, (i + 2 * k) % groups) for i in range(groups)]
        return lax.ppermute(after(block, *gate), "grp", pairs)

    def own_part(first, last, gate, *before):
        return own(after(points, *gate), charges, range(first, last), leaf_size, gamma, before)

    blocks = [after(block, weights) for block in blocks]
    cut = leaf_count * 2 // 3
    got_1 = [step(v, d) for v, d in zip(blocks[:count], DIRECTIONS)]
    x_1 = along_x(1, weights, *blocks[:count])
    total, norms = own_part(0, cut, blocks[:count])
    got_2 = send((got_1, total, x_1), blocks[count : 2 * count])
    x_2 = along_x(2, weights, *got_1)
    total, norms = own_part(cut, leaf_count, got_1, total, norms)
    got_3 = send((got_2, total, x_2), got_1)
    x_3 = along_x(3, weights, *got_2, total)
    mine = jnp.concatenate([weights, x_1, x_2, x_3], axis=0)
    got_4 = send((got_3, x_3), blocks[2 * count :])
    swap = [(i, i ^ 1) for i in range(groups)]
    other = lax.ppermute(after(mine, *got_3), "grp", swap)
    plan_5, plan_6 = [], []
    for axis, way in DIRECTIONS:
        plus, minus = (DIRECTIONS.index((1 - axis, w)) for w in range(2))
        same = (plus, minus)[way]
        plan_5.append([(plus, 4 + way, 1), (minus, 4 + way, 1), (count + same, 4, 1)])
        plan_6.append(
            [(plus, 2 * way, 2), (minus, 2 * way, 2)]
            + [(count + plus, 2 + way, 1), (count + minus, 2 + way, 1)]
        )
    woven = weave([*got_2, *got_3], plan_5 + plan_6)
    far_ids = coarse_far[0]
    far_alive = (far_ids >= 0).astype(F32)
    ids = jnp.maximum(far_ids, 0)
    group = lax.axis_index("grp")
    from_group, node = ids // members, ids % members
    side = (from_group % 2) != (group % 2)
    at = (group // 2 - from_group // 2) % chips * members
    at = at + node
    sources = jnp.where(side[:, None, None], other[at], mine[at])
    far_terms = lax.dot_general(
        sources, coarse_coupling[0], (((2,), (1,)), ((0,), (0,))), preferred_element_type=F32
    )
    field = jnp.sum(far_terms * far_alive[:, None, None], axis=0).astype(BF)
    fields = exchange(spread(field))
    got_5 = send((got_4, *woven, fields), woven[:count])
    got_6 = send((got_5, fields), woven[count:])
    add = functools.partial(near, leaf_size=leaf_size, gamma=gamma)
    groups_4, groups_6, groups_7 = [], [], []
    for d, (axis, way) in enumerate(DIRECTIONS):
        groups_4.append(([(count + d, 0), (count + d, 1)], number(offset(axis, 2, 0))))
        for k in range(0, QUARTERS, 2):
            groups_4.append(([(d, k), (d, k + 1)], number(offset(axis, one(way), 0))))
        for k, along in enumerate((1, 3, 2)):
            pair = [(d, 2 * k), (d, 2 * k + 1)]
            groups_6.append((pair, number(offset(1 - axis, along, one(way)))))
            if way == 0:
                pair = [(d, k), (DIRECTIONS.index((axis, 1)), k)]
                groups_7.append((pair, number(offset(1 - axis, along, 2))))
    flat = near_list.reshape(-1)
    owner = jnp.where(flat >= 0, flat // leaf_count, 0)
    back = (y - owner // RING) % RING * RING + (z - owner % RING) % RING
    leaves = jnp.arange(flat.shape[0]) // near_count + 1
    match = (back[None, :] == jnp.arange(members)[:, None]) & (flat >= 0)[None, :]
    target = jnp.sum(jnp.where(match, leaves[None, :], 0), axis=1) - 1
    total = add([*got_4, *got_3], groups_4, target, points, norms, after(total, *got_5))
    total = finish(fields, parent, transfer, leaf_basis, total)
    got_7 = send((got_6, total), got_5)
    total = add(got_6, groups_6, target, points, norms, total)
    return add(got_7, groups_7, target, points, norms, total)


def solution(mesh):
    placed = (
        P(("grp", "sub"), None),
        P(None, ("grp", "sub")),
        P(("grp", "sub"), None),
        P(("grp", "sub"), None, None),
        P(("grp", "sub"), None, None),
        P(("grp", "sub")),
        P(("grp", "sub"), None),
        P(("grp", "sub"), None, None, None),
    )
    return jax.shard_map(
        local, mesh=mesh, in_specs=placed, out_specs=P(None, ("grp", "sub")), check_vma=False
    )
```
